128 devices in a mesh: dp: 32 (over y_hi, x, z), tensor: 4 (over y_lo, core).
Axes of the slice: x: 4, y: 4 (y_hi: 2, y_lo: 2; y = y_hi * 2 + y_lo), z: 4, core: 2. Of those that a mesh axis runs over, the one named last changes fastest.
Arguments:
- hidden_in: bfloat16 [16384, 2048], P(('dp', 'tensor')), may hold values from -6 to 6
- seq_lengths: int32 [32, 4], P('dp'), may hold values from 1 to 384, 512 in all within a row
- norm_gain: float32 [2048], P(('dp', 'tensor')), may hold values from 0.5 to 1.5
- norm_offset: float32 [2048], P(('dp', 'tensor')), may hold values from -3 to 3
- attn_weight: bfloat16 [3, 2048, 2048], P(None, 'dp', 'tensor'), may hold values from -0.125 to 0.125
- attn_bias: bfloat16 [3, 2048], P(None, ('tensor', 'dp')), may hold values from -3 to 3
- dense_weight: bfloat16 [2048, 2048], P('tensor', 'dp'), may hold values from -0.5 to 0.5
- dense_bias: bfloat16 [2048], P(('tensor', 'dp')), may hold values from -3 to 3
- expand_weight: bfloat16 [2048, 8192], P('dp', 'tensor'), may hold values from -0.125 to 0.125
- expand_bias: bfloat16 [8192], P(('tensor', 'dp')), may hold values from -3 to 3
- reduce_weight: bfloat16 [8192, 2048], P('tensor', 'dp'), may hold values from -0.0625 to 0.0625
- reduce_bias: bfloat16 [2048], P(('tensor', 'dp')), may hold values from -3 to 3
- out_grad: bfloat16 [16384, 2048], P(('dp', 'tensor')), may hold values from -6 to 6
Outputs:
- block_out: bfloat16 [16384, 2048], P(('dp', 'tensor'))
- input_grad: bfloat16 [16384, 2048], P(('dp', 'tensor'))
- norm_gain_grad: float32 [2048], P(('dp', 'tensor'))
- norm_offset_grad: float32 [2048], P(('dp', 'tensor'))
- attn_weight_grad: float32 [3, 2048, 2048], P(None, 'dp', 'tensor')
- attn_bias_grad: float32 [3, 2048], P(None, ('tensor', 'dp'))
- dense_weight_grad: float32 [2048, 2048], P('tensor', 'dp')
- dense_bias_grad: float32 [2048], P(('tensor', 'dp'))
- expand_weight_grad: float32 [2048, 8192], P('dp', 'tensor')
- expand_bias_grad: float32 [8192], P(('tensor', 'dp'))
- reduce_weight_grad: float32 [8192, 2048], P('tensor', 'dp')
- reduce_bias_grad: float32 [2048], P(('tensor', 'dp'))
The draws below stay inside these ranges and needn't reach their ends.
Inputs may be any that keep to these rules, and one draw needn't show every extreme that they name: Each row of seq_lengths holds 4 lengths that sum to 512, the largest exactly 384.
All inputs are finite; a program needn't handle non-finite values.
Results may differ from the reference program's by a relative error of at most 0.013.
Values may be sent and summed in bfloat16 or wider, within the bound.
No kernel may reach another device: no remote copies, remote signals or barrier semaphores. Data moves between devices by JAX's collectives and lax.ppermute only.
A program may use at most 192 MiB of HBM per device.

```python
import math
import jax
import jax.numpy as jnp
import numpy as np
from jax import lax

D = 2048
HEADS = 32
HEAD_DIM = 64
ROT = 32
FF = 8192
TOK_DEV = 128
SEQS = 4
TOK_GRP = 512
MOST = 384
TOKENS = 16384
N_DP = 32
N_TENSOR = 4


def levels(rng, dims, split, least, high):
    level = 1.0
    for dim, shards_of in split:
        draws = jax.random.uniform(jax.random.fold_in(jax.random.fold_in(rng, 6), dim), (shards_of,), jnp.float32, least / len(split), high / len(split))
        level = level * jnp.repeat(jnp.exp(draws), dims[dim] // shards_of).reshape((-1,) + (1,) * (len(dims) - 1 - dim))
    return level


def split_up(amount, total, most, skew):
    loads = [(1 << 20) // math.isqrt(standing ** skew) + 1 for standing in range(2, amount + 1)]
    surplus, holding = total - most - (amount - 1), [1] * (amount - 1)
    while surplus > 0:
        candidates = [i for i in range(amount - 1) if holding[i] < most]
        pool, budget = sum([loads[i] for i in candidates]), surplus
        for i in candidates:
            more = min(most - holding[i], max(1, budget * loads[i] // pool), surplus)
            holding[i] = holding[i] + more
            surplus = surplus - more
    return np.array([most] + holding)


def ragged_sizes(key, amount, total, limit, lean):
    if amount == 2:
        one = jax.random.randint(key, (), max(1, total - limit), min(limit, total - 1) + 1)
        return jnp.stack([one, total - one])
    lengths = jnp.asarray(split_up(amount, total, limit, lean), jnp.int32)
    couples = (amount - 1) // 2
    donor, taker = lengths[1:1 + 2 * couples:2], lengths[2:2 + 2 * couples:2]
    margin = jnp.minimum(donor - 1, limit - taker)
    moved = jax.random.randint(jax.random.fold_in(key, 1), (couples,), 0, 1 << 20) % (margin + 1)
    lengths = lengths.at[1:1 + 2 * couples:2].set(donor - moved).at[2:2 + 2 * couples:2].set(taker + moved)
    return lengths[jax.random.permutation(jax.random.fold_in(key, 2), amount)]


def normal_values(key, extent, scale, bound, pieces=(), kind=jnp.bfloat16):
    loudness = levels(key, extent, pieces, -0.22, 0.18) if pieces else 1.0
    array = jax.random.normal(key, extent, jnp.float32) * scale * loudness
    return jnp.minimum(jnp.maximum(array, -bound), bound).astype(kind)


def setup_inputs(seed: int = 0) -> dict:
    arg_keys = jax.random.split(jax.random.key(seed), 14)
    return {
        "hidden_in": normal_values(arg_keys[0], (TOKENS, D), 1.0, 6.0, ((0, 128),)),
        "seq_lengths": jax.vmap(lambda own: ragged_sizes(own, SEQS, TOK_GRP, MOST, 2))(jax.random.split(arg_keys[1], N_DP)).reshape((N_DP, SEQS)).astype(jnp.int32),
        "norm_gain": jnp.clip(1.0 + 0.1 * jax.random.normal(arg_keys[2], (D,), jnp.float32), 0.5, 1.5),
        "norm_offset": normal_values(arg_keys[3], (D,), 0.3, 3.0, ((0, 128),), jnp.float32),
        "attn_weight": normal_values(arg_keys[4], (3, D, D), D ** -0.5, 0.125, ((1, 32), (2, 4))),
        "attn_bias": normal_values(arg_keys[5], (3, D), 0.5, 3.0, ((1, 128),)),
        "dense_weight": normal_values(arg_keys[6], (D, D), (D // 16) ** -0.5, 0.5, ((0, 4), (1, 32))),
        "dense_bias": normal_values(arg_keys[7], (D,), 0.3, 3.0, ((0, 128),)),
        "expand_weight": normal_values(arg_keys[8], (D, FF), D ** -0.5, 0.125, ((0, 32), (1, 4))),
        "expand_bias": normal_values(arg_keys[9], (FF,), 0.5, 3.0, ((0, 128),)),
        "reduce_weight": normal_values(arg_keys[10], (FF, D), FF ** -0.5, 0.0625, ((0, 4), (1, 32))),
        "reduce_bias": normal_values(arg_keys[11], (D,), 0.3, 3.0, ((0, 128),)),
        "out_grad": normal_values(arg_keys[12], (TOKENS, D), 1.0, 6.0, ((0, 128),)),
    }


@jax.custom_vjp
def low(v):
    return lax.optimization_barrier(v.astype(jnp.bfloat16)).astype(jnp.float32)

@jax.custom_vjp
def low_back(v):
    return v

def low_keep(v):
    return (low(v), None)

def low_pass(kept, grad):
    return (grad,)

def back_keep(v):
    return (v, None)

def back_low(kept, grad):
    return (low(grad),)
low.defvjp(low_keep, low_pass)
low_back.defvjp(back_keep, back_low)

def layer_norm(values, gain_full, offset_full):
    center = values - lax.optimization_barrier(jnp.mean(values, -1, keepdims=True))
    spread = lax.optimization_barrier(jnp.mean(center * center, -1, keepdims=True))
    return center * lax.rsqrt(spread + 1e-05) * gain_full + offset_full

def sequence_layout(length_row, row_total):
    seq_ends = jnp.cumsum(length_row, dtype=jnp.int32)
    seq_starts = seq_ends - length_row
    row_ids = jnp.arange(row_total, dtype=jnp.int32)
    segment = lax.optimization_barrier(jnp.sum((row_ids[:, None] >= seq_ends[None, :]).astype(jnp.int32), 1))
    picked = segment[:, None] == jnp.arange(length_row.shape[0], dtype=jnp.int32)[None, :]
    first_row = lax.optimization_barrier(jnp.sum(jnp.where(picked, seq_starts[None, :], 0), 1)).astype(jnp.int32)
    return (segment, row_ids, row_ids - first_row)

def rotary_tables(position):
    half_rot = ROT // 2
    inverse = 10000.0 ** (-2.0 * jnp.arange(half_rot, dtype=jnp.float32) / ROT)
    angles = position.astype(jnp.float32)[:, None] * inverse[None, :]
    return (jnp.cos(angles), jnp.sin(angles))

def rotate(heads_in, cosine, sine, sign):
    half_rot = ROT // 2
    first_half = heads_in[..., :half_rot]
    second = heads_in[..., half_rot:ROT]
    cos_rows = cosine[:, None, :]
    sin_rows = sign * sine[:, None, :]
    return jnp.concatenate([first_half * cos_rows - second * sin_rows, second * cos_rows + first_half * sin_rows, heads_in[..., ROT:]], -1)

def block_forward(x_rows, gain_full, offset_full, attn_w, attn_b, dense_w, dense_b, expand_w, expand_b, reduce_w, reduce_b, cosine, sine, allowed):
    highest = lax.Precision.HIGHEST
    row_total = x_rows.shape[0]
    normed = low(layer_norm(x_rows, gain_full, offset_full))
    projected = low_back(jnp.einsum('rd,jde->jre', normed, attn_w, precision=highest) + attn_b[:, None, :])
    split_heads = projected.reshape(3, row_total, HEADS, HEAD_DIM)
    query_rot = low(rotate(split_heads[0], cosine, sine, 1.0))
    key_rot = low(rotate(split_heads[1], cosine, sine, 1.0))
    value_rows = low(split_heads[2])
    raw_scores = low_back(jnp.einsum('qhd,khd->hqk', query_rot, key_rot, precision=highest) * HEAD_DIM ** (-0.5))
    masked = jnp.where(allowed[None], raw_scores, -1000000000.0)
    row_top = lax.optimization_barrier(jnp.max(masked, -1, keepdims=True))
    exp_scores = jnp.exp(masked - row_top)
    prob_low = low(exp_scores / lax.optimization_barrier(jnp.sum(exp_scores, -1, keepdims=True)))
    attended = jnp.einsum('hqk,khd->qhd', prob_low, value_rows, precision=highest).reshape(row_total, D)
    attended = low_back(low(attended))
    expanded = low_back(jnp.dot(normed, expand_w, precision=highest) + expand_b)
    activated = low(jax.nn.gelu(expanded, approximate=True))
    attn_branch = jnp.dot(attended, dense_w, precision=highest) + dense_b
    mlp_branch = jnp.dot(activated, reduce_w, precision=highest) + reduce_b
    return x_rows + attn_branch + mlp_branch

def reference(hidden_in, seq_lengths, norm_gain, norm_offset, attn_weight, attn_bias, dense_weight, dense_bias, expand_weight, expand_bias, reduce_weight, reduce_bias, out_grad):
    params = tuple((weight.astype(jnp.float32) for weight in (norm_gain, norm_offset, attn_weight, attn_bias, dense_weight, dense_bias, expand_weight, expand_bias, reduce_weight, reduce_bias)))
    group_rows = TOK_DEV * N_TENSOR
    hidden_groups = hidden_in.reshape(N_DP, group_rows, D)
    grad_groups = out_grad.reshape(N_DP, group_rows, D)

    def one_group(running, inputs):
        x_group, cot_group, length_row = inputs
        segment, row_ids, position = sequence_layout(length_row, group_rows)
        cosine, sine = rotary_tables(position)
        allowed = (segment[:, None] == segment[None, :]) & (row_ids[None, :] <= row_ids[:, None])

        def forward_of(x_rows, *weights):
            return block_forward(x_rows, *weights, cosine, sine, allowed)
        out_rows, pull_back = jax.vjp(forward_of, x_group.astype(jnp.float32), *params)
        grads = pull_back(cot_group.astype(jnp.float32))
        running = tuple((total + part for total, part in zip(running, grads[1:])))
        return (running, (out_rows.astype(jnp.bfloat16), grads[0].astype(jnp.bfloat16)))
    start_sums = tuple((jnp.zeros(weight.shape, jnp.float32) for weight in params))
    sums, outputs = lax.scan(one_group, start_sums, (hidden_groups, grad_groups, seq_lengths))
    block_out = outputs[0].reshape(TOKENS, D)
    input_grad = outputs[1].reshape(TOKENS, D)
    return (block_out, input_grad, sums[0], sums[1], sums[2], sums[3], sums[4], sums[5], sums[6], sums[7], sums[8], sums[9])
```

```python
import numpy as np
import jax
import jax.numpy as jnp
from jax import lax
from jax.experimental import pallas as pl
from jax.experimental.pallas import tpu as pltpu
from jax.sharding import Mesh, PartitionSpec as P

HEAD_DIM = 64
ROT = 32
RING = 4
AXES = ("yhi", "x", "z", "ylo", "core")
COLUMN = ("yhi", "ylo", "core")
BF = jnp.bfloat16
F32 = jnp.float32
MIB = 1 << 20


def ring_pairs(first_ring, step):
    pairs = []
    for x in range(RING):
        for z in range(RING):
            for core in range(2):
                along_x = (core == 0) == first_ring
                to_x = (x + step) % RING if along_x else x
                to_z = z if along_x else (z + step) % RING
                pairs.append(((x * RING + z) * 2 + core, (to_x * RING + to_z) * 2 + core))
    return pairs


def move(value, first_ring, step):
    return lax.ppermute(value, ("x", "z", "core"), ring_pairs(first_ring, step))


def swap(value, axis):
    return lax.ppermute(value, axis, [(0, 1), (1, 0)])


def gather_ring(block, first_ring):
    half = block.shape[0] // 2
    below = move(block, first_ring, 1)
    above = move(block, first_ring, -1)
    far_low = move(below[:half], first_ring, 1)
    far_high = move(above[half:], first_ring, -1)
    return below, above, far_low, far_high


def scatter_ring(blocks, first_ring, split):
    low = move(blocks[2][:split], first_ring, 1)
    high = move(blocks[2][split:], first_ring, -1)
    up = jnp.concatenate([add_low(blocks[1][:split], low), blocks[1][split:]], 0)
    down = jnp.concatenate([blocks[3][:split], add_low(blocks[3][split:], high)], 0)
    from_below = move(up, first_ring, 1)
    from_above = move(down, first_ring, -1)
    return blocks[0].astype(F32) + from_below.astype(F32) + from_above.astype(F32)


def add_low(a, b):
    return (a.astype(F32) + b.astype(F32)).astype(BF)


def through_vmem(moves, hold, in_sems, out_sems):
    inward, outward = [], []
    for n, (source, target) in enumerate(moves):
        slot = hold.at[n, pl.ds(0, source.shape[0])]
        inward.append(pltpu.make_async_copy(source, slot, in_sems.at[n]))
        outward.append(pltpu.make_async_copy(slot, target, out_sems.at[n]))
    for copy in inward:
        copy.start()
    for came, goes in zip(inward, outward):
        came.wait()
        goes.start()
    for copy in outward:
        copy.wait()


def block_mover(kernel, out_shape, operands, count, rows, extra, cols, name):
    any_space = pl.BlockSpec(memory_space=pl.ANY)
    return pl.pallas_call(
        kernel,
        out_shape=out_shape,
        in_specs=[pl.BlockSpec(memory_space=pltpu.SMEM)] + [any_space] * (len(operands) - 1),
        out_specs=jax.tree.map(lambda _: any_space, out_shape),
        scratch_shapes=[
            pltpu.VMEM((count, rows, cols), BF),
            pltpu.SemaphoreType.DMA((count,)),
            pltpu.SemaphoreType.DMA((count,)),
        ],
        compiler_params=pltpu.CompilerParams(vmem_limit_bytes=16 * MIB),
        cost_estimate=pl.CostEstimate(
            flops=0, bytes_accessed=4 * RING * RING * (2 * rows + extra) * cols, transcendentals=0
        ),
        name=name,
    )(*operands)


def assemble(place, rows, extra, own, below, above, far_low, far_high):
    cols = own.shape[-1]
    outs = [jax.ShapeDtypeStruct((2 * RING * RING, rows, cols), BF)]
    if extra:
        outs.append(jax.ShapeDtypeStruct((RING * RING, extra, cols), BF))

    def kernel(place, own, below, above, far_low, far_high, *rest):
        *results, hold, in_sems, out_sems = rest
        sources = [(ref, i) for ref in (own, below, above) for i in range(RING)]
        sources += [(far_low, 0), (far_low, 1), (far_high, 0), (far_high, 1)]
        moves = []
        for n, (ref, i) in enumerate(sources):
            for r in range(2):
                moves.append((ref.at[i, pl.ds(r * rows, rows)], results[0].at[place[2 * n + r]]))
            if extra:
                target = results[1].at[place[2 * n] % (RING * RING)]
                moves.append((ref.at[i, pl.ds(2 * rows, extra)], target))
        through_vmem(moves, hold, in_sems, out_sems)

    operands = (place, own, below, above, far_low, far_high)
    count = RING * RING * (3 if extra else 2)
    return block_mover(kernel, tuple(outs), operands, count, rows, extra, cols, "assemble")


def pack(place, grad, small=None):
    rows, cols = grad.shape[1:]
    extra = 0 if small is None else small.shape[1]

    def kernel(place, grad, *rest):
        *more, out, hold, in_sems, out_sems = rest
        moves = []
        for n in range(RING * RING):
            target = out.at[n // RING, n % RING]
            for r in range(2):
                moves.append((grad.at[place[2 * n + r]], target.at[pl.ds(r * rows, rows)]))
            if extra:
                source = more[0].at[place[2 * n] % (RING * RING)]
                moves.append((source, target.at[pl.ds(2 * rows, extra)]))
        through_vmem(moves, hold, in_sems, out_sems)

    operands = (place, grad) if small is None else (place, grad, small)
    out_shape = jax.ShapeDtypeStruct((RING, RING, 2 * rows + extra, cols), BF)
    count = RING * RING * (3 if extra else 2)
    return block_mover(kernel, out_shape, operands, count, rows, extra, cols, "pack")


def rolled(value, shift):
    return pltpu.roll(value, shift % value.shape[-1], value.ndim - 1)


def rotate(value, cos, sin_low, sin_high, sign):
    half = ROT // 2
    turned = rolled(value, -half) * sin_low + rolled(value, half) * sin_high
    return value * cos + sign * turned


def dot_nt(a, b):
    return lax.dot_general(a, b, (((1,), (1,)), ((), ())), preferred_element_type=F32)


def dot_tn(a, b):
    return lax.dot_general(a, b, (((0,), (0,)), ((), ())), preferred_element_type=F32)


def attention_kernel(
    query, key, value, out_grad, cos, sin_low, sin_high, start, mixed, query_out, key_out, value_out
):
    rows, lanes = query.shape
    scale = HEAD_DIM**-0.5
    cos_v, low_v, high_v = cos[...], sin_low[...], sin_high[...]
    query_rot = (rotate(query[...], cos_v, low_v, high_v, 1.0).astype(BF) * scale).astype(BF)
    key_rot = rotate(key[...], cos_v, low_v, high_v, 1.0).astype(BF)
    value_rows = value[...].astype(BF)
    grad_rows = out_grad[...]
    lane = lax.broadcasted_iota(jnp.int32, (rows, lanes), 1)
    row_id = lax.broadcasted_iota(jnp.int32, (rows, rows), 0)
    col_id = lax.broadcasted_iota(jnp.int32, (rows, rows), 1)
    allowed = (col_id <= row_id) & (col_id >= start[:, 0:1])
    zero = jnp.zeros((rows, lanes), BF)
    sums = None
    for head in range(lanes // HEAD_DIM):
        mine = (lane >= head * HEAD_DIM) & (lane < (head + 1) * HEAD_DIM)
        q_h = jnp.where(mine, query_rot, zero)
        k_h = jnp.where(mine, key_rot, zero)
        v_h = jnp.where(mine, value_rows, zero)
        g_h = jnp.where(mine, grad_rows, zero)
        scores = jnp.where(allowed, dot_nt(q_h, key_rot), -1000000000.0)
        top = jnp.max(scores, -1, keepdims=True)
        expd = jnp.exp(scores - top)
        probs = expd * (1.0 / jnp.sum(expd, -1, keepdims=True))
        prob_low = probs.astype(BF)
        prob_grad = dot_nt(g_h, value_rows)
        row_dot = jnp.sum(probs * prob_grad, -1, keepdims=True)
        score_grad = (probs * (prob_grad - row_dot)).astype(BF)
        parts = (
            jnp.dot(prob_low, v_h, preferred_element_type=F32),
            jnp.dot(score_grad, k_h, preferred_element_type=F32),
            dot_tn(score_grad, q_h),
            dot_tn(prob_low, g_h),
        )
        sums = parts if sums is None else tuple(a + b for a, b in zip(sums, parts))
    mixed[...] = sums[0].astype(BF)
    query_out[...] = rotate(sums[1] * scale, cos_v, low_v, high_v, -1.0).astype(BF)
    key_out[...] = rotate(sums[2], cos_v, low_v, high_v, -1.0).astype(BF)
    value_out[...] = sums[3].astype(BF)


def attention(projected, out_grad, cos, sin_low, sin_high, start, pack_rows):
    rows, width = out_grad.shape
    lanes = 2 * HEAD_DIM
    packs, pairs = rows // pack_rows, width // lanes

    def column(offset):
        return pl.BlockSpec((pack_rows, lanes), lambda p, b: (p, offset + b))

    table = pl.BlockSpec((pack_rows, lanes), lambda p, b: (p, 0))
    shape = jax.ShapeDtypeStruct((rows, width), BF)
    return pl.pallas_call(
        attention_kernel,
        grid=(packs, pairs),
        in_specs=[column(0), column(pairs), column(2 * pairs), column(0)] + [table] * 4,
        out_specs=(column(0),) * 4,
        out_shape=(shape,) * 4,
        compiler_params=pltpu.CompilerParams(vmem_limit_bytes=48 * MIB),
        cost_estimate=pl.CostEstimate(
            flops=14 * rows * pack_rows * width,
            bytes_accessed=rows * width * 32,
            transcendentals=rows * pack_rows * width // HEAD_DIM,
        ),
        name="attention",
    )(projected, projected, projected, out_grad, cos, sin_low, sin_high, start)


def pick(first, a, b):
    return jnp.where(first, a, b), jnp.where(first, b, a)


def three_parts(value):
    high = lax.reduce_precision(value, 8, 7)
    rest = value - high
    mid = lax.reduce_precision(rest, 8, 7)
    return [high.astype(BF), mid.astype(BF), (rest - mid).astype(BF)]


def body(
    hidden_in,
    seq_lengths,
    norm_gain,
    norm_offset,
    attn_weight,
    attn_bias,
    dense_weight,
    dense_bias,
    expand_weight,
    expand_bias,
    reduce_weight,
    reduce_bias,
    out_grad,
):
    at_yhi, at_x, at_z, at_ylo, at_core = (lax.axis_index(a) for a in AXES)
    first_yhi, first_ylo, first_core = at_yhi == 0, at_ylo == 0, at_core == 0
    local_rows, width = hidden_in.shape
    pack_rows = local_rows * RING
    column_rank = (at_ylo * 2 + at_core) * 2 + at_yhi
    plane = RING * RING

    hidden = lax.all_gather(hidden_in, COLUMN, axis=0, tiled=True)
    grad_all = lax.all_gather(out_grad, COLUMN, axis=0, tiled=True)

    def places(order_one, order_two, first_major):
        table = []
        for j in range(RING):
            for i in range(RING):
                one = order_one[i] if first_major else order_one[j]
                two = order_two[j] if first_major else order_two[i]
                x = (at_x + jnp.where(first_core, one, two)) % RING
                z = (at_z + jnp.where(first_core, two, one)) % RING
                table.append(x * RING + z)
        return table

    gather_xz = places((0, 3, 1, 2), (0, 3, 1, 2), True)
    gather_place = jnp.stack(
        [p for xz in gather_xz for p in (at_yhi * plane + xz, (1 - at_yhi) * plane + xz)]
    ).astype(jnp.int32)
    scatter_xz = places((0, 1, 2, 3), (0, 1, 2, 3), True)
    scatter_place = jnp.stack([p for xz in scatter_xz for p in (xz, plane + xz)]).astype(jnp.int32)

    def halves(rows_of_d):
        half = rows_of_d.shape[1] // 2
        own = lax.dynamic_slice_in_dim(rows_of_d, at_yhi * half, half, 1)
        other = lax.dynamic_slice_in_dim(rows_of_d, (1 - at_yhi) * half, half, 1)
        return own, other

    attn_own, attn_other = zip(
        *[halves(w) for w in (attn_weight[0], attn_weight[1], attn_weight[2], dense_weight.T)]
    )
    expand_own, expand_other = halves(expand_weight)
    reduce_own, reduce_other = halves(reduce_weight.T)
    block_rows, cols = expand_own.shape

    def small_block(values):
        values = jnp.concatenate(values)
        return jnp.pad(values, (0, 16 * cols - values.shape[0])).reshape(16, cols)

    lengths = seq_lengths[0]
    count = lengths.shape[0]
    packed = jnp.concatenate(
        three_parts(norm_gain)
        + three_parts(norm_offset)
        + [(lengths // 16).astype(BF), (lengths % 16).astype(BF)]
    )
    unit = packed.shape[0]
    first_other = jnp.concatenate([jnp.concatenate(attn_other, 1), small_block([packed])], 0)
    first_got = swap(first_other, "yhi")
    small_yhi = jnp.stack(pick(first_yhi, packed, first_got[block_rows, :unit]))
    length_rows = small_yhi[:, unit - 2 * count :].astype(F32)
    length_rows = (length_rows[:, :count] * 16.0 + length_rows[:, count:]).astype(jnp.int32)
    small_ylo = jnp.stack(pick(first_ylo, small_yhi, swap(small_yhi, "ylo")), 1)
    small_all = jnp.stack(pick(first_core, small_ylo, swap(small_ylo, "core")), 2)
    norms = 6 * norm_gain.shape[0]
    small_all = small_all[..., :norms].reshape(-1)
    small_own = small_block(
        [small_all, attn_bias.reshape(-1), dense_bias, reduce_bias, expand_bias]
    )
    first = jnp.concatenate(
        [jnp.concatenate(attn_own, 1), first_got[:block_rows], small_own], 0
    )

    def gather_plane(block, extra):
        ring = jnp.stack([block, *gather_whole(block)], 0)
        parts = gather_ring(ring, False)
        return assemble(gather_place, block_rows, extra, ring, *parts)

    def gather_whole(block):
        below, above, far_low, far_high = gather_ring(block, True)
        return below, above, jnp.concatenate([far_low, far_high], 0)

    attn_w, small = gather_plane(first, 16)
    attn_w = attn_w.reshape(width, cols)
    expand_w = gather_plane(
        jnp.concatenate([expand_own, swap(expand_other, "yhi")], 0), 0
    )[0].reshape(width, cols)
    reduce_w = gather_plane(
        jnp.concatenate([reduce_own, swap(reduce_other, "yhi")], 0), 0
    )[0].reshape(width, cols)

    small = small[:, 0].astype(F32)
    norm_all = small[:, : 8 * norms].reshape(plane, 2, 4, 2, 3, -1).sum(4)
    norm_all = norm_all.transpose(3, 1, 0, 2, 4).reshape(2, width)
    gain_full, offset_full = norm_all[0], norm_all[1]
    at = 8 * norms
    bias_unit = attn_bias.shape[1]
    attn_b = small[:, at : at + 3 * bias_unit].reshape(plane, 3, bias_unit)
    attn_b = attn_b.transpose(1, 0, 2).reshape(1, -1)
    at += 3 * bias_unit
    out_b = (small[:, at : at + bias_unit] + small[:, at + bias_unit : at + 2 * bias_unit]).reshape(-1)
    at += 2 * bias_unit
    expand_b = small[:, at : at + expand_bias.shape[0]].reshape(1, -1)

    def statistics(rows):
        mean = jnp.mean(rows, -1, keepdims=True)
        center = rows - mean
        return center, lax.rsqrt(jnp.mean(center * center, -1, keepdims=True) + 1e-05)

    center, spread = statistics(hidden.astype(F32))
    normed = (center * spread * gain_full + offset_full).astype(BF)

    ends = jnp.cumsum(length_rows, 1)
    row_ids = jnp.arange(pack_rows, dtype=jnp.int32)
    begun = row_ids[None, :, None] >= ends[:, None, :]
    start = jnp.max(jnp.where(begun, ends[:, None, :], 0), 2).reshape(-1, 1)
    position = (jnp.tile(row_ids, 2)[:, None] - start).astype(F32)
    lanes = 2 * HEAD_DIM
    lane = np.arange(lanes) % HEAD_DIM
    half = ROT // 2
    inverse = 10000.0 ** (-2.0 * jnp.arange(half, dtype=F32) / ROT)
    inverse = inverse[lane % half][None, :]
    angles = position * inverse
    cos = jnp.where((lane < ROT)[None, :], jnp.cos(angles), 1.0)
    sine = jnp.sin(angles)
    sin_low = jnp.where((lane < half)[None, :], -sine, 0.0)
    sin_high = jnp.where(((lane >= half) & (lane < ROT))[None, :], sine, 0.0)
    start = jnp.broadcast_to(start, (start.shape[0], lanes))

    heads = cols // 4
    projected = jnp.dot(normed, attn_w[:, : 3 * heads], preferred_element_type=F32) + attn_b
    attended_grad = jnp.dot(
        grad_all, attn_w[:, 3 * heads :], preferred_element_type=F32
    ).astype(BF)
    attended, query_grad, key_grad, value_grad = attention(
        projected, attended_grad, cos, sin_low, sin_high, start, pack_rows
    )
    proj_grad = jnp.concatenate([query_grad, key_grad, value_grad], 1)

    expanded = jnp.dot(normed, expand_w, preferred_element_type=F32) + expand_b
    activated, gelu_back = jax.vjp(lambda pre: jax.nn.gelu(pre, approximate=True), expanded)
    activated = activated.astype(BF)
    activated_grad = jnp.dot(grad_all, reduce_w, preferred_element_type=F32)
    expanded_grad = gelu_back(activated_grad)[0].astype(BF)

    reduce_grad = dot_tn(grad_all, activated).astype(BF)
    expand_grad = dot_tn(normed, expanded_grad).astype(BF)
    attn_grad = jnp.concatenate(
        [dot_tn(normed, proj_grad), dot_tn(grad_all, attended)], 1
    ).astype(BF)

    branch = (
        dot_nt(attended, attn_w[:, 3 * heads :])
        + dot_nt(activated, reduce_w)
        + lax.dynamic_update_slice(jnp.zeros((width,), F32), out_b, (column_rank * heads,))
    ).astype(BF)
    branch = lax.psum_scatter(branch, COLUMN, scatter_dimension=0, tiled=True)
    x_rows = hidden_in.astype(F32)
    block_out = (x_rows + branch.astype(F32)).astype(BF)

    normed_part = dot_nt(proj_grad, attn_w[:, : 3 * heads]) + dot_nt(expanded_grad, expand_w)
    gain_part = jnp.sum(normed_part * (center * spread), 0)
    offset_part = jnp.sum(normed_part, 0)
    normed_grad = lax.psum_scatter(
        normed_part.astype(BF), COLUMN, scatter_dimension=0, tiled=True
    ).astype(F32)
    center_own, spread_own = statistics(x_rows)
    x_hat = center_own * spread_own
    scaled = normed_grad * gain_full
    x_grad = spread_own * (
        scaled
        - jnp.mean(scaled, -1, keepdims=True)
        - x_hat * jnp.mean(scaled * x_hat, -1, keepdims=True)
    )
    input_grad = (out_grad.astype(F32) + x_grad).astype(BF)

    attn_bias_grad = jnp.sum(proj_grad.astype(F32), 0).reshape(3, plane, -1).transpose(1, 0, 2)
    expand_bias_grad = jnp.sum(expanded_grad.astype(F32), 0).reshape(plane, -1)
    grad_cols = lax.dynamic_slice_in_dim(grad_all, column_rank * heads, heads, 1)
    out_bias_grad = jnp.sum(grad_cols.astype(F32), 0).reshape(plane, -1)
    norm_part = jnp.stack([gain_part, offset_part]).reshape(2, 2, plane, 4, -1)
    norm_part = norm_part.transpose(2, 1, 3, 0, 4).reshape(plane, -1)
    small_grad = jnp.concatenate(
        [norm_part, attn_bias_grad.reshape(plane, -1), expand_bias_grad, out_bias_grad], 1
    )
    used = small_grad.shape[1]
    small_grad = jnp.pad(small_grad.astype(BF)[:, None], ((0, 0), (0, 15), (0, cols - used)))

    def scatter_plane(grad, extra=None):
        blocks = pack(scatter_place, grad.reshape(2 * plane, block_rows, cols), extra)
        ring = scatter_ring(blocks, False, 2)
        return scatter_ring(ring.astype(BF), True, block_rows)

    def finish(total, rider=None):
        rows = total[: 2 * block_rows].reshape(2, block_rows, cols)
        keep = jnp.where(first_yhi, rows[0], rows[1])
        send = jnp.where(first_yhi, rows[1], rows[0]).astype(BF)
        if rider is not None:
            send = jnp.concatenate([send, rider], 0)
        got = swap(send, "yhi")
        return pick(first_yhi, keep, got[:block_rows].astype(F32)) + (got[block_rows:],)

    reduce_low, reduce_high, _ = finish(scatter_plane(reduce_grad))
    expand_low, expand_high, _ = finish(scatter_plane(expand_grad))
    attn_total = scatter_plane(attn_grad, small_grad)
    small_total = attn_total[2 * block_rows]
    norm_total = small_total[: norm_part.shape[1]].reshape(2, 4, -1)
    keep = jnp.where(first_yhi, norm_total[0], norm_total[1])
    send = jnp.where(first_yhi, norm_total[1], norm_total[0]).reshape(1, -1)
    send = jnp.pad(send.astype(BF), ((0, 15), (0, cols - send.shape[1])))
    attn_low, attn_high, got = finish(attn_total, send)
    keep = keep + got[0, : keep.size].astype(F32).reshape(keep.shape)
    keep = keep.reshape(2, 2, -1)
    send = jnp.where(first_ylo, keep[1], keep[0])
    keep = jnp.where(first_ylo, keep[0], keep[1]) + swap(send, "ylo")
    send = jnp.where(first_core, keep[1], keep[0])
    keep = jnp.where(first_core, keep[0], keep[1]) + swap(send, "core")
    norm_grads = keep.reshape(2, -1)

    attn_cols = [
        jnp.concatenate(
            [attn_low[:, j * heads : (j + 1) * heads], attn_high[:, j * heads : (j + 1) * heads]], 1
        )
        for j in range(4)
    ]
    at = norm_part.shape[1]
    attn_b_grad = small_total[at : at + 3 * bias_unit].reshape(3, bias_unit)
    at += 3 * bias_unit
    expand_b_grad = small_total[at : at + expand_bias.shape[0]]
    at += expand_bias.shape[0]
    out_b_grad = small_total[at : at + bias_unit]
    return (
        block_out,
        input_grad,
        norm_grads[0],
        norm_grads[1],
        jnp.stack(attn_cols[:3]),
        attn_b_grad,
        attn_cols[3].T,
        out_b_grad,
        jnp.concatenate([expand_low, expand_high], 1),
        expand_b_grad,
        jnp.concatenate([reduce_low, reduce_high], 1).T,
        out_b_grad,
    )


def solution(mesh):
    split = Mesh(mesh.devices.reshape(2, RING, RING, 2, 2), AXES)
    dp, tensor = ("yhi", "x", "z"), ("ylo", "core")
    rows = P(dp + tensor, None)
    vector = P(dp + tensor)
    bias = P(tensor + dp)
    params = (
        vector,
        vector,
        P(None, dp, tensor),
        P(None, tensor + dp),
        P(tensor, dp),
        bias,
        P(dp, tensor),
        bias,
        P(tensor, dp),
        bias,
    )
    return jax.shard_map(
        body,
        mesh=split,
        in_specs=(rows, P(dp, None)) + params + (rows,),
        out_specs=(rows, rows) + params,
        check_vma=False,
    )
```

```python
import numpy as np
import jax
import jax.numpy as jnp
from jax import lax
from jax.experimental import pallas as pl
from jax.experimental.pallas import tpu as pltpu
from jax.sharding import Mesh, PartitionSpec as P

HEAD_DIM = 64
ROT = 32
RING = 4
AXES = ("yhi", "x", "z", "ylo", "core")
COLUMN = ("yhi", "ylo", "core")
BF = jnp.bfloat16
F32 = jnp.float32
MIB = 1 << 20


def ring_pairs(first_ring, step):
    pairs = []
    for x in range(RING):
        for z in range(RING):
            for core in range(2):
                along_x = (core == 0) == first_ring
                to_x = (x + step) % RING if along_x else x
                to_z = z if along_x else (z + step) % RING
                pairs.append(((x * RING + z) * 2 + core, (to_x * RING + to_z) * 2 + core))
    return pairs


def move(value, first_ring, step):
    return lax.ppermute(value, ("x", "z", "core"), ring_pairs(first_ring, step))


def swap(value, axis):
    return lax.ppermute(value, axis, [(0, 1), (1, 0)])


def gather_ring(block, first_ring, split):
    below = move(block, first_ring, 1)
    above = move(block, first_ring, -1)
    far_low = move(below[:split], first_ring, 1)
    far_high = move(above[split:], first_ring, -1)
    return below, above, far_low, far_high


def gather_plane(block, split):
    below, above, far_low, far_high = gather_ring(block, True, split)
    ring = jnp.stack([block, below, above, jnp.concatenate([far_low, far_high], 0)], 0)
    return (ring,) + gather_ring(ring, False, 2)


def scatter_ring(blocks, first_ring, split):
    low = move(blocks[2][:split], first_ring, 1)
    high = move(blocks[2][split:], first_ring, -1)
    up = jnp.concatenate([add_low(blocks[1][:split], low), blocks[1][split:]], 0)
    down = jnp.concatenate([blocks[3][:split], add_low(blocks[3][split:], high)], 0)
    from_below = move(up, first_ring, 1)
    from_above = move(down, first_ring, -1)
    return blocks[0].astype(F32) + from_below.astype(F32) + from_above.astype(F32)


def scatter_plane(blocks, split):
    ring = scatter_ring(blocks, False, 2)
    return scatter_ring(ring.astype(BF), True, split)


def add_low(a, b):
    return (a.astype(F32) + b.astype(F32)).astype(BF)


ANY = pl.BlockSpec(memory_space=pl.ANY)
SMEM = pl.BlockSpec(memory_space=pltpu.SMEM)


def whole(shape):
    return pl.BlockSpec(shape, lambda *at: (0,) * len(shape))


def row_block(rows, cols):
    return pl.BlockSpec((rows, cols), lambda i: (i, 0))


def shaped(shape, dtype):
    return jax.ShapeDtypeStruct(shape, dtype)


def params(megabytes):
    return pltpu.CompilerParams(vmem_limit_bytes=megabytes * MIB)


def cost(flops, moved, special=0):
    return pl.CostEstimate(flops=flops, bytes_accessed=moved, transcendentals=special)


def dot_nn(a, b):
    return jnp.dot(a, b, preferred_element_type=F32)


def dot_nt(a, b):
    return lax.dot_general(a, b, (((1,), (1,)), ((), ())), preferred_element_type=F32)


def dot_tn(a, b):
    return lax.dot_general(a, b, (((0,), (0,)), ((), ())), preferred_element_type=F32)


def split_kernel(at_yhi, *refs):
    ins, outs = refs[:4], refs[4:]
    attn, dense, expand, reduce = ins
    for n, rank in enumerate((at_yhi[0], 1 - at_yhi[0])):
        cols = attn.shape[2] // 2
        at = pl.ds(pl.multiple_of(rank * cols, 128), cols)
        for j in range(3):
            outs[n][:, j * cols : (j + 1) * cols] = attn[j, :, at]
        outs[n][:, 3 * cols :] = dense[:, at]
        cols = expand.shape[1] // 2
        at = pl.ds(pl.multiple_of(rank * cols, 128), cols)
        outs[2 + n][...] = expand[:, at]
        outs[4 + n][...] = reduce[:, at]


def split_columns(at_yhi, attn, dense, expand, reduce):
    rows, cols = expand.shape[0], expand.shape[1] // 2
    vmem = pl.BlockSpec(memory_space=pltpu.VMEM)
    return pl.pallas_call(
        split_kernel,
        in_specs=[SMEM] + [vmem] * 4,
        out_specs=(vmem,) * 6,
        out_shape=(shaped((rows, cols), BF),) * 6,
        compiler_params=params(16),
        cost_estimate=cost(0, 6 * rows * cols * 4),
        name="split_columns",
    )(at_yhi, attn, dense, expand, reduce)


def load_weight(place, pieces, weight, sems, small=None):
    sources = [(ref, i) for ref in pieces[:3] for i in range(RING)]
    sources += [(ref, i) for ref in pieces[3:] for i in range(RING // 2)]
    rows = weight.shape[2]
    copies = []
    for n, (ref, i) in enumerate(sources):
        at = place[n]
        if small is None:
            pairs = [(ref.at[i], weight.at[:, at])]
        else:
            pairs = [(ref.at[i, pl.ds(r * rows, rows)], weight.at[r, at]) for r in range(2)]
            pairs.append((ref.at[i, pl.ds(2 * rows, small.shape[1])], small.at[at]))
        for source, target in pairs:
            copies.append(pltpu.make_async_copy(source, target, sems.at[len(copies)]))
    for copy in copies:
        copy.start()
    for copy in copies:
        copy.wait()


def as_matrix(weight, first, last):
    part = weight[:, :, :, first:last]
    return part.reshape(-1, part.shape[-1])


def norm_rows(small):
    def row(at):
        return small[at : at + 1] + small[at + 1 : at + 2] + small[at + 2 : at + 3]

    gain = jnp.concatenate([row(0), row(6)], 1)
    offset = jnp.concatenate([row(3), row(9)], 1)
    return gain, offset


def first_kernel(
    place, own, below, above, far_low, far_high, hidden, grad,
    normed, projected, attended_grad, small, stats, grad_sum, weight_out,
    weight, small_parts, sems, out_sem,
):
    step, last = pl.program_id(0), pl.num_programs(0) - 1
    stored = pltpu.make_async_copy(weight, weight_out, out_sem)
    heads = attended_grad.shape[1]

    @pl.when(step == 0)
    def _():
        load_weight(place, (own, below, above, far_low, far_high), weight, sems, small_parts)
        stored.start()
        total = small_parts[0].astype(F32)
        for n in range(1, small_parts.shape[0]):
            total = total + small_parts[n].astype(F32)
        small[...] = total
        grad_sum[...] = jnp.zeros_like(grad_sum)

    rows = hidden[...].astype(F32)
    gain, offset = norm_rows(small)
    mean = jnp.mean(rows, -1, keepdims=True)
    center = rows - mean
    spread = lax.rsqrt(jnp.mean(center * center, -1, keepdims=True) + 1e-05)
    normed_rows = (center * spread * gain + offset).astype(BF)
    normed[...] = normed_rows
    lane = lax.broadcasted_iota(jnp.int32, stats.shape, 1)
    stats[...] = jnp.where(lane == 0, mean, spread)
    projected[...] = (
        dot_nn(normed_rows, as_matrix(weight, 0, 3 * heads)) + small[12:13, : 3 * heads]
    )
    grad_rows = grad[...]
    attended_grad[...] = dot_nn(grad_rows, as_matrix(weight, 3 * heads, 4 * heads)).astype(BF)
    grad_sum[...] += jnp.sum(grad_rows.astype(F32), 0, keepdims=True)

    @pl.when(step == last)
    def _():
        stored.wait()


def first_layer(place, pieces, hidden, grad, block_rows):
    rows, width = hidden.shape
    cols = pieces[0].shape[-1]
    heads = cols // 4
    plane = RING * RING
    weight = (2, plane, block_rows, cols)
    at_once = 256
    return pl.pallas_call(
        first_kernel,
        grid=(rows // at_once,),
        in_specs=[SMEM] + [ANY] * 5 + [row_block(at_once, width)] * 2,
        out_specs=(
            row_block(at_once, width),
            row_block(at_once, 3 * heads),
            row_block(at_once, heads),
            whole((16, cols)),
            row_block(at_once, 128),
            whole((1, width)),
            ANY,
        ),
        out_shape=(
            shaped((rows, width), BF),
            shaped((rows, 3 * heads), F32),
            shaped((rows, heads), BF),
            shaped((16, cols), F32),
            shaped((rows, 128), F32),
            shaped((1, width), F32),
            shaped(weight, BF),
        ),
        scratch_shapes=[
            pltpu.VMEM(weight, BF),
            pltpu.VMEM((plane, 16, cols), BF),
            pltpu.SemaphoreType.DMA((3 * plane,)),
            pltpu.SemaphoreType.DMA,
        ],
        compiler_params=params(48),
        cost_estimate=cost(2 * rows * width * cols, 2 * (5 * rows * width + 2 * width * cols)),
        name="first_layer",
    )(place, *pieces, hidden, grad)


def expand_kernel(
    place, own, below, above, far_low, far_high, normed, small,
    activated, slope, weight_out, weight, sems, out_sem,
):
    step, last = pl.program_id(0), pl.num_programs(0) - 1
    stored = pltpu.make_async_copy(weight, weight_out, out_sem)

    @pl.when(step == 0)
    def _():
        load_weight(place, (own, below, above, far_low, far_high), weight, sems)
        stored.start()

    u = dot_nn(normed[...], as_matrix(weight, 0, weight.shape[3])) + small[14:15]
    factor = (2.0 / np.pi) ** 0.5
    square = u * u
    bent = jnp.tanh(factor * u * (1.0 + 0.044715 * square))
    half = 0.5 + 0.5 * bent
    activated[...] = (u * half).astype(BF)
    rise = factor * (1.0 + 3.0 * 0.044715 * square)
    slope[...] = (half + 0.5 * u * (1.0 - bent * bent) * rise).astype(BF)

    @pl.when(step == last)
    def _():
        stored.wait()


def reduce_kernel(
    place, own, below, above, far_low, far_high, grad, slope,
    expanded_grad, bias_grad, weight_out, weight, sems, out_sem,
):
    step, last = pl.program_id(0), pl.num_programs(0) - 1
    stored = pltpu.make_async_copy(weight, weight_out, out_sem)

    @pl.when(step == 0)
    def _():
        load_weight(place, (own, below, above, far_low, far_high), weight, sems)
        stored.start()
        bias_grad[...] = jnp.zeros_like(bias_grad)

    activated_grad = dot_nn(grad[...], as_matrix(weight, 0, weight.shape[3]))
    low = (activated_grad * slope[...].astype(F32)).astype(BF)
    expanded_grad[...] = low
    bias_grad[...] += jnp.sum(low.astype(F32), 0, keepdims=True)

    @pl.when(step == last)
    def _():
        stored.wait()


def feed_layer(kernel, place, pieces, left, other, other_spec, second, second_spec, name):
    rows, width = left.shape
    cols = pieces[0].shape[-1]
    weight = (2, RING * RING, pieces[0].shape[2], cols)
    at_once = 256
    return pl.pallas_call(
        kernel,
        grid=(rows // at_once,),
        in_specs=[SMEM] + [ANY] * 5 + [row_block(at_once, width), other_spec(at_once)],
        out_specs=(row_block(at_once, cols), second_spec(at_once), ANY),
        out_shape=(shaped((rows, cols), BF), second, shaped(weight, BF)),
        scratch_shapes=[
            pltpu.VMEM(weight, BF),
            pltpu.SemaphoreType.DMA((RING * RING,)),
            pltpu.SemaphoreType.DMA,
        ],
        compiler_params=params(48),
        cost_estimate=cost(
            2 * rows * width * cols, 2 * (rows * (width + 3 * cols) + 2 * width * cols), rows * cols
        ),
        name=name,
    )(place, *pieces, left, other)


def branch_kernel(rank, activated, attended, reduce_w, dense_w, small, branch):
    heads = attended.shape[1]
    bias = small[12:13, 3 * heads :] + small[13:14, 3 * heads :]
    parts = [
        jnp.where(rank[0] == n, bias, 0.0) for n in range(branch.shape[1] // heads)
    ]
    total = dot_nt(activated[...], reduce_w[...]) + dot_nt(attended[...], dense_w[...])
    branch[...] = (total + jnp.concatenate(parts, 1)).astype(BF)


def branch_layer(rank, activated, attended, reduce_w, attn_w, small):
    rows, cols = activated.shape
    heads = attended.shape[1]
    width = reduce_w.shape[0]
    at_once = 256
    return pl.pallas_call(
        branch_kernel,
        grid=(rows // at_once,),
        in_specs=[
            SMEM,
            row_block(at_once, cols),
            row_block(at_once, heads),
            whole((width, cols)),
            pl.BlockSpec((width, heads), lambda i: (0, 3)),
            whole(small.shape),
        ],
        out_specs=row_block(at_once, width),
        out_shape=shaped((rows, width), BF),
        compiler_params=params(48),
        cost_estimate=cost(
            2 * rows * width * (cols + heads), 2 * (width + rows) * (cols + heads) + 2 * rows * width
        ),
        name="branch",
    )(rank, activated, attended, reduce_w, attn_w, small)


def normed_grad_kernel(
    proj_grad, expanded_grad, attn_w, expand_w, hidden, stats, part, sums
):
    step = pl.program_id(0)

    @pl.when(step == 0)
    def _():
        sums[...] = jnp.zeros_like(sums)

    total = dot_nt(proj_grad[...], attn_w[...]) + dot_nt(expanded_grad[...], expand_w[...])
    part[...] = total.astype(BF)
    x_hat = (hidden[...].astype(F32) - stats[:, 0:1]) * stats[:, 1:2]
    gain = jnp.sum(total * x_hat, 0, keepdims=True)
    offset = jnp.sum(total, 0, keepdims=True)
    sums[...] += jnp.concatenate([gain, offset], 0)


def normed_grad_layer(proj_grad, expanded_grad, attn_w, expand_w, hidden, stats):
    rows, width = hidden.shape
    cols, three = expanded_grad.shape[1], proj_grad.shape[1]
    at_once = 256
    return pl.pallas_call(
        normed_grad_kernel,
        grid=(rows // at_once,),
        in_specs=[
            row_block(at_once, three),
            row_block(at_once, cols),
            whole((width, three)),
            whole((width, cols)),
            row_block(at_once, width),
            row_block(at_once, stats.shape[1]),
        ],
        out_specs=(row_block(at_once, width), whole((2, width))),
        out_shape=(shaped((rows, width), BF), shaped((2, width), F32)),
        compiler_params=params(56),
        cost_estimate=cost(
            2 * rows * width * (cols + three), 2 * (width + rows) * (cols + three) + 4 * rows * width
        ),
        name="normed_grad",
    )(proj_grad, expanded_grad, attn_w, expand_w, hidden, stats)


def weight_grad_kernel(count, place, *refs):
    lefts, rights = refs[:count], refs[count : 2 * count]
    *small, out, hold, sems = refs[2 * count :]
    step, last = pl.program_id(0), pl.num_programs(0) - 1
    plane = out.shape[0]
    blocks, rows = hold.shape[1:3]

    def copies(at):
        made = []
        for k in range(blocks):
            block = at * blocks + k
            target = out.at[place[block % plane], pl.ds((block // plane) * rows, rows)]
            made.append(pltpu.make_async_copy(hold.at[at, k], target, sems.at[at * blocks + k]))
        return made

    def small_copies():
        made = []
        for n in range(plane):
            target = out.at[n, pl.ds(2 * rows, small[0].shape[0])]
            made.append(pltpu.make_async_copy(small[0], target, sems.at[2 * plane + n]))
        return made

    for at in range(hold.shape[0]):

        @pl.when(step == at)
        def _(at=at):
            if at == 0 and small:
                for copy in small_copies():
                    copy.start()
            parts = [dot_tn(a[...], b[...]).astype(BF) for a, b in zip(lefts, rights)]
            grad = parts[0] if count == 1 else jnp.concatenate(parts, 1)
            hold[at] = grad.reshape(hold.shape[1:])
            for copy in copies(at):
                copy.start()

    @pl.when(step == last)
    def _():
        for at in range(hold.shape[0]):
            for copy in copies(at):
                copy.wait()
        if small:
            for copy in small_copies():
                copy.wait()


def weight_grad(place, pairs, block_rows, small=None):
    rows, width = pairs[0][0].shape
    cols = sum(right.shape[1] for _, right in pairs)
    extra = 0 if small is None else small.shape[0]
    plane = RING * RING
    at_once = 512
    steps, blocks = width // at_once, at_once // block_rows

    def kernel(*refs):
        weight_grad_kernel(len(pairs), *refs)

    left = pl.BlockSpec((rows, at_once), lambda i: (0, i))
    out_rows = 2 * block_rows + extra
    out = pl.pallas_call(
        kernel,
        grid=(steps,),
        in_specs=[SMEM]
        + [left] * len(pairs)
        + [whole(right.shape) for _, right in pairs]
        + ([] if small is None else [whole(small.shape)]),
        out_specs=ANY,
        out_shape=shaped((plane, out_rows, cols), BF),
        scratch_shapes=[
            pltpu.VMEM((steps, blocks, block_rows, cols), BF),
            pltpu.SemaphoreType.DMA((3 * plane,)),
        ],
        compiler_params=params(48),
        cost_estimate=cost(
            2 * rows * width * cols, 2 * (len(pairs) * rows * width + rows * cols + width * cols)
        ),
        name="weight_grad",
    )(place, *[a for a, _ in pairs], *[b for _, b in pairs], *([] if small is None else [small]))
    return out.reshape(RING, RING, out_rows, cols)


def rolled(value, shift):
    return pltpu.roll(value, shift % value.shape[-1], value.ndim - 1)


def rotate(value, cos, sin_low, sin_high, sign):
    half = ROT // 2
    turned = rolled(value, -half) * sin_low + rolled(value, half) * sin_high
    return value * cos + sign * turned


def attention_kernel(
    projected, out_grad, cos, sin_low, sin_high, start, mixed, proj_grad, bias_grad
):
    rows, width = out_grad.shape
    lanes = cos.shape[1]
    scale = HEAD_DIM**-0.5
    tables = cos[...], sin_low[...], sin_high[...]
    lane = lax.broadcasted_iota(jnp.int32, (rows, lanes), 1)
    row_id = lax.broadcasted_iota(jnp.int32, (rows, rows), 0)
    col_id = lax.broadcasted_iota(jnp.int32, (rows, rows), 1)
    allowed = (col_id <= row_id) & (col_id >= start[:, 0:1])
    zero = jnp.zeros((rows, lanes), BF)
    for pair in range(width // lanes):
        at = [slice(j * width + pair * lanes, j * width + (pair + 1) * lanes) for j in range(3)]
        query_rot = (rotate(projected[:, at[0]], *tables, 1.0).astype(BF) * scale).astype(BF)
        key_rot = rotate(projected[:, at[1]], *tables, 1.0).astype(BF)
        value_rows = projected[:, at[2]].astype(BF)
        grad_rows = out_grad[:, at[0]]
        sums = None
        for head in range(lanes // HEAD_DIM):
            mine = (lane >= head * HEAD_DIM) & (lane < (head + 1) * HEAD_DIM)
            q_h = jnp.where(mine, query_rot, zero)
            k_h = jnp.where(mine, key_rot, zero)
            v_h = jnp.where(mine, value_rows, zero)
            g_h = jnp.where(mine, grad_rows, zero)
            scores = jnp.where(allowed, dot_nt(q_h, key_rot), -1000000000.0)
            top = jnp.max(scores, -1, keepdims=True)
            expd = jnp.exp(scores - top)
            probs = expd * (1.0 / jnp.sum(expd, -1, keepdims=True))
            prob_low = probs.astype(BF)
            prob_grad = dot_nt(g_h, value_rows)
            row_dot = jnp.sum(probs * prob_grad, -1, keepdims=True)
            score_grad = (probs * (prob_grad - row_dot)).astype(BF)
            parts = (
                dot_nn(prob_low, v_h),
                dot_nn(score_grad, k_h),
                dot_tn(score_grad, q_h),
                dot_tn(prob_low, g_h),
            )
            sums = parts if sums is None else tuple(a + b for a, b in zip(sums, parts))
        mixed[:, at[0]] = sums[0].astype(BF)
        grads = (
            rotate(sums[1] * scale, *tables, -1.0),
            rotate(sums[2], *tables, -1.0),
            sums[3],
        )
        for j in range(3):
            low = grads[j].astype(BF)
            proj_grad[:, at[j]] = low
            bias_grad[0, :, at[j]] = jnp.sum(low.astype(F32), 0, keepdims=True)


def attention(projected, out_grad, cos, sin_low, sin_high, start, pack_rows):
    rows, width = out_grad.shape
    lanes = cos.shape[1]
    packs = rows // pack_rows
    return pl.pallas_call(
        attention_kernel,
        grid=(packs,),
        in_specs=[row_block(pack_rows, 3 * width), row_block(pack_rows, width)]
        + [row_block(pack_rows, lanes)] * 4,
        out_specs=(
            row_block(pack_rows, width),
            row_block(pack_rows, 3 * width),
            pl.BlockSpec((1, 1, 3 * width), lambda p: (p, 0, 0)),
        ),
        out_shape=(
            shaped((rows, width), BF),
            shaped((rows, 3 * width), BF),
            shaped((packs, 1, 3 * width), F32),
        ),
        compiler_params=params(48),
        cost_estimate=cost(
            14 * rows * pack_rows * width, rows * width * 32, rows * pack_rows * width // HEAD_DIM
        ),
        name="attention",
    )(projected, out_grad, cos, sin_low, sin_high, start)


def pick(first, a, b):
    return jnp.where(first, a, b), jnp.where(first, b, a)


def three_parts(value):
    high = lax.reduce_precision(value, 8, 7)
    rest = value - high
    mid = lax.reduce_precision(rest, 8, 7)
    return [high, mid, rest - mid]


def body(
    hidden_in,
    seq_lengths,
    norm_gain,
    norm_offset,
    attn_weight,
    attn_bias,
    dense_weight,
    dense_bias,
    expand_weight,
    expand_bias,
    reduce_weight,
    reduce_bias,
    out_grad,
):
    at_yhi, at_x, at_z, at_ylo, at_core = (lax.axis_index(a) for a in AXES)
    first_yhi, first_ylo, first_core = at_yhi == 0, at_ylo == 0, at_core == 0
    local_rows, width = hidden_in.shape
    pack_rows = local_rows * RING
    at_tensor = at_ylo * 2 + at_core
    column_rank = at_tensor * 2 + at_yhi
    plane = RING * RING
    at_plane = at_x * RING + at_z

    hidden = lax.all_gather(hidden_in, COLUMN, axis=0, tiled=True)
    grad_all = lax.all_gather(out_grad, COLUMN, axis=0, tiled=True)

    order = np.array([0, 3, 1, 2], np.int32)
    inner, outer = np.tile(order, RING), np.repeat(order, RING)
    x = (at_x + jnp.where(first_core, inner, outer)) % RING
    z = (at_z + jnp.where(first_core, outer, inner)) % RING
    gather_place = (x * RING + z).astype(jnp.int32)
    place = np.arange(plane, dtype=np.int32)
    x, z = (place // RING - at_x) % RING, (place % RING - at_z) % RING
    scatter_place = jnp.where(first_core, z * RING + x, x * RING + z).astype(jnp.int32)

    attn_own, attn_other, expand_own, expand_other, reduce_own, reduce_other = split_columns(
        at_yhi.reshape(1).astype(jnp.int32), attn_weight, dense_weight.T, expand_weight, reduce_weight.T
    )
    block_rows, cols = expand_own.shape
    heads = cols // 4

    unit = norm_gain.shape[0]
    norms = jnp.stack(three_parts(norm_gain) + three_parts(norm_offset))
    lengths = seq_lengths[0]
    count = lengths.shape[0]
    small = lax.dynamic_update_slice(
        jnp.zeros((16, cols), F32), norms, (at_yhi * 6, at_plane * 4 * unit + at_tensor * unit)
    )
    two = jnp.concatenate([lengths // 16, lengths % 16]).astype(F32)
    small = lax.dynamic_update_slice(small, two[None], (15, at_yhi * 2 * count)).astype(BF)
    got = swap(jnp.concatenate([attn_other, small], 0), "yhi")
    attn_got = got[:block_rows]
    small = small + got[block_rows:]
    two = small[15, : 4 * count].astype(F32).reshape(2, 2, count)
    length_rows = (two[:, 0] * 16.0 + two[:, 1]).astype(jnp.int32)
    small = small + swap(small, "ylo")
    small = small + swap(small, "core")
    biases = jnp.stack([dense_bias, reduce_bias])
    biases = jnp.concatenate([jnp.stack([attn_bias, 0 * attn_bias]), biases[:, None]], 1)
    bias_rows = lax.dynamic_update_slice(
        jnp.zeros((2, 4, heads), BF), biases, (0, 0, at_plane * unit)
    ).reshape(2, cols)
    expand_row = lax.dynamic_update_slice(
        jnp.zeros((2, cols), BF), expand_bias[None], (0, at_plane * expand_bias.shape[0])
    )
    small = jnp.concatenate([small[:12], bias_rows, expand_row], 0)

    def both(own, got):
        return jnp.stack(pick(first_yhi, own, got))

    first = jnp.concatenate([both(attn_own, attn_got).reshape(-1, cols), small], 0)
    first_pieces = gather_plane(first, block_rows)
    expand_pieces = gather_plane(both(expand_own, swap(expand_other, "yhi")), 1)
    reduce_pieces = gather_plane(both(reduce_own, swap(reduce_other, "yhi")), 1)

    ends = jnp.cumsum(length_rows, 1)
    row_ids = jnp.arange(pack_rows, dtype=jnp.int32)
    begun = row_ids[None, :, None] >= ends[:, None, :]
    start = jnp.max(jnp.where(begun, ends[:, None, :], 0), 2).reshape(-1, 1)
    position = (jnp.tile(row_ids, 2)[:, None] - start).astype(F32)
    lanes = 2 * HEAD_DIM
    lane = np.arange(lanes) % HEAD_DIM
    half = ROT // 2
    inverse = np.float32(10000.0) ** (np.float32(-2.0) * (lane % half).astype(np.float32) / ROT)
    angles = position * inverse.astype(np.float32)[None, :]
    cos = jnp.where((lane < ROT)[None, :], jnp.cos(angles), 1.0)
    sine = jnp.sin(angles)
    sin_low = jnp.where((lane < half)[None, :], -sine, 0.0)
    sin_high = jnp.where(((lane >= half) & (lane < ROT))[None, :], sine, 0.0)
    start = jnp.broadcast_to(start, (start.shape[0], lanes))

    normed, projected, attended_grad, small, stats, grad_sum, attn_w = first_layer(
        gather_place, first_pieces, hidden, grad_all, block_rows
    )
    attn_w = attn_w.reshape(width, cols)
    rows = hidden.shape[0]
    activated, slope, expand_w = feed_layer(
        expand_kernel, gather_place, expand_pieces, normed, small,
        lambda n: whole(small.shape), shaped((rows, cols), BF), lambda n: row_block(n, cols), "expand",
    )
    expanded_grad, expand_bias_grad, reduce_w = feed_layer(
        reduce_kernel, gather_place, reduce_pieces, grad_all, slope,
        lambda n: row_block(n, cols), shaped((1, cols), F32), lambda n: whole((1, cols)), "reduce",
    )
    expand_w, reduce_w = expand_w.reshape(width, cols), reduce_w.reshape(width, cols)
    attended, proj_grad, attn_bias_grad = attention(
        projected, attended_grad, cos, sin_low, sin_high, start, pack_rows
    )

    branch = branch_layer(
        column_rank.reshape(1).astype(jnp.int32), activated, attended, reduce_w, attn_w, small
    )
    branch = lax.psum_scatter(branch, COLUMN, scatter_dimension=0, tiled=True)
    x_rows = hidden_in.astype(F32)
    block_out = (x_rows + branch.astype(F32)).astype(BF)

    normed_part, norm_sums = normed_grad_layer(
        proj_grad, expanded_grad, attn_w, expand_w, hidden, stats
    )
    normed_grad = lax.psum_scatter(
        normed_part, COLUMN, scatter_dimension=0, tiled=True
    ).astype(F32)
    mean = jnp.mean(x_rows, -1, keepdims=True)
    center = x_rows - mean
    spread = lax.rsqrt(jnp.mean(center * center, -1, keepdims=True) + 1e-05)
    x_hat = center * spread
    gain_full, _ = norm_rows(small)
    scaled = normed_grad * gain_full
    x_grad = spread * (
        scaled
        - jnp.mean(scaled, -1, keepdims=True)
        - x_hat * jnp.mean(scaled * x_hat, -1, keepdims=True)
    )
    input_grad = (out_grad.astype(F32) + x_grad).astype(BF)

    reduce_blocks = weight_grad(scatter_place, [(grad_all, activated)], block_rows)
    expand_blocks = weight_grad(scatter_place, [(normed, expanded_grad)], block_rows)
    out_bias_grad = lax.dynamic_slice_in_dim(grad_sum, column_rank * heads, heads, 1)
    attn_row = jnp.concatenate([jnp.sum(attn_bias_grad, 0), out_bias_grad], 1)
    small_grad = jnp.concatenate(
        [norm_sums.reshape(4, cols), attn_row, expand_bias_grad, jnp.zeros((10, cols), F32)], 0
    ).astype(BF)
    attn_blocks = weight_grad(
        scatter_place, [(normed, proj_grad), (grad_all, attended)], block_rows, small_grad
    )

    def finish(total, rider=None):
        halves = total[: 2 * block_rows].reshape(2, block_rows, cols)
        keep, send = pick(first_yhi, halves[0], halves[1])
        send = send.astype(BF)
        if rider is not None:
            send = jnp.concatenate([send, rider], 0)
        got = swap(send, "yhi")
        return pick(first_yhi, keep, got[:block_rows].astype(F32)) + (got[block_rows:],)

    reduce_low, reduce_high, _ = finish(scatter_plane(reduce_blocks, block_rows))
    expand_low, expand_high, _ = finish(scatter_plane(expand_blocks, block_rows))
    attn_total = scatter_plane(attn_blocks, block_rows)
    small_total = attn_total[2 * block_rows :]
    norm_total = lax.dynamic_slice_in_dim(
        small_total[:4].reshape(2, 2, cols), at_plane * 4 * unit, 4 * unit, 2
    )
    keep, send = pick(first_yhi, norm_total[:, 0], norm_total[:, 1])
    rider = jnp.pad(send.astype(BF), ((0, 14), (0, cols - 4 * unit)))
    attn_low, attn_high, got = finish(attn_total, rider)
    keep = (keep + got[:2, : 4 * unit].astype(F32)).reshape(2, 2, 2, unit)
    keep, send = pick(first_ylo, keep[:, 0], keep[:, 1])
    keep = keep + swap(send, "ylo")
    keep, send = pick(first_core, keep[:, 0], keep[:, 1])
    norm_grads = keep + swap(send, "core")

    attn_cols = [
        jnp.concatenate([attn_low[:, at : at + heads], attn_high[:, at : at + heads]], 1)
        for at in range(0, cols, heads)
    ]
    bias_total = lax.dynamic_slice_in_dim(
        small_total[4].reshape(4, heads), at_plane * unit, unit, 1
    )
    expand_b_grad = lax.dynamic_slice_in_dim(
        small_total[5], at_plane * expand_bias.shape[0], expand_bias.shape[0]
    )
    return (
        block_out,
        input_grad,
        norm_grads[0],
        norm_grads[1],
        jnp.stack(attn_cols[:3]),
        bias_total[:3],
        attn_cols[3].T,
        bias_total[3],
        jnp.concatenate([expand_low, expand_high], 1),
        expand_b_grad,
        jnp.concatenate([reduce_low, reduce_high], 1).T,
        bias_total[3],
    )


def solution(mesh):
    split = Mesh(mesh.devices.reshape(2, RING, RING, 2, 2), AXES)
    dp, tensor = ("yhi", "x", "z"), ("ylo", "core")
    rows = P(dp + tensor, None)
    vector = P(dp + tensor)
    bias = P(tensor + dp)
    parameters = (
        vector,
        vector,
        P(None, dp, tensor),
        P(None, tensor + dp),
        P(tensor, dp),
        bias,
        P(dp, tensor),
        bias,
        P(tensor, dp),
        bias,
    )
    return jax.shard_map(
        body,
        mesh=split,
        in_specs=(rows, P(dp, None)) + parameters + (rows,),
        out_specs=(rows, rows) + parameters,
        check_vma=False,
    )
```

```python
import numpy as np
import jax
import jax.numpy as jnp
from jax import lax
from jax.experimental import pallas as pl
from jax.experimental.pallas import tpu as pltpu
from jax.sharding import Mesh, PartitionSpec as P

HEAD_DIM = 64
ROT = 32
RING = 4
AXES = ("yhi", "x", "z", "ylo", "core")
COLUMN = ("yhi", "ylo", "core")
BF = jnp.bfloat16
F32 = jnp.float32
MIB = 1 << 20
BIG = 58
SMALL = 16


def ring_pairs(first_ring, step):
    pairs = []
    for x in range(RING):
        for z in range(RING):
            for core in range(2):
                along_x = (core == 0) == first_ring
                to_x = (x + step) % RING if along_x else x
                to_z = z if along_x else (z + step) % RING
                pairs.append(((x * RING + z) * 2 + core, (to_x * RING + to_z) * 2 + core))
    return pairs


def move(value, first_ring, step):
    return lax.ppermute(value, ("x", "z", "core"), ring_pairs(first_ring, step))


def axis_swaps(odd):
    return [(n, (n + (1 if n % 2 == odd else -1)) % RING) for n in range(RING)]


def pair_swaps(odd):
    pairs = []
    for x in range(RING):
        for z in range(RING):
            for core in range(2):
                to = [x, z]
                along = 0 if core else 1
                step = 1 if to[along] % 2 == odd else -1
                to[along] = (to[along] + step) % RING
                pairs.append(((x * RING + z) * 2 + core, (to[0] * RING + to[1]) * 2 + core))
    return pairs


def move_y(value, step):
    pairs = [(y, (y + step) % RING) for y in range(RING)]
    return lax.ppermute(value, ("yhi", "ylo"), pairs)


def swap(value, axis):
    return lax.ppermute(value, axis, [(0, 1), (1, 0)])


def ring_send(blocks, first_ring, way):
    _, minus, plus, far = blocks
    direct = move(minus, first_ring, -1) if way > 0 else move(plus, first_ring, 1)
    return move(far, first_ring, way), direct


ANY = pl.BlockSpec(memory_space=pl.ANY)
SMEM = pl.BlockSpec(memory_space=pltpu.SMEM)


def whole(shape):
    return pl.BlockSpec(shape, lambda *at: (0,) * len(shape))


def row_block(rows, cols):
    return pl.BlockSpec((rows, cols), lambda i: (i, 0))


def shaped(shape, dtype):
    return jax.ShapeDtypeStruct(shape, dtype)


def kernel_call(kernel, operands, waits, *, in_specs, **options):
    count, more = len(operands), len(waits)

    def run(*refs):
        kernel(*refs[:count], *refs[count + more :])

    in_specs = list(in_specs) + [ANY] * more
    scalars = count - len(in_specs) + more
    if scalars:
        parts = {key: options.pop(key) for key in ("grid", "out_specs", "scratch_shapes")}
        options["grid_spec"] = pltpu.PrefetchScalarGridSpec(
            num_scalar_prefetch=scalars, in_specs=in_specs, **parts
        )
    else:
        options["in_specs"] = in_specs
    return pl.pallas_call(run, **options)(*operands, *waits)


def parts_kernel(*refs):
    count = len(refs) // 2
    for ref, out in zip(refs[:count], refs[count:]):
        out[...] = ref[...]


def take_parts(*chosen):
    specs = [pl.BlockSpec(shape, lambda i, at=at: at) for _, shape, at in chosen]
    return kernel_call(
        parts_kernel,
        tuple(array for array, _, _ in chosen),
        (),
        grid=(1,),
        in_specs=specs,
        out_specs=tuple(whole(shape) for _, shape, _ in chosen),
        out_shape=tuple(shaped(shape, array.dtype) for array, shape, _ in chosen),
        compiler_params=params(SMALL),
        cost_estimate=cost(0, 4 * sum(int(np.prod(shape)) for _, shape, _ in chosen)),
        name="take_parts",
    )


def add_pairs_kernel(*refs):
    count = (len(refs) - 2) // 3
    for n in range(count):
        a, b, out = refs[2 * n], refs[2 * n + 1], refs[2 * count + 1 + n]
        out[...] = (a[...].astype(F32) + b[...].astype(F32)).astype(BF)


def add_pairs(pairs, carried, waits=()):
    shapes = [a.shape for a, _ in pairs]
    flat = [term.reshape(-1, term.shape[-1]) for pair in pairs for term in pair]
    halves = [row_block(term.shape[0] // 2, term.shape[1]) for term in flat]
    *sums, carried = kernel_call(
        add_pairs_kernel,
        (*flat, carried),
        waits,
        grid=(2,),
        in_specs=halves + [ANY],
        out_specs=tuple(halves[::2]) + (ANY,),
        out_shape=tuple(shaped(term.shape, BF) for term in flat[::2])
        + (shaped(carried.shape, carried.dtype),),
        input_output_aliases={len(flat): len(pairs)},
        compiler_params=params(BIG),
        cost_estimate=cost(0, 3 * sum(term.size for term in flat)),
        name="add_pairs",
    )
    return [total.reshape(shape) for total, shape in zip(sums, shapes)] + [carried]


def add_lines_kernel(riders, *refs):
    outs = refs[-RING:]
    sources, at = refs[: -RING - riders], 0
    for n in range(0, len(sources), 3):
        total = sum(ref[...].astype(F32) for ref in sources[n : n + 3])
        for i, out in enumerate(outs):
            out[:, at : at + total.shape[-1]] = total[i].astype(BF)
        at += total.shape[-1]
    for ref in refs[len(sources) : -RING]:
        for out in outs:
            out[:, at:] = ref[...]


def add_lines(lines, riders=(), waits=()):
    operands = [term for terms in lines for term in terms]
    rows = operands[0].shape[1]
    cols = sum(terms[0].shape[2] for terms in lines) + sum(rider.shape[1] for rider in riders)
    at_once = rows // 2

    def kernel(*refs):
        add_lines_kernel(len(riders), *refs)

    specs = [
        pl.BlockSpec((RING, at_once, term.shape[2]), lambda i: (0, i, 0)) for term in operands
    ]
    return kernel_call(
        kernel,
        (*operands, *riders),
        waits,
        grid=(2,),
        in_specs=specs + [row_block(at_once, rider.shape[1]) for rider in riders],
        out_specs=(row_block(at_once, cols),) * RING,
        out_shape=(shaped((rows, cols), BF),) * RING,
        compiler_params=params(SMALL),
        cost_estimate=cost(0, 8 * RING * rows * cols),
        name="add_lines",
    )


def add_up(here, direct, second):
    return here.astype(F32) + direct.astype(F32) + second.astype(F32)


def params(megabytes):
    return pltpu.CompilerParams(vmem_limit_bytes=megabytes * MIB)


def cost(flops, moved, special=0):
    return pl.CostEstimate(flops=flops, bytes_accessed=moved, transcendentals=special)


def dot_nn(a, b):
    return jnp.dot(a, b, preferred_element_type=F32)


def dot_nt(a, b):
    return lax.dot_general(a, b, (((1,), (1,)), ((), ())), preferred_element_type=F32)


def dot_tn(a, b):
    return lax.dot_general(a, b, (((0,), (0,)), ((), ())), preferred_element_type=F32)


def split_kernel(at_yhi, *refs):
    ins, outs = refs[:8], refs[8:]
    for n, out in enumerate(outs):
        attn, *others = ins[4 * n : 4 * n + 4]
        at = 0
        for part in [attn[j] for j in range(3)] + [ref[...] for ref in others]:
            out[:, at : at + part.shape[1]] = part
            at += part.shape[1]


def split_columns(at_yhi, attn, dense, expand, reduce):
    rows, cols = expand.shape[0], expand.shape[1] // 2
    ins = []
    for n in range(2):

        def side(at, n=n):
            return at[0] if n == 0 else 1 - at[0]

        ins.append(pl.BlockSpec((3, rows, cols // 4), lambda i, at, side=side: (0, 0, side(at))))
        for width in (cols // 4, cols, cols):
            ins.append(pl.BlockSpec((rows, width), lambda i, at, side=side: (0, side(at))))
    return pl.pallas_call(
        split_kernel,
        grid_spec=pltpu.PrefetchScalarGridSpec(
            num_scalar_prefetch=1,
            grid=(1,),
            in_specs=ins,
            out_specs=(whole((rows, 3 * cols)),) * 2,
        ),
        out_shape=(shaped((rows, 3 * cols), BF),) * 2,
        compiler_params=params(BIG),
        cost_estimate=cost(0, 6 * rows * cols * 4),
        name="split_columns",
    )(at_yhi, *[attn, dense, expand, reduce] * 2)


def paired(rows):
    lanes = 2 * HEAD_DIM
    low = lax.broadcasted_iota(jnp.int32, (rows.shape[0], lanes), 1) < HEAD_DIM
    half = rows.shape[1] // 2
    for k in range(half // lanes):
        a = rows[:, k * lanes : (k + 1) * lanes]
        b = rows[:, half + k * lanes : half + (k + 1) * lanes]
        yield 2 * k * lanes, jnp.where(low, a, pltpu.roll(b, HEAD_DIM, 1))
        yield (2 * k + 1) * lanes, jnp.where(low, pltpu.roll(a, HEAD_DIM, 1), b)


def unpaired(rows):
    lanes = 2 * HEAD_DIM
    low = lax.broadcasted_iota(jnp.int32, (rows.shape[0], lanes), 1) < HEAD_DIM
    half = rows.shape[1] // 2
    for k in range(half // lanes):
        a = rows[:, 2 * k * lanes : (2 * k + 1) * lanes]
        b = rows[:, (2 * k + 1) * lanes : (2 * k + 2) * lanes]
        yield k * lanes, jnp.where(low, a, pltpu.roll(b, HEAD_DIM, 1))
        yield half + k * lanes, jnp.where(low, pltpu.roll(a, HEAD_DIM, 1), b)


def pair_kernel(hidden, grad, out):
    for n, ref in enumerate((hidden, grad)):
        for at, block in paired(ref[...].astype(F32)):
            out[n, :, at : at + block.shape[1]] = block.astype(BF)


def pair_columns(hidden, grad, *waits):
    rows, width = hidden.shape
    at_once = rows // 2
    return kernel_call(
        pair_kernel,
        (hidden, grad),
        waits,
        grid=(2,),
        in_specs=[row_block(at_once, width)] * 2,
        out_specs=pl.BlockSpec((2, at_once, width), lambda i: (0, i, 0)),
        out_shape=shaped((2, rows, width), BF),
        compiler_params=params(SMALL),
        cost_estimate=cost(0, 8 * rows * width),
        name="pair_columns",
    )


def output_kernel(hidden, branch, out):
    total = hidden[0].astype(F32) + branch[...].astype(F32)
    for at, block in unpaired(total):
        out[:, at : at + block.shape[1]] = block.astype(BF)


def own_block(which, rows, width):
    return pl.BlockSpec((1, rows, width), lambda i: (which, i, 0))


def output_layer(own, branch):
    _, rows, width = own.shape
    at_once = rows // 2
    return pl.pallas_call(
        output_kernel,
        grid=(2,),
        in_specs=[own_block(0, at_once, width), row_block(at_once, width)],
        out_specs=row_block(at_once, width),
        out_shape=shaped((rows, width), BF),
        compiler_params=params(SMALL),
        cost_estimate=cost(0, 6 * rows * width),
        name="output",
    )(own, branch)


def input_grad_kernel(hidden, grad, normed_grad, small, out):
    rows = hidden[0].astype(F32)
    center = rows - jnp.mean(rows, -1, keepdims=True)
    spread = lax.rsqrt(jnp.mean(center * center, -1, keepdims=True) + 1e-05)
    x_hat = center * spread
    gain, _ = norm_rows(small)
    scaled = normed_grad[...].astype(F32) * gain
    total = grad[0].astype(F32) + spread * (
        scaled
        - jnp.mean(scaled, -1, keepdims=True)
        - x_hat * jnp.mean(scaled * x_hat, -1, keepdims=True)
    )
    for at, block in unpaired(total):
        out[:, at : at + block.shape[1]] = block.astype(BF)


def input_grad_layer(own, normed_grad, small):
    _, rows, width = own.shape
    at_once = rows // 2
    return pl.pallas_call(
        input_grad_kernel,
        grid=(2,),
        in_specs=[own_block(n, at_once, width) for n in range(2)]
        + [row_block(at_once, width), whole(small.shape)],
        out_specs=row_block(at_once, width),
        out_shape=shaped((rows, width), BF),
        compiler_params=params(SMALL),
        cost_estimate=cost(0, 8 * rows * width),
        name="input_grad",
    )(own, own, normed_grad, small)


def put_in_turn(rows, turned, out):
    lanes = 2 * HEAD_DIM
    for n in range(rows.shape[1] // lanes):
        at = pl.multiple_of(turned[n] * lanes, lanes)
        out[:, pl.ds(at, lanes)] = rows[:, n * lanes : (n + 1) * lanes].astype(out.dtype)


def fold(small):
    return small.reshape(16, -1, 128).transpose(1, 0, 2).reshape(-1, 128)


def unfold(small):
    return small.reshape(-1, 16, 128).transpose(1, 0, 2).reshape(16, -1)


def norm_rows(small):
    def row(at):
        return small[at : at + 1] + small[at + 1 : at + 2] + small[at + 2 : at + 3]

    gain = jnp.concatenate([row(0), row(6)], 1)
    offset = jnp.concatenate([row(3), row(9)], 1)
    return gain, offset


def load_rows(chips, sources, held, sems, step):
    copies = []
    for n, ref in enumerate(sources):
        core = chips[RING] if n % 2 == 0 else 1 - chips[RING]
        copies.append(pltpu.make_async_copy(ref, held.at[n // 2, core], sems.at[n]))

    @pl.when(step == 0)
    def _():
        for copy in copies:
            copy.start()

    for n in range(RING):

        @pl.when(step == n)
        def _(n=n):
            copies[2 * n].wait()
            copies[2 * n + 1].wait()

    rows = held[step]
    return rows.reshape(-1, rows.shape[-1])


def chip_block(rows, cols):
    return pl.BlockSpec((rows, cols), lambda i, chips: (chips[i], 0))


def prefetched(specs):
    return [
        spec
        if spec.index_map is None
        else pl.BlockSpec(spec.block_shape, lambda i, chips, at=spec.index_map: at(i))
        for spec in specs
    ]


def rows_kernel(chips, turned, small, *refs):
    sources, rest = refs[: 2 * RING], refs[2 * RING :]
    normed, normed_turned, x_hat, grad, grad_turned, grad_sum, held, grad_held, sems, grad_sems = rest
    step = pl.program_id(0)

    @pl.when(step == 0)
    def _():
        grad_sum[...] = jnp.zeros_like(grad_sum)

    rows = load_rows(chips, [hidden_of(ref) for ref in sources], held, sems, step).astype(F32)
    gain, offset = norm_rows(small)
    center = rows - jnp.mean(rows, -1, keepdims=True)
    scaled = center * lax.rsqrt(jnp.mean(center * center, -1, keepdims=True) + 1e-05)
    x_hat[...] = scaled.astype(BF)
    normed[...] = (scaled * gain + offset).astype(BF)
    put_in_turn(normed, turned, normed_turned)
    rows = load_rows(chips, [grad_of(ref) for ref in sources], grad_held, grad_sems, step)
    grad[...] = rows
    put_in_turn(grad, turned, grad_turned)
    grad_sum[...] += jnp.sum(rows.astype(F32), 0, keepdims=True)


def hidden_of(ref):
    return ref.at[0] if len(ref.shape) == 3 else ref


def grad_of(ref):
    return ref.at[1] if len(ref.shape) == 3 else ref


def rows_layer(chips, turned, small, sources, *waits):
    local_rows, width = sources[0].shape[-2:]
    rows = 2 * RING * local_rows
    at_once = 2 * local_rows
    return kernel_call(
        rows_kernel,
        (chips, turned, small, *sources),
        waits,
        grid=(RING,),
        in_specs=[SMEM] + prefetched([whole(small.shape)]) + [ANY] * len(sources),
        out_specs=(chip_block(at_once, width),) * 5 + tuple(prefetched([whole((1, width))])),
        out_shape=(shaped((rows, width), BF),) * 5 + (shaped((1, width), F32),),
        scratch_shapes=[pltpu.VMEM((RING, 2, local_rows, width), BF)] * 2
        + [pltpu.SemaphoreType.DMA((2 * RING,))] * 2,
        compiler_params=params(BIG),
        cost_estimate=cost(0, 14 * rows * width),
        name="rows",
    )


def attn_in_kernel(qkv_w, dense_w, small, normed, grad, projected, attended_grad):
    three = projected.shape[1]
    projected[...] = dot_nn(normed[...], qkv_w[...]) + small[12:13, :three]
    attended_grad[...] = dot_nn(grad[...], dense_w[...]).astype(BF)


def attn_in(weights, small, normed, grad, *waits):
    rows, width = normed.shape
    heads = weights.shape[1] // 12
    at_once = 256
    return kernel_call(
        attn_in_kernel,
        (weights, weights, small, normed, grad),
        waits,
        grid=(rows // at_once,),
        in_specs=[
            pl.BlockSpec((width, 3 * heads), lambda i: (0, 0)),
            pl.BlockSpec((width, heads), lambda i: (0, 3)),
            whole(small.shape),
            row_block(at_once, width),
            row_block(at_once, width),
        ],
        out_specs=(row_block(at_once, 3 * heads), row_block(at_once, heads)),
        out_shape=(shaped((rows, 3 * heads), F32), shaped((rows, heads), BF)),
        compiler_params=params(BIG),
        cost_estimate=cost(8 * rows * width * heads, 6 * rows * width),
        name="attn_in",
    )


def expand_kernel(weight, normed, small, activated, slope):
    u = dot_nn(normed[...], weight[...]) + small[14:15]
    factor = (2.0 / np.pi) ** 0.5
    square = u * u
    bent = jnp.tanh(factor * u * (1.0 + 0.044715 * square))
    half = 0.5 + 0.5 * bent
    activated[...] = (u * half).astype(BF)
    rise = factor * (1.0 + 3.0 * 0.044715 * square)
    slope[...] = (half + 0.5 * u * (1.0 - bent * bent) * rise).astype(BF)


def expand_layer(weights, normed, small, *waits):
    rows, width = normed.shape
    cols = weights.shape[1] // 3
    at_once = 256
    return kernel_call(
        expand_kernel,
        (weights, normed, small),
        waits,
        grid=(rows // at_once,),
        in_specs=[
            pl.BlockSpec((width, cols), lambda i: (0, 1)),
            row_block(at_once, width),
            whole(small.shape),
        ],
        out_specs=(row_block(at_once, cols),) * 2,
        out_shape=(shaped((rows, cols), BF),) * 2,
        compiler_params=params(BIG),
        cost_estimate=cost(2 * rows * width * cols, 4 * rows * width, rows * cols),
        name="expand",
    )


def feed_back_kernel(weights, grad, slope, normed, activated, grad_turned, *refs):
    eg_out, bias_grad, *outs = refs[: 2 + 2 * RING]
    weight_v, grad_v, slope_v, normed_v, activated_v, turned_v, eg_v, hold, sems, out_sems = refs[
        2 + 2 * RING :
    ]
    step = pl.program_id(0)
    tile = grad.shape[0] // RING
    quarter = grad.shape[1] // RING

    def loads():
        cols = weight_v.shape[1]
        made = [(weights.at[:, pl.ds(2 * cols, cols)], weight_v)]
        for n in range(RING):
            made.append((grad.at[pl.ds(n * tile, tile)], grad_v.at[pl.ds(n * tile, tile)]))
        made += [
            (slope, slope_v), (normed, normed_v), (activated, activated_v), (grad_turned, turned_v)
        ]
        return [pltpu.make_async_copy(a, b, sems.at[n]) for n, (a, b) in enumerate(made)]

    def stores():
        made = [pltpu.make_async_copy(hold.at[n], out, out_sems.at[n]) for n, out in enumerate(outs)]
        return made + [pltpu.make_async_copy(eg_v, eg_out, out_sems.at[2 * RING])]

    @pl.when(step == 0)
    def _():
        copies = loads()
        for n in (0, 1, 5, 2, 3, 4, 6, 7, 8):
            copies[n].start()
        copies[0].wait()
        copies[5].wait()
        bias_grad[...] = jnp.zeros_like(bias_grad)

    for n in range(RING):

        @pl.when(step == n)
        def _(n=n):
            loads()[1 + n].wait()

    @pl.when(step < RING)
    def _():
        at = pl.ds(pl.multiple_of(step * tile, tile), tile)
        low = dot_nn(grad_v[at, :], weight_v[...]) * slope_v[at, :].astype(F32)
        low = low.astype(BF)
        eg_v[at, :] = low
        bias_grad[...] += jnp.sum(low.astype(F32), 0, keepdims=True)

    @pl.when(step == RING)
    def _():
        stores()[2 * RING].start()
        loads()[6].wait()

    @pl.when(step == 2 * RING)
    def _():
        loads()[7].wait()
        loads()[8].wait()

    def columns(first):
        return pl.ds(pl.multiple_of((step - first) * quarter, quarter), quarter)

    @pl.when((step >= RING) & (step < 2 * RING))
    def _():
        hold[step - RING] = dot_tn(normed_v[:, columns(RING)], eg_v[...]).astype(BF)

    @pl.when(step >= 2 * RING)
    def _():
        hold[step - RING] = dot_tn(turned_v[:, columns(2 * RING)], activated_v[...]).astype(BF)

    for n in range(2 * RING):

        @pl.when(step == n + RING)
        def _(n=n):
            stores()[n].start()

    @pl.when(step == 3 * RING - 1)
    def _():
        for copy in stores():
            copy.wait()


def feed_back(weights, grad, slope, normed, activated, grad_turned, *waits):
    rows, width = grad.shape
    cols = weights.shape[1] // 3
    depth = width // RING
    outs = kernel_call(
        feed_back_kernel,
        (weights, grad, slope, normed, activated, grad_turned),
        waits,
        grid=(3 * RING,),
        in_specs=[ANY] * 6,
        out_specs=(ANY, whole((1, cols))) + (ANY,) * (2 * RING),
        out_shape=(shaped((rows, cols), BF), shaped((1, cols), F32))
        + (shaped((depth, cols), BF),) * (2 * RING),
        scratch_shapes=[
            pltpu.VMEM((width, cols), BF),
            pltpu.VMEM((rows, width), BF),
            pltpu.VMEM((rows, cols), BF),
            pltpu.VMEM((rows, width), BF),
            pltpu.VMEM((rows, cols), BF),
            pltpu.VMEM((rows, width), BF),
            pltpu.VMEM((rows, cols), BF),
            pltpu.VMEM((2 * RING, depth, cols), BF),
            pltpu.SemaphoreType.DMA((RING + 5,)),
            pltpu.SemaphoreType.DMA((2 * RING + 1,)),
        ],
        compiler_params=params(BIG),
        cost_estimate=cost(6 * rows * width * cols, 20 * rows * width),
        name="feed_back",
    )
    quarters = [quarter.reshape(RING, -1, cols) for quarter in outs[2:]]
    return outs[0], outs[1], quarters[:RING], quarters[RING:]


def branch_kernel(rank, dense, reduce, activated, attended, small, branch, bias):
    heads = attended.shape[1]
    lanes = 2 * HEAD_DIM

    @pl.when(pl.program_id(0) == 0)
    def _():
        mine = small[12:13, 3 * heads :] + small[13:14, 3 * heads :]
        lane = lax.broadcasted_iota(jnp.int32, (1, lanes), 1)
        places = heads // HEAD_DIM
        side = (lane // HEAD_DIM) == rank[0] // (RING * RING // places)
        for n in range(RING * RING):
            part = mine[:, (n % places) * HEAD_DIM : (n % places + 1) * HEAD_DIM]
            part = jnp.concatenate([part, part], 1)
            here = rank[0] % (RING * RING // places) == n // places
            bias[:, n * lanes : (n + 1) * lanes] = jnp.where(side & here, part, 0.0)

    total = dot_nt(activated[...], reduce[...]) + dot_nt(attended[...], dense[...])
    branch[...] = (total + bias[...]).astype(BF)


def branch_layer(rank, activated, attended, weights, small, *waits):
    rows, cols = activated.shape
    heads = attended.shape[1]
    width = weights.shape[0]
    at_once = 256
    return kernel_call(
        branch_kernel,
        (rank, weights, weights, activated, attended, small),
        waits,
        grid=(rows // at_once,),
        in_specs=[SMEM]
        + [pl.BlockSpec((width, heads), lambda i: (0, 3))]
        + [pl.BlockSpec((width, cols), lambda i: (0, 2))]
        + [row_block(at_once, cols), row_block(at_once, heads), whole(small.shape)],
        out_specs=row_block(at_once, width),
        out_shape=shaped((rows, width), BF),
        scratch_shapes=[pltpu.VMEM((1, width), F32)],
        compiler_params=params(BIG),
        cost_estimate=cost(
            2 * rows * width * (cols + heads), 2 * (width + rows) * (cols + heads) + 2 * rows * width
        ),
        name="branch",
    )


def normed_grad_kernel(qkv_w, expand_w, proj_grad, expanded_grad, x_hat, part, sums):
    @pl.when(pl.program_id(0) == 0)
    def _():
        sums[...] = jnp.zeros_like(sums)

    total = dot_nt(proj_grad[...], qkv_w[...]) + dot_nt(expanded_grad[...], expand_w[...])
    part[...] = total.astype(BF)
    gain = jnp.sum(total * x_hat[...].astype(F32), 0, keepdims=True)
    offset = jnp.sum(total, 0, keepdims=True)
    sums[...] += jnp.concatenate([gain, offset], 0)


def normed_grad_layer(proj_grad, expanded_grad, weights, x_hat, *waits):
    rows, width = x_hat.shape
    cols, three = expanded_grad.shape[1], proj_grad.shape[1]
    depth = width // RING
    at_once = 256
    return kernel_call(
        normed_grad_kernel,
        (weights, weights, proj_grad, expanded_grad, x_hat),
        waits,
        grid=(rows // at_once,),
        in_specs=[pl.BlockSpec((width, three), lambda i: (0, 0))]
        + [pl.BlockSpec((width, cols), lambda i: (0, 1))]
        + [row_block(at_once, three), row_block(at_once, cols), row_block(at_once, width)],
        out_specs=(row_block(at_once, width), whole((2, width))),
        out_shape=(shaped((rows, width), BF), shaped((2, width), F32)),
        compiler_params=params(BIG),
        cost_estimate=cost(
            2 * rows * width * (cols + three), 2 * (width + rows) * (cols + three) + 4 * rows * width
        ),
        name="normed_grad",
    )


def weight_grad_kernel(count, *refs):
    lefts, rights = refs[:count], refs[count : 2 * count]
    *small, out0, out1, out2, out3, hold, sems = refs[2 * count :]
    outs = (out0, out1, out2, out3)
    step, last = pl.program_id(0), pl.num_programs(0) - 1
    cols = 0
    for a, b in zip(lefts, rights):
        hold[step, :, cols : cols + b.shape[1]] = dot_tn(a[...], b[...]).astype(BF)
        cols += b.shape[1]
    for ref in small:
        for n in range(RING):
            lanes = ref.shape[1]
            hold[step, n * lanes : (n + 1) * lanes, cols:] = ref[...]
    for n, out in enumerate(outs):

        @pl.when(step == n)
        def _(n=n, out=out):
            pltpu.make_async_copy(hold.at[n], out, sems.at[n]).start()

    @pl.when(step == last)
    def _():
        for n, out in enumerate(outs):
            pltpu.make_async_copy(hold.at[n], out, sems.at[n]).wait()


def weight_grad(pairs, small=None, waits=()):
    rows, width = pairs[0][0].shape
    more = [] if small is None else [small]
    cols = sum(right.shape[1] for _, right in pairs) + sum(extra.shape[1] for extra in more)
    at_once = width // RING

    def kernel(*refs):
        weight_grad_kernel(len(pairs), *refs)

    left = pl.BlockSpec((rows, at_once), lambda i: (0, i))
    quarters = kernel_call(
        kernel,
        (*[a for a, _ in pairs], *[b for _, b in pairs], *more),
        waits,
        grid=(RING,),
        in_specs=[left] * len(pairs)
        + [whole(right.shape) for _, right in pairs]
        + [whole(extra.shape) for extra in more],
        out_specs=(ANY,) * RING,
        out_shape=(shaped((at_once, cols), BF),) * RING,
        scratch_shapes=[
            pltpu.VMEM((RING, at_once, cols), BF),
            pltpu.SemaphoreType.DMA((RING,)),
        ],
        compiler_params=params(BIG),
        cost_estimate=cost(
            2 * rows * width * cols, 2 * (len(pairs) * rows * width + rows * cols + width * cols)
        ),
        name="weight_grad",
    )
    return [quarter.reshape(RING, -1, cols) for quarter in quarters]


def rolled(value, shift):
    return pltpu.roll(value, shift % value.shape[-1], value.ndim - 1)


def rotate(value, cos, sin_low, sin_high, sign):
    half = ROT // 2
    turned = rolled(value, -half) * sin_low + rolled(value, half) * sin_high
    return value * cos + sign * turned


def attention_kernel(
    projected, out_grad, cos, sin_low, sin_high, start, mixed, proj_grad, bias_grad
):
    rows, width = out_grad.shape
    lanes = cos.shape[1]
    scale = HEAD_DIM**-0.5
    tables = cos[...], sin_low[...], sin_high[...]
    lane = lax.broadcasted_iota(jnp.int32, (rows, lanes), 1)
    row_id = lax.broadcasted_iota(jnp.int32, (rows, rows), 0)
    col_id = lax.broadcasted_iota(jnp.int32, (rows, rows), 1)
    allowed = (col_id <= row_id) & (col_id >= start[:, 0:1])
    zero = jnp.zeros((rows, lanes), BF)
    for pair in range(width // lanes):
        at = [slice(j * width + pair * lanes, j * width + (pair + 1) * lanes) for j in range(3)]
        query_rot = (rotate(projected[:, at[0]], *tables, 1.0).astype(BF) * scale).astype(BF)
        key_rot = rotate(projected[:, at[1]], *tables, 1.0).astype(BF)
        value_rows = projected[:, at[2]].astype(BF)
        grad_rows = out_grad[:, at[0]]
        sums = None
        for head in range(lanes // HEAD_DIM):
            mine = (lane >= head * HEAD_DIM) & (lane < (head + 1) * HEAD_DIM)
            q_h = jnp.where(mine, query_rot, zero)
            k_h = jnp.where(mine, key_rot, zero)
            v_h = jnp.where(mine, value_rows, zero)
            g_h = jnp.where(mine, grad_rows, zero)
            scores = jnp.where(allowed, dot_nt(q_h, key_rot), -1000000000.0)
            top = jnp.max(scores, -1, keepdims=True)
            expd = jnp.exp(scores - top)
            probs = expd * (1.0 / jnp.sum(expd, -1, keepdims=True))
            prob_low = probs.astype(BF)
            prob_grad = dot_nt(g_h, value_rows)
            row_dot = jnp.sum(probs * prob_grad, -1, keepdims=True)
            score_grad = (probs * (prob_grad - row_dot)).astype(BF)
            parts = (
                dot_nn(prob_low, v_h),
                dot_nn(score_grad, k_h),
                dot_tn(score_grad, q_h),
                dot_tn(prob_low, g_h),
            )
            sums = parts if sums is None else tuple(a + b for a, b in zip(sums, parts))
        mixed[:, at[0]] = sums[0].astype(BF)
        grads = (
            rotate(sums[1] * scale, *tables, -1.0),
            rotate(sums[2], *tables, -1.0),
            sums[3],
        )
        for j in range(3):
            low = grads[j].astype(BF)
            proj_grad[:, at[j]] = low
            bias_grad[0, :, at[j]] = jnp.sum(low.astype(F32), 0, keepdims=True)


def attention(projected, out_grad, cos, sin_low, sin_high, start, pack_rows, *waits):
    rows, width = out_grad.shape
    lanes = cos.shape[1]
    packs = rows // pack_rows
    return kernel_call(
        attention_kernel,
        (projected, out_grad, cos, sin_low, sin_high, start),
        waits,
        grid=(packs,),
        in_specs=[row_block(pack_rows, 3 * width), row_block(pack_rows, width)]
        + [row_block(pack_rows, lanes)] * 4,
        out_specs=(
            row_block(pack_rows, width),
            row_block(pack_rows, 3 * width),
            pl.BlockSpec((1, 1, 3 * width), lambda p: (p, 0, 0)),
        ),
        out_shape=(
            shaped((rows, width), BF),
            shaped((rows, 3 * width), BF),
            shaped((packs, 1, 3 * width), F32),
        ),
        compiler_params=params(BIG),
        cost_estimate=cost(
            14 * rows * pack_rows * width, rows * width * 32, rows * pack_rows * width // HEAD_DIM
        ),
        name="attention",
    )


def pick(first, a, b):
    return jnp.where(first, a, b), jnp.where(first, b, a)


def three_parts(value):
    high = lax.reduce_precision(value, 8, 7)
    rest = value - high
    mid = lax.reduce_precision(rest, 8, 7)
    return [high, mid, rest - mid]


def body(
    hidden_in,
    seq_lengths,
    norm_gain,
    norm_offset,
    attn_weight,
    attn_bias,
    dense_weight,
    dense_bias,
    expand_weight,
    expand_bias,
    reduce_weight,
    reduce_bias,
    out_grad,
):
    at_yhi, at_x, at_z, at_ylo, at_core = (lax.axis_index(a) for a in AXES)
    first_yhi, first_ylo, first_core = at_yhi == 0, at_ylo == 0, at_core == 0
    local_rows, width = hidden_in.shape
    pack_rows = local_rows * RING
    at_tensor = at_ylo * 2 + at_core
    column_rank = at_tensor * 2 + at_yhi
    plane = RING * RING
    at_plane = at_x * RING + at_z

    place = np.arange(plane, dtype=np.int32)
    x, z = (place // RING - at_x) % RING, (place % RING - at_z) % RING
    inner, outer = jnp.where(first_core, x, z), jnp.where(first_core, z, x)
    order = np.array([0, 2, 3, 1], np.int32)

    def position(step):
        return sum(jnp.where(step == n, order[n], 0) for n in range(1, RING))

    turned = (position(outer) * RING + position(inner)).astype(jnp.int32)

    lanes = 2 * HEAD_DIM
    block_rows, cols = expand_weight.shape[0], expand_weight.shape[1] // 2
    heads = cols // 4

    unit = norm_gain.shape[0]
    norms = jnp.stack(three_parts(norm_gain) + three_parts(norm_offset))
    lengths = seq_lengths[0]
    count = lengths.shape[0]
    small = lax.dynamic_update_slice(
        jnp.zeros((16, cols), F32),
        norms,
        (at_plane // 8 * 6, at_plane % 8 * 8 * unit + at_yhi * 4 * unit + at_tensor * unit),
    )
    two = jnp.concatenate([lengths // 16, lengths % 16]).astype(F32)
    small = lax.dynamic_update_slice(small, two[None], (15, at_yhi * 2 * count)).astype(BF)

    own, other = split_columns(
        at_yhi.reshape(1).astype(jnp.int32),
        attn_weight, dense_weight.T, expand_weight, reduce_weight.T,
    )
    got = swap(other, "yhi")
    block = jnp.concatenate(pick(first_yhi, own, got), 0)
    weights = lax.all_gather(block, ("x", "z"), axis=0, tiled=True)

    small = small + swap(small, "yhi")
    two = small[15, : 4 * count].astype(F32).reshape(2, 2, count)
    length_rows = (two[:, 0] * 16.0 + two[:, 1]).astype(jnp.int32)
    biases = jnp.stack([dense_bias, reduce_bias])
    biases = jnp.concatenate([jnp.stack([attn_bias, 0 * attn_bias]), biases[:, None]], 1)
    bias_rows = lax.dynamic_update_slice(
        jnp.zeros((2, 4, heads), BF), biases, (0, 0, at_plane * unit)
    ).reshape(2, cols)
    expand_row = lax.dynamic_update_slice(
        jnp.zeros((2, cols), BF), expand_bias[None], (0, at_plane * expand_bias.shape[0])
    )
    small = jnp.concatenate([small[:12], bias_rows, expand_row], 0)

    for axis in ("x", "z"):
        for odd in range(2):
            small = small + lax.ppermute(small, axis, axis_swaps(odd))
    parts = jnp.where((np.arange(16) < 12)[:, None], small, jnp.zeros_like(small))
    others = swap(parts, "ylo")
    small = (small + others + swap(parts + others, "core")).astype(F32)

    own_rows = pair_columns(hidden_in, out_grad, got)
    below, above = move_y(own_rows, 1), move_y(own_rows, -1)
    one = (1,) + own_rows.shape[1:]
    far_hidden, far_grad = take_parts((below, one, (0, 0, 0)), (above, one, (1, 0, 0)))
    far_hidden, far_grad = move_y(far_hidden, 1), move_y(far_grad, -1)
    far_rows = jnp.concatenate([far_hidden, far_grad], 0)
    sources = [
        ref for rows in (own_rows, below, above, far_rows) for ref in (rows, swap(rows, "core"))
    ]
    at_y = at_yhi * 2 + at_ylo
    chips = jnp.stack([at_y, (at_y + 3) % RING, (at_y + 1) % RING, (at_y + 2) % RING, at_core])
    chips = chips.astype(jnp.int32)

    ends = jnp.cumsum(length_rows, 1)
    row_ids = jnp.arange(pack_rows, dtype=jnp.int32)
    begun = row_ids[None, :, None] >= ends[:, None, :]
    start = jnp.max(jnp.where(begun, ends[:, None, :], 0), 2).reshape(-1, 1)
    position = (jnp.tile(row_ids, 2)[:, None] - start).astype(F32)
    lane = np.arange(lanes) % HEAD_DIM
    half = ROT // 2
    inverse = np.float32(10000.0) ** (np.float32(-2.0) * (lane % half).astype(np.float32) / ROT)
    angles = position * inverse.astype(np.float32)[None, :]
    cos = jnp.where((lane < ROT)[None, :], jnp.cos(angles), 1.0)
    sine = jnp.sin(angles)
    sin_low = jnp.where((lane < half)[None, :], -sine, 0.0)
    sin_high = jnp.where(((lane >= half) & (lane < ROT))[None, :], sine, 0.0)
    start = jnp.broadcast_to(start, (start.shape[0], lanes))

    normed, normed_turned, x_hat, grad_all, grad_turned, grad_sum = rows_layer(
        chips, turned, small, sources, cos, sin_low, sin_high, start
    )
    activated, slope = expand_layer(weights, normed, small)
    expanded_grad, expand_bias_grad, expand_1, reduce_1 = feed_back(
        weights, grad_all, slope, normed_turned, activated, grad_turned
    )
    expand_sent = ring_send(expand_1, False, 1)
    reduce_sent = ring_send(reduce_1, False, -1)
    projected, attended_grad = attn_in(weights, small, normed, grad_all, expanded_grad)
    attended, proj_grad, attn_bias_grad = attention(
        projected, attended_grad, cos, sin_low, sin_high, start, pack_rows
    )
    branch = branch_layer(
        column_rank.reshape(1).astype(jnp.int32), activated, attended, weights, small
    )
    expand_up, reduce_up, branch = add_pairs(
        [(expand_1[2], expand_sent[0]), (reduce_1[1], reduce_sent[0])],
        branch,
        (expand_sent[1], reduce_sent[1]),
    )
    expand_last, reduce_last = move(expand_up, False, 1), move(reduce_up, False, -1)
    attn_1 = weight_grad(
        [(normed_turned, proj_grad), (grad_turned, attended)], None, (expand_up,)
    )
    attn_sent = ring_send(attn_1, False, -1)
    feed_2 = add_lines(
        [
            (expand_1[0], expand_sent[1], expand_last),
            (reduce_1[0], reduce_sent[1], reduce_last),
        ],
        waits=(attn_1[0],),
    )
    feed_sent = ring_send(feed_2, True, 1)
    normed_part, norm_sums = normed_grad_layer(
        proj_grad, expanded_grad, weights, x_hat, attn_1[0], feed_2[0]
    )
    attn_up, feed_up, normed_part = add_pairs(
        [(attn_1[1], attn_sent[0]), (feed_2[2], feed_sent[0])],
        normed_part,
        (attn_sent[1], feed_sent[1]),
    )
    attn_last, feed_last = move(attn_up, False, -1), move(feed_up, True, 1)

    places = heads // block_rows
    out_bias_grad = lax.dynamic_slice(
        grad_sum.reshape(plane, 2, block_rows),
        (column_rank % (plane // places) * places, column_rank // (plane // places), 0),
        (places, 1, block_rows),
    ).reshape(1, heads)
    attn_row = jnp.concatenate([jnp.sum(attn_bias_grad, 0), out_bias_grad], 1)
    small_sums = jnp.concatenate(
        [norm_sums.reshape(4, cols), attn_row, expand_bias_grad, jnp.zeros((10, cols), F32)], 0
    )
    for odd in range(2):
        small_sums = small_sums + lax.ppermute(small_sums, ("x", "z", "core"), pair_swaps(odd))

    branch = lax.psum_scatter(branch, COLUMN, scatter_dimension=0, tiled=True)
    block_out = output_layer(own_rows, branch)
    normed_grad = lax.psum_scatter(normed_part, COLUMN, scatter_dimension=0, tiled=True)
    input_grad = input_grad_layer(own_rows, normed_grad, small)

    attn_2 = add_lines(
        [(attn_1[0], attn_sent[1], attn_last)], [fold(small_sums).astype(BF)], (block_out,)
    )
    attn_sent = ring_send(attn_2, True, -1)
    feed_total = add_up(feed_2[0], feed_sent[1], feed_last).reshape(2, block_rows, 2 * cols)
    keep, send = pick(first_yhi, feed_total[0], feed_total[1])
    feed_low, feed_high = pick(first_yhi, keep, swap(send.astype(BF), "yhi").astype(F32))
    expand_low, reduce_low = feed_low[:, :cols], feed_low[:, cols:]
    expand_high, reduce_high = feed_high[:, :cols], feed_high[:, cols:]

    attn_up, here = add_pairs([(attn_2[1], attn_sent[0])], attn_2[0])
    attn_total = add_up(here, attn_sent[1], move(attn_up, True, -1))
    small_total = unfold(attn_total[:, cols:])
    norm_total = lax.dynamic_slice_in_dim(
        small_total[:4].reshape(2, width), at_plane * 8 * unit, 8 * unit, 1
    ).reshape(2, 2, 4 * unit)
    attn_total = attn_total[:, :cols].reshape(2, block_rows, cols)
    keep, send = pick(first_yhi, attn_total[0], attn_total[1])
    norm_keep, norm_send = pick(first_yhi, norm_total[:, 0], norm_total[:, 1])
    rider = jnp.pad(norm_send, ((0, 14), (0, cols - 4 * unit)))
    got = swap(jnp.concatenate([send, rider], 0).astype(BF), "yhi")
    attn_low, attn_high = pick(first_yhi, keep, got[:block_rows].astype(F32))
    keep = norm_keep + got[block_rows : block_rows + 2, : 4 * unit].astype(F32)
    keep = keep.reshape(2, 2, 2, unit)
    keep, send = pick(first_ylo, keep[:, 0], keep[:, 1])
    keep = keep + swap(send, "ylo")
    keep, send = pick(first_core, keep[:, 0], keep[:, 1])
    norm_grads = keep + swap(send, "core")

    attn_cols = [
        jnp.concatenate([attn_low[:, at : at + heads], attn_high[:, at : at + heads]], 1)
        for at in range(0, cols, heads)
    ]
    bias_total = lax.dynamic_slice_in_dim(
        small_total[4].reshape(4, heads), at_plane * unit, unit, 1
    )
    expand_b_grad = lax.dynamic_slice_in_dim(
        small_total[5], at_plane * expand_bias.shape[0], expand_bias.shape[0]
    )
    return (
        block_out,
        input_grad,
        norm_grads[0],
        norm_grads[1],
        jnp.stack(attn_cols[:3]),
        bias_total[:3],
        attn_cols[3].T,
        bias_total[3],
        jnp.concatenate([expand_low, expand_high], 1),
        expand_b_grad,
        jnp.concatenate([reduce_low, reduce_high], 1).T,
        bias_total[3],
    )


def solution(mesh):
    split = Mesh(mesh.devices.reshape(2, RING, RING, 2, 2), AXES)
    dp, tensor = ("yhi", "x", "z"), ("ylo", "core")
    rows = P(dp + tensor, None)
    vector = P(dp + tensor)
    bias = P(tensor + dp)
    parameters = (
        vector,
        vector,
        P(None, dp, tensor),
        P(None, tensor + dp),
        P(tensor, dp),
        bias,
        P(dp, tensor),
        bias,
        P(tensor, dp),
        bias,
    )
    return jax.shard_map(
        body,
        mesh=split,
        in_specs=(rows, P(dp, None)) + parameters + (rows,),
        out_specs=(rows, rows) + parameters,
        check_vma=False,
    )
```

```python
import numpy as np
import jax
import jax.numpy as jnp
from jax import lax
from jax.experimental import pallas as pl
from jax.experimental.pallas import tpu as pltpu
from jax.sharding import Mesh, PartitionSpec as P

HEAD_DIM = 64
ROT = 32
RING = 4
AXES = ("yhi", "x", "z", "ylo", "core")
COLUMN = ("yhi", "ylo", "core")
BF = jnp.bfloat16
F32 = jnp.float32
MIB = 1 << 20
BIG = 58
SMALL = 16


def ring_pairs(first_ring, step):
    pairs = []
    for x in range(RING):
        for z in range(RING):
            for core in range(2):
                along_x = (core == 0) == first_ring
                to_x = (x + step) % RING if along_x else x
                to_z = z if along_x else (z + step) % RING
                pairs.append(((x * RING + z) * 2 + core, (to_x * RING + to_z) * 2 + core))
    return pairs


def move(value, first_ring, step):
    return lax.ppermute(value, ("x", "z", "core"), ring_pairs(first_ring, step))


def axis_swaps(odd):
    return [(n, (n + (1 if n % 2 == odd else -1)) % RING) for n in range(RING)]


def move_y(value, step):
    pairs = [(y, (y + step) % RING) for y in range(RING)]
    return lax.ppermute(value, ("yhi", "ylo"), pairs)


def swap(value, axis):
    return lax.ppermute(value, axis, [(0, 1), (1, 0)])


def ring_send(blocks, first_ring, way):
    _, minus, plus, far = blocks
    direct = move(minus, first_ring, -1) if way > 0 else move(plus, first_ring, 1)
    return move(far, first_ring, way), direct


def ring_terms(blocks):
    here, minus, plus, far = blocks
    return here, move(minus, True, -1), move(plus, True, 1), move(far, True, 2)


ANY = pl.BlockSpec(memory_space=pl.ANY)
SMEM = pl.BlockSpec(memory_space=pltpu.SMEM)


def whole(shape):
    return pl.BlockSpec(shape, lambda *at: (0,) * len(shape))


def row_block(rows, cols):
    return pl.BlockSpec((rows, cols), lambda i: (i, 0))


def shaped(shape, dtype):
    return jax.ShapeDtypeStruct(shape, dtype)


def kernel_call(kernel, operands, waits, *, in_specs, **options):
    count, more = len(operands), len(waits)

    def run(*refs):
        kernel(*refs[:count], *refs[count + more :])

    in_specs = list(in_specs) + [ANY] * more
    scalars = count - len(in_specs) + more
    if scalars:
        parts = {key: options.pop(key) for key in ("grid", "out_specs", "scratch_shapes")}
        options["grid_spec"] = pltpu.PrefetchScalarGridSpec(
            num_scalar_prefetch=scalars, in_specs=in_specs, **parts
        )
    else:
        options["in_specs"] = in_specs
    return pl.pallas_call(run, **options)(*operands, *waits)


def parts_kernel(*refs):
    count = len(refs) // 2
    for ref, out in zip(refs[:count], refs[count:]):
        out[...] = ref[...]


def take_parts(*chosen):
    specs = [pl.BlockSpec(shape, lambda i, at=at: at) for _, shape, at in chosen]
    return kernel_call(
        parts_kernel,
        tuple(array for array, _, _ in chosen),
        (),
        grid=(1,),
        in_specs=specs,
        out_specs=tuple(whole(shape) for _, shape, _ in chosen),
        out_shape=tuple(shaped(shape, array.dtype) for array, shape, _ in chosen),
        compiler_params=params(SMALL),
        cost_estimate=cost(0, 4 * sum(int(np.prod(shape)) for _, shape, _ in chosen)),
        name="take_parts",
    )


def add_pairs_kernel(*refs):
    count = (len(refs) - 2) // 3
    for n in range(count):
        a, b, out = refs[2 * n], refs[2 * n + 1], refs[2 * count + 1 + n]
        out[...] = (a[...].astype(F32) + b[...].astype(F32)).astype(BF)


def add_pairs(pairs, carried, waits=()):
    shapes = [a.shape for a, _ in pairs]
    flat = [term.reshape(-1, term.shape[-1]) for pair in pairs for term in pair]
    halves = [row_block(term.shape[0] // 2, term.shape[1]) for term in flat]
    *sums, carried = kernel_call(
        add_pairs_kernel,
        (*flat, carried),
        waits,
        grid=(2,),
        in_specs=halves + [ANY],
        out_specs=tuple(halves[::2]) + (ANY,),
        out_shape=tuple(shaped(term.shape, BF) for term in flat[::2])
        + (shaped(carried.shape, carried.dtype),),
        input_output_aliases={len(flat): len(pairs)},
        compiler_params=params(BIG),
        cost_estimate=cost(0, 3 * sum(term.size for term in flat)),
        name="add_pairs",
    )
    return [total.reshape(shape) for total, shape in zip(sums, shapes)] + [carried]


def add_lines_kernel(*refs):
    outs = refs[-RING:]
    sources, at = refs[:-RING], 0
    for n in range(0, len(sources), 3):
        total = sum(ref[...].astype(F32) for ref in sources[n : n + 3])
        for i, out in enumerate(outs):
            out[:, at : at + total.shape[-1]] = total[i].astype(BF)
        at += total.shape[-1]


def add_lines(lines, waits=()):
    operands = [term for terms in lines for term in terms]
    rows = operands[0].shape[1]
    cols = sum(terms[0].shape[2] for terms in lines)
    at_once = rows // 2
    specs = [
        pl.BlockSpec((RING, at_once, term.shape[2]), lambda i: (0, i, 0)) for term in operands
    ]
    return kernel_call(
        add_lines_kernel,
        tuple(operands),
        waits,
        grid=(2,),
        in_specs=specs,
        out_specs=(row_block(at_once, cols),) * RING,
        out_shape=(shaped((rows, cols), BF),) * RING,
        compiler_params=params(SMALL),
        cost_estimate=cost(0, 8 * RING * rows * cols),
        name="add_lines",
    )


def finish_kernel(count, at_yhi, *refs):
    outs = refs[count * (len(refs) // (count + 1)) :]
    for n, out in enumerate(outs):
        total = sum(ref[...].astype(F32) for ref in refs[n * count : (n + 1) * count])
        out[...] = total.astype(out.dtype)


def finish_sums(at_yhi, terms, cols, waits=()):
    rows, more = terms[0].shape[0], terms[0].shape[1] - cols
    half = rows // 2
    keep = pl.BlockSpec((half, cols), lambda i, at: (at[0], 0))
    send = pl.BlockSpec((half, cols), lambda i, at: (1 - at[0], 0))
    out = pl.BlockSpec((half, cols), lambda i, at: (0, 0))
    count = len(terms)
    specs, outs = [keep] * count + [send] * count, [out] * 2
    shapes = [shaped((half, cols), F32), shaped((half, cols), BF)]
    if more:
        specs += [pl.BlockSpec((rows, more), lambda i, at: (0, cols // more))] * count
        outs.append(pl.BlockSpec((rows, more), lambda i, at: (0, 0)))
        shapes.append(shaped((rows, more), F32))

    def kernel(*refs):
        finish_kernel(count, *refs)

    return kernel_call(
        kernel,
        (at_yhi, *(tuple(terms) * (len(specs) // count))),
        waits,
        grid=(1,),
        in_specs=specs,
        out_specs=tuple(outs),
        out_shape=tuple(shapes),
        scratch_shapes=(),
        compiler_params=params(SMALL),
        cost_estimate=cost(0, 8 * rows * cols),
        name="finish_sums",
    )


def join_kernel(layout, at_yhi, keep, got, *outs):
    part = jnp.where(pl.program_id(0) == 0, keep[...], got[...].astype(F32))
    for (count, first, width), out in zip(layout, outs):
        for n in range(count):
            block = part[:, first + n * width : first + (n + 1) * width]
            if len(out.shape) == 3:
                out[n] = block
            else:
                out[...] = block


def join_halves(at_yhi, keep, got, layout, waits=()):
    rows, cols = keep.shape

    def kernel(*refs):
        join_kernel(layout, *refs)

    def side(i, at):
        return at[0] + i * (1 - 2 * at[0])

    specs, shapes = [], []
    for count, _, width in layout:
        lead = (count,) if count > 1 else ()
        zeros = (0,) * (len(lead) + 1)
        specs.append(
            pl.BlockSpec(lead + (rows, width), lambda i, at, zeros=zeros: (*zeros, side(i, at)))
        )
        shapes.append(shaped(lead + (rows, 2 * width), F32))
    here = pl.BlockSpec((rows, cols), lambda i, at: (0, 0))
    return kernel_call(
        kernel,
        (at_yhi, keep, got),
        waits,
        grid=(2,),
        in_specs=[here, here],
        out_specs=tuple(specs),
        out_shape=tuple(shapes),
        scratch_shapes=(),
        compiler_params=params(BIG),
        cost_estimate=cost(0, 12 * rows * cols),
        name="join_halves",
    )


def params(megabytes):
    return pltpu.CompilerParams(vmem_limit_bytes=megabytes * MIB)


def cost(flops, moved, special=0):
    return pl.CostEstimate(flops=flops, bytes_accessed=moved, transcendentals=special)


def dot_nn(a, b):
    return jnp.dot(a, b, preferred_element_type=F32)


def dot_nt(a, b):
    return lax.dot_general(a, b, (((1,), (1,)), ((), ())), preferred_element_type=F32)


def dot_tn(a, b):
    return lax.dot_general(a, b, (((0,), (0,)), ((), ())), preferred_element_type=F32)


def split_kernel(at_yhi, *refs):
    ins, outs = refs[:8], refs[8:]
    for n, out in enumerate(outs):
        attn, *others = ins[4 * n : 4 * n + 4]
        at = 0
        for part in [attn[j] for j in range(3)] + [ref[...] for ref in others]:
            out[:, at : at + part.shape[1]] = part
            at += part.shape[1]


def split_columns(at_yhi, attn, dense, expand, reduce):
    rows, cols = expand.shape[0], expand.shape[1] // 2
    ins = []
    for n in range(2):

        def side(at, n=n):
            return at[0] if n == 0 else 1 - at[0]

        ins.append(pl.BlockSpec((3, rows, cols // 4), lambda i, at, side=side: (0, 0, side(at))))
        for width in (cols // 4, cols, cols):
            ins.append(pl.BlockSpec((rows, width), lambda i, at, side=side: (0, side(at))))
    return pl.pallas_call(
        split_kernel,
        grid_spec=pltpu.PrefetchScalarGridSpec(
            num_scalar_prefetch=1,
            grid=(1,),
            in_specs=ins,
            out_specs=(whole((rows, 3 * cols)),) * 2,
        ),
        out_shape=(shaped((rows, 3 * cols), BF),) * 2,
        compiler_params=params(BIG),
        cost_estimate=cost(0, 6 * rows * cols * 4),
        name="split_columns",
    )(at_yhi, *[attn, dense, expand, reduce] * 2)


def paired(rows):
    lanes = 2 * HEAD_DIM
    low = lax.broadcasted_iota(jnp.int32, (rows.shape[0], lanes), 1) < HEAD_DIM
    half = rows.shape[1] // 2
    for k in range(half // lanes):
        a = rows[:, k * lanes : (k + 1) * lanes]
        b = rows[:, half + k * lanes : half + (k + 1) * lanes]
        yield 2 * k * lanes, jnp.where(low, a, pltpu.roll(b, HEAD_DIM, 1))
        yield (2 * k + 1) * lanes, jnp.where(low, pltpu.roll(a, HEAD_DIM, 1), b)


def unpaired(rows):
    lanes = 2 * HEAD_DIM
    low = lax.broadcasted_iota(jnp.int32, (rows.shape[0], lanes), 1) < HEAD_DIM
    half = rows.shape[1] // 2
    for k in range(half // lanes):
        a = rows[:, 2 * k * lanes : (2 * k + 1) * lanes]
        b = rows[:, (2 * k + 1) * lanes : (2 * k + 2) * lanes]
        yield k * lanes, jnp.where(low, a, pltpu.roll(b, HEAD_DIM, 1))
        yield half + k * lanes, jnp.where(low, pltpu.roll(a, HEAD_DIM, 1), b)


def pair_kernel(hidden, grad, out):
    for n, ref in enumerate((hidden, grad)):
        for at, block in paired(ref[...].astype(F32)):
            out[n, :, at : at + block.shape[1]] = block.astype(BF)


def pair_columns(hidden, grad, *waits):
    rows, width = hidden.shape
    at_once = rows // 2
    return kernel_call(
        pair_kernel,
        (hidden, grad),
        waits,
        grid=(2,),
        in_specs=[row_block(at_once, width)] * 2,
        out_specs=pl.BlockSpec((2, at_once, width), lambda i: (0, i, 0)),
        out_shape=shaped((2, rows, width), BF),
        compiler_params=params(SMALL),
        cost_estimate=cost(0, 8 * rows * width),
        name="pair_columns",
    )


def output_kernel(hidden, branch, out):
    total = hidden[0].astype(F32) + branch[...].astype(F32)
    for at, block in unpaired(total):
        out[:, at : at + block.shape[1]] = block.astype(BF)


def own_block(which, rows, width):
    return pl.BlockSpec((1, rows, width), lambda i: (which, i, 0))


def output_layer(own, branch, *waits):
    _, rows, width = own.shape
    at_once = rows // 2
    return kernel_call(
        output_kernel,
        (own, branch),
        waits,
        grid=(2,),
        in_specs=[own_block(0, at_once, width), row_block(at_once, width)],
        out_specs=row_block(at_once, width),
        out_shape=shaped((rows, width), BF),
        compiler_params=params(SMALL),
        cost_estimate=cost(0, 6 * rows * width),
        name="output",
    )


def input_grad_kernel(hidden, grad, normed_grad, small, out):
    rows = hidden[0].astype(F32)
    center = rows - jnp.mean(rows, -1, keepdims=True)
    spread = lax.rsqrt(jnp.mean(center * center, -1, keepdims=True) + 1e-05)
    x_hat = center * spread
    gain, _ = norm_rows(small)
    scaled = normed_grad[...].astype(F32) * gain
    total = grad[0].astype(F32) + spread * (
        scaled
        - jnp.mean(scaled, -1, keepdims=True)
        - x_hat * jnp.mean(scaled * x_hat, -1, keepdims=True)
    )
    for at, block in unpaired(total):
        out[:, at : at + block.shape[1]] = block.astype(BF)


def input_grad_layer(own, normed_grad, small, *waits):
    _, rows, width = own.shape
    at_once = rows // 2
    return kernel_call(
        input_grad_kernel,
        (own, own, normed_grad, small),
        waits,
        grid=(2,),
        in_specs=[own_block(n, at_once, width) for n in range(2)]
        + [row_block(at_once, width), whole(small.shape)],
        out_specs=row_block(at_once, width),
        out_shape=shaped((rows, width), BF),
        compiler_params=params(SMALL),
        cost_estimate=cost(0, 8 * rows * width),
        name="input_grad",
    )


def put_in_turn(rows, turned, out):
    lanes = 2 * HEAD_DIM
    for n in range(rows.shape[1] // lanes):
        at = pl.multiple_of(turned[n] * lanes, lanes)
        out[:, pl.ds(at, lanes)] = rows[:, n * lanes : (n + 1) * lanes].astype(out.dtype)


def fold(small):
    return small.reshape(16, -1, 128).transpose(1, 0, 2).reshape(-1, 128)


def unfold(small):
    return small.reshape(-1, 16, 128).transpose(1, 0, 2).reshape(16, -1)


def norm_rows(small):
    def row(at):
        return small[at : at + 1] + small[at + 1 : at + 2] + small[at + 2 : at + 3]

    gain = jnp.concatenate([row(0), row(6)], 1)
    offset = jnp.concatenate([row(3), row(9)], 1)
    return gain, offset


def load_rows(chips, sources, held, sems, step):
    copies = []
    for n, ref in enumerate(sources):
        core = chips[RING] if n % 2 == 0 else 1 - chips[RING]
        copies.append(pltpu.make_async_copy(ref, held.at[n // 2, core], sems.at[n]))

    @pl.when(step == 0)
    def _():
        for copy in copies:
            copy.start()

    for n in range(RING):

        @pl.when(step == n)
        def _(n=n):
            copies[2 * n].wait()
            copies[2 * n + 1].wait()

    rows = held[step]
    return rows.reshape(-1, rows.shape[-1])


def chip_block(rows, cols):
    return pl.BlockSpec((rows, cols), lambda i, chips: (chips[i], 0))


def prefetched(specs):
    return [
        spec
        if spec.index_map is None
        else pl.BlockSpec(spec.block_shape, lambda i, chips, at=spec.index_map: at(i))
        for spec in specs
    ]


def rows_kernel(chips, turned, small, *refs):
    sources, rest = refs[: 2 * RING], refs[2 * RING :]
    normed, normed_turned, x_hat, grad, grad_turned, grad_sum, held, grad_held, sems, grad_sems = rest
    step = pl.program_id(0)

    @pl.when(step == 0)
    def _():
        grad_sum[...] = jnp.zeros_like(grad_sum)

    rows = load_rows(chips, [hidden_of(ref) for ref in sources], held, sems, step).astype(F32)
    gain, offset = norm_rows(small)
    center = rows - jnp.mean(rows, -1, keepdims=True)
    scaled = center * lax.rsqrt(jnp.mean(center * center, -1, keepdims=True) + 1e-05)
    x_hat[...] = scaled.astype(BF)
    normed[...] = (scaled * gain + offset).astype(BF)
    put_in_turn(normed, turned, normed_turned)
    rows = load_rows(chips, [grad_of(ref) for ref in sources], grad_held, grad_sems, step)
    grad[...] = rows
    put_in_turn(grad, turned, grad_turned)
    grad_sum[...] += jnp.sum(rows.astype(F32), 0, keepdims=True)


def hidden_of(ref):
    return ref.at[0] if len(ref.shape) == 3 else ref


def grad_of(ref):
    return ref.at[1] if len(ref.shape) == 3 else ref


def rows_layer(chips, turned, small, sources, *waits):
    local_rows, width = sources[0].shape[-2:]
    rows = 2 * RING * local_rows
    at_once = 2 * local_rows
    return kernel_call(
        rows_kernel,
        (chips, turned, small, *sources),
        waits,
        grid=(RING,),
        in_specs=[SMEM] + prefetched([whole(small.shape)]) + [ANY] * len(sources),
        out_specs=(chip_block(at_once, width),) * 5 + tuple(prefetched([whole((1, width))])),
        out_shape=(shaped((rows, width), BF),) * 5 + (shaped((1, width), F32),),
        scratch_shapes=[pltpu.VMEM((RING, 2, local_rows, width), BF)] * 2
        + [pltpu.SemaphoreType.DMA((2 * RING,))] * 2,
        compiler_params=params(BIG),
        cost_estimate=cost(0, 14 * rows * width),
        name="rows",
    )


def expand_kernel(weight, qkv_w, normed, small, activated, slope, projected):
    projected[...] = dot_nn(normed[...], qkv_w[...]) + small[12:13, : projected.shape[1]]
    u = dot_nn(normed[...], weight[...]) + small[14:15]
    factor = (2.0 / np.pi) ** 0.5
    square = u * u
    bent = jnp.tanh(factor * u * (1.0 + 0.044715 * square))
    half = 0.5 + 0.5 * bent
    activated[...] = (u * half).astype(BF)
    rise = factor * (1.0 + 3.0 * 0.044715 * square)
    slope[...] = (half + 0.5 * u * (1.0 - bent * bent) * rise).astype(BF)


def expand_layer(weights, normed, small, *waits):
    rows, width = normed.shape
    cols = weights.shape[1] // 3
    three = cols // 4 * 3
    at_once = 256
    return kernel_call(
        expand_kernel,
        (weights, weights, normed, small),
        waits,
        grid=(rows // at_once,),
        in_specs=[
            pl.BlockSpec((width, cols), lambda i: (0, 1)),
            pl.BlockSpec((width, three), lambda i: (0, 0)),
            row_block(at_once, width),
            whole(small.shape),
        ],
        out_specs=(row_block(at_once, cols),) * 2 + (row_block(at_once, three),),
        out_shape=(shaped((rows, cols), BF),) * 2 + (shaped((rows, three), F32),),
        compiler_params=params(BIG),
        cost_estimate=cost(2 * rows * width * (cols + three), 4 * rows * width, rows * cols),
        name="expand",
    )


def feed_back_kernel(weights, grad, slope, normed, activated, grad_turned, *refs):
    eg_out, bias_grad, attended_grad, *outs = refs[: 3 + 2 * RING]
    weight_v, dense_v, grad_v, slope_v, normed_v, activated_v, turned_v, eg_v, hold, *rest = refs[
        3 + 2 * RING :
    ]
    sems, out_sems = rest
    step = pl.program_id(0)
    tile = grad.shape[0] // RING
    quarter = grad.shape[1] // RING

    def loads():
        cols = weight_v.shape[1]
        made = [(weights.at[:, pl.ds(2 * cols, cols)], weight_v)]
        for n in range(RING):
            made.append((grad.at[pl.ds(n * tile, tile)], grad_v.at[pl.ds(n * tile, tile)]))
        made += [
            (slope, slope_v), (normed, normed_v), (activated, activated_v), (grad_turned, turned_v),
            (weights.at[:, pl.ds(cols - dense_v.shape[1], dense_v.shape[1])], dense_v),
        ]
        return [pltpu.make_async_copy(a, b, sems.at[n]) for n, (a, b) in enumerate(made)]

    def stores():
        made = [pltpu.make_async_copy(hold.at[n], out, out_sems.at[n]) for n, out in enumerate(outs)]
        return made + [pltpu.make_async_copy(eg_v, eg_out, out_sems.at[2 * RING])]

    @pl.when(step == 0)
    def _():
        copies = loads()
        for n in (0, 1, 5, 9, 2, 3, 4, 6, 7, 8):
            copies[n].start()
        copies[0].wait()
        copies[5].wait()
        copies[9].wait()
        bias_grad[...] = jnp.zeros_like(bias_grad)

    for n in range(RING):

        @pl.when(step == n)
        def _(n=n):
            loads()[1 + n].wait()

    @pl.when(step < RING)
    def _():
        at = pl.ds(pl.multiple_of(step * tile, tile), tile)
        low = dot_nn(grad_v[at, :], weight_v[...]) * slope_v[at, :].astype(F32)
        low = low.astype(BF)
        eg_v[at, :] = low
        attended_grad[at, :] = dot_nn(grad_v[at, :], dense_v[...]).astype(BF)
        bias_grad[...] += jnp.sum(low.astype(F32), 0, keepdims=True)

    @pl.when(step == RING)
    def _():
        stores()[2 * RING].start()
        loads()[6].wait()

    @pl.when(step == 2 * RING)
    def _():
        loads()[7].wait()
        loads()[8].wait()

    def columns(first):
        return pl.ds(pl.multiple_of((step - first) * quarter, quarter), quarter)

    @pl.when((step >= RING) & (step < 2 * RING))
    def _():
        hold[step - RING] = dot_tn(normed_v[:, columns(RING)], eg_v[...]).astype(BF)

    @pl.when(step >= 2 * RING)
    def _():
        hold[step - RING] = dot_tn(turned_v[:, columns(2 * RING)], activated_v[...]).astype(BF)

    for n in range(2 * RING):

        @pl.when(step == n + RING)
        def _(n=n):
            stores()[n].start()

    @pl.when(step == 3 * RING - 1)
    def _():
        for copy in stores():
            copy.wait()


def feed_back(weights, grad, slope, normed, activated, grad_turned, *waits):
    rows, width = grad.shape
    cols = weights.shape[1] // 3
    depth = width // RING
    outs = kernel_call(
        feed_back_kernel,
        (weights, grad, slope, normed, activated, grad_turned),
        waits,
        grid=(3 * RING,),
        in_specs=[ANY] * 6,
        out_specs=(ANY, whole((1, cols)), whole((rows, cols // 4))) + (ANY,) * (2 * RING),
        out_shape=(shaped((rows, cols), BF), shaped((1, cols), F32), shaped((rows, cols // 4), BF))
        + (shaped((depth, cols), BF),) * (2 * RING),
        scratch_shapes=[
            pltpu.VMEM((width, cols), BF),
            pltpu.VMEM((width, cols // 4), BF),
            pltpu.VMEM((rows, width), BF),
            pltpu.VMEM((rows, cols), BF),
            pltpu.VMEM((rows, width), BF),
            pltpu.VMEM((rows, cols), BF),
            pltpu.VMEM((rows, width), BF),
            pltpu.VMEM((rows, cols), BF),
            pltpu.VMEM((2 * RING, depth, cols), BF),
            pltpu.SemaphoreType.DMA((RING + 6,)),
            pltpu.SemaphoreType.DMA((2 * RING + 1,)),
        ],
        compiler_params=params(BIG),
        cost_estimate=cost(6 * rows * width * cols, 20 * rows * width),
        name="feed_back",
    )
    quarters = [quarter.reshape(RING, -1, cols) for quarter in outs[3:]]
    return *outs[:3], quarters[:RING], quarters[RING:]


def branch_kernel(rank, dense, reduce, activated, attended, small, branch, bias):
    heads = attended.shape[1]
    lanes = 2 * HEAD_DIM

    @pl.when(pl.program_id(0) == 0)
    def _():
        mine = small[12:13, 3 * heads :] + small[13:14, 3 * heads :]
        lane = lax.broadcasted_iota(jnp.int32, (1, lanes), 1)
        places = heads // HEAD_DIM
        side = (lane // HEAD_DIM) == rank[0] // (RING * RING // places)
        for n in range(RING * RING):
            part = mine[:, (n % places) * HEAD_DIM : (n % places + 1) * HEAD_DIM]
            part = jnp.concatenate([part, part], 1)
            here = rank[0] % (RING * RING // places) == n // places
            bias[:, n * lanes : (n + 1) * lanes] = jnp.where(side & here, part, 0.0)

    total = dot_nt(activated[...], reduce[...]) + dot_nt(attended[...], dense[...])
    branch[...] = (total + bias[...]).astype(BF)


def branch_layer(rank, activated, attended, weights, small, *waits):
    rows, cols = activated.shape
    heads = attended.shape[1]
    width = weights.shape[0]
    at_once = 256
    return kernel_call(
        branch_kernel,
        (rank, weights, weights, activated, attended, small),
        waits,
        grid=(rows // at_once,),
        in_specs=[SMEM]
        + [pl.BlockSpec((width, heads), lambda i: (0, 3))]
        + [pl.BlockSpec((width, cols), lambda i: (0, 2))]
        + [row_block(at_once, cols), row_block(at_once, heads), whole(small.shape)],
        out_specs=row_block(at_once, width),
        out_shape=shaped((rows, width), BF),
        scratch_shapes=[pltpu.VMEM((1, width), F32)],
        compiler_params=params(BIG),
        cost_estimate=cost(
            2 * rows * width * (cols + heads), 2 * (width + rows) * (cols + heads) + 2 * rows * width
        ),
        name="branch",
    )


def normed_grad_kernel(qkv_w, expand_w, proj_grad, expanded_grad, x_hat, part, sums):
    @pl.when(pl.program_id(0) == 0)
    def _():
        sums[...] = jnp.zeros_like(sums)

    total = dot_nt(proj_grad[...], qkv_w[...]) + dot_nt(expanded_grad[...], expand_w[...])
    part[...] = total.astype(BF)
    gain = jnp.sum(total * x_hat[...].astype(F32), 0, keepdims=True)
    offset = jnp.sum(total, 0, keepdims=True)
    sums[...] += jnp.concatenate([gain, offset], 0)


def normed_grad_layer(proj_grad, expanded_grad, weights, x_hat, *waits):
    rows, width = x_hat.shape
    cols, three = expanded_grad.shape[1], proj_grad.shape[1]
    depth = width // RING
    at_once = 256
    return kernel_call(
        normed_grad_kernel,
        (weights, weights, proj_grad, expanded_grad, x_hat),
        waits,
        grid=(rows // at_once,),
        in_specs=[pl.BlockSpec((width, three), lambda i: (0, 0))]
        + [pl.BlockSpec((width, cols), lambda i: (0, 1))]
        + [row_block(at_once, three), row_block(at_once, cols), row_block(at_once, width)],
        out_specs=(row_block(at_once, width), whole((2, width))),
        out_shape=(shaped((rows, width), BF), shaped((2, width), F32)),
        compiler_params=params(BIG),
        cost_estimate=cost(
            2 * rows * width * (cols + three), 2 * (width + rows) * (cols + three) + 4 * rows * width
        ),
        name="normed_grad",
    )


def weight_grad_kernel(count, *refs):
    lefts, rights = refs[:count], refs[count : 2 * count]
    *small, out0, out1, out2, out3, hold, sems = refs[2 * count :]
    outs = (out0, out1, out2, out3)
    step, last = pl.program_id(0), pl.num_programs(0) - 1
    cols = 0
    for a, b in zip(lefts, rights):
        hold[step, :, cols : cols + b.shape[1]] = dot_tn(a[...], b[...]).astype(BF)
        cols += b.shape[1]
    for ref in small:
        for n in range(RING):
            lanes = ref.shape[1]
            hold[step, n * lanes : (n + 1) * lanes, cols:] = ref[...]
    for n, out in enumerate(outs):

        @pl.when(step == n)
        def _(n=n, out=out):
            pltpu.make_async_copy(hold.at[n], out, sems.at[n]).start()

    @pl.when(step == last)
    def _():
        for n, out in enumerate(outs):
            pltpu.make_async_copy(hold.at[n], out, sems.at[n]).wait()


def weight_grad(pairs, small=None, waits=()):
    rows, width = pairs[0][0].shape
    more = [] if small is None else [small]
    cols = sum(right.shape[1] for _, right in pairs) + sum(extra.shape[1] for extra in more)
    at_once = width // RING

    def kernel(*refs):
        weight_grad_kernel(len(pairs), *refs)

    left = pl.BlockSpec((rows, at_once), lambda i: (0, i))
    quarters = kernel_call(
        kernel,
        (*[a for a, _ in pairs], *[b for _, b in pairs], *more),
        waits,
        grid=(RING,),
        in_specs=[left] * len(pairs)
        + [whole(right.shape) for _, right in pairs]
        + [whole(extra.shape) for extra in more],
        out_specs=(ANY,) * RING,
        out_shape=(shaped((at_once, cols), BF),) * RING,
        scratch_shapes=[
            pltpu.VMEM((RING, at_once, cols), BF),
            pltpu.SemaphoreType.DMA((RING,)),
        ],
        compiler_params=params(BIG),
        cost_estimate=cost(
            2 * rows * width * cols, 2 * (len(pairs) * rows * width + rows * cols + width * cols)
        ),
        name="weight_grad",
    )
    return [quarter.reshape(RING, -1, cols) for quarter in quarters]


def rolled(value, shift):
    return pltpu.roll(value, shift % value.shape[-1], value.ndim - 1)


def rotate(value, cos, sin_low, sin_high, sign):
    half = ROT // 2
    turned = rolled(value, -half) * sin_low + rolled(value, half) * sin_high
    return value * cos + sign * turned


def attention_kernel(
    projected, out_grad, cos, sin_low, sin_high, start, mixed, proj_grad, bias_grad
):
    rows, width = out_grad.shape
    heads = width // HEAD_DIM
    scale = HEAD_DIM**-0.5
    tables = [
        jnp.concatenate([ref[...]] * (width // ref.shape[1]), 1) for ref in (cos, sin_low, sin_high)
    ]
    query_rot = (rotate(projected[:, :width], *tables, 1.0).astype(BF) * scale).astype(BF)
    key_rot = rotate(projected[:, width : 2 * width], *tables, 1.0).astype(BF)
    value_rows = projected[:, 2 * width :].astype(BF)
    grad_rows = out_grad[...]
    half = rows // 4
    lane = lax.broadcasted_iota(jnp.int32, (half, width), 1)
    mine = [(lane >= h * HEAD_DIM) & (lane < (h + 1) * HEAD_DIM) for h in range(heads)]

    def stacked(block):
        return jnp.concatenate([jnp.where(m, block, jnp.zeros_like(block)) for m in mine], 0)

    def gathered(stack):
        total = None
        for h in range(heads):
            part = stack[h * half : (h + 1) * half]
            total = part if total is None else jnp.where(mine[h], part, total)
        return total

    key_sum, value_sum = {}, {}
    for first in range(0, rows, half):
        last = first + half
        here = slice(first, last)
        row_id = lax.broadcasted_iota(jnp.int32, (half, last), 0) + first
        col_id = lax.broadcasted_iota(jnp.int32, (half, last), 1)
        allowed = ((col_id <= row_id) & (col_id >= start[here, 0:1]))[None]
        queries, grads = stacked(query_rot[here]), stacked(grad_rows[here])
        scores = dot_nt(queries, key_rot[:last]).reshape(heads, half, last)
        scores = jnp.where(allowed, scores, -1000000000.0)
        top = jnp.max(scores, -1, keepdims=True)
        expd = jnp.exp(scores - top)
        probs = expd * (1.0 / jnp.sum(expd, -1, keepdims=True))
        prob_low = probs.astype(BF).reshape(heads * half, last)
        prob_grad = dot_nt(grads, value_rows[:last]).reshape(heads, half, last)
        row_dot = jnp.sum(probs * prob_grad, -1, keepdims=True)
        score_grad = (probs * (prob_grad - row_dot)).astype(BF).reshape(heads * half, last)
        mixed[here, :] = gathered(dot_nn(prob_low, value_rows[:last])).astype(BF)
        query_part = gathered(dot_nn(score_grad, key_rot[:last])) * scale
        query_part = rotate(query_part, *[table[here] for table in tables], -1.0).astype(BF)
        proj_grad[here, :width] = query_part
        query_bias = jnp.sum(query_part.astype(F32), 0, keepdims=True)
        bias_grad[0, :, :width] = query_bias if first == 0 else bias_grad[0, :, :width] + query_bias
        key_part, value_part = dot_tn(score_grad, queries), dot_tn(prob_low, grads)
        for n in range(0, last, half):
            for sums, part in ((key_sum, key_part), (value_sum, value_part)):
                block = part[n : n + half]
                sums[n] = sums[n] + block if n in sums else block
    for j, sums in ((1, key_sum), (2, value_sum)):
        total = jnp.concatenate([sums[n] for n in range(0, rows, half)], 0)
        if j == 1:
            total = rotate(total, *tables, -1.0)
        low = total.astype(BF)
        proj_grad[:, j * width : (j + 1) * width] = low
        bias_grad[0, :, j * width : (j + 1) * width] = jnp.sum(low.astype(F32), 0, keepdims=True)


def attention(projected, out_grad, cos, sin_low, sin_high, start, pack_rows, *waits):
    rows, width = out_grad.shape
    lanes = cos.shape[1]
    packs = rows // pack_rows
    return kernel_call(
        attention_kernel,
        (projected, out_grad, cos, sin_low, sin_high, start),
        waits,
        grid=(packs,),
        in_specs=[row_block(pack_rows, 3 * width), row_block(pack_rows, width)]
        + [row_block(pack_rows, lanes)] * 4,
        out_specs=(
            row_block(pack_rows, width),
            row_block(pack_rows, 3 * width),
            pl.BlockSpec((1, 1, 3 * width), lambda p: (p, 0, 0)),
        ),
        out_shape=(
            shaped((rows, width), BF),
            shaped((rows, 3 * width), BF),
            shaped((packs, 1, 3 * width), F32),
        ),
        compiler_params=params(BIG),
        cost_estimate=cost(
            14 * rows * pack_rows * width, rows * width * 32, rows * pack_rows * width // HEAD_DIM
        ),
        name="attention",
    )


def pick(first, a, b):
    return jnp.where(first, a, b), jnp.where(first, b, a)


def three_parts(value):
    high = lax.reduce_precision(value, 8, 7)
    rest = value - high
    mid = lax.reduce_precision(rest, 8, 7)
    return [high, mid, rest - mid]


def body(
    hidden_in,
    seq_lengths,
    norm_gain,
    norm_offset,
    attn_weight,
    attn_bias,
    dense_weight,
    dense_bias,
    expand_weight,
    expand_bias,
    reduce_weight,
    reduce_bias,
    out_grad,
):
    at_yhi, at_x, at_z, at_ylo, at_core = (lax.axis_index(a) for a in AXES)
    first_yhi, first_ylo, first_core = at_yhi == 0, at_ylo == 0, at_core == 0
    local_rows, width = hidden_in.shape
    pack_rows = local_rows * RING
    at_tensor = at_ylo * 2 + at_core
    column_rank = at_tensor * 2 + at_yhi
    plane = RING * RING
    at_plane = at_x * RING + at_z

    place = np.arange(plane, dtype=np.int32)
    x, z = (place // RING - at_x) % RING, (place % RING - at_z) % RING
    inner, outer = jnp.where(first_core, x, z), jnp.where(first_core, z, x)
    order = np.array([0, 2, 3, 1], np.int32)

    def position(step):
        return sum(jnp.where(step == n, order[n], 0) for n in range(1, RING))

    turned = (position(outer) * RING + position(inner)).astype(jnp.int32)

    lanes = 2 * HEAD_DIM
    block_rows, cols = expand_weight.shape[0], expand_weight.shape[1] // 2
    heads = cols // 4

    unit = norm_gain.shape[0]
    norms = jnp.stack(three_parts(norm_gain) + three_parts(norm_offset))
    lengths = seq_lengths[0]
    count = lengths.shape[0]
    small = lax.dynamic_update_slice(
        jnp.zeros((16, cols), F32),
        norms,
        (at_plane // 8 * 6, at_plane % 8 * 8 * unit + at_yhi * 4 * unit + at_tensor * unit),
    )
    two = jnp.concatenate([lengths // 16, lengths % 16]).astype(F32)
    small = lax.dynamic_update_slice(small, two[None], (15, at_yhi * 2 * count)).astype(BF)

    own, other = split_columns(
        at_yhi.reshape(1).astype(jnp.int32),
        attn_weight, dense_weight.T, expand_weight, reduce_weight.T,
    )
    got = swap(other, "yhi")
    block = jnp.concatenate(pick(first_yhi, own, got), 0)
    weights = lax.all_gather(block, ("x", "z"), axis=0, tiled=True)

    small = small + swap(small, "yhi")
    two = small[15, : 4 * count].astype(F32).reshape(2, 2, count)
    length_rows = (two[:, 0] * 16.0 + two[:, 1]).astype(jnp.int32)
    biases = jnp.stack([dense_bias, reduce_bias])
    biases = jnp.concatenate([jnp.stack([attn_bias, 0 * attn_bias]), biases[:, None]], 1)
    bias_rows = lax.dynamic_update_slice(
        jnp.zeros((2, 4, heads), BF), biases, (0, 0, at_plane * unit)
    ).reshape(2, cols)
    expand_row = lax.dynamic_update_slice(
        jnp.zeros((2, cols), BF), expand_bias[None], (0, at_plane * expand_bias.shape[0])
    )
    small = jnp.concatenate([small[:12], bias_rows, expand_row], 0)

    for axis in ("x", "z"):
        for odd in range(2):
            small = small + lax.ppermute(small, axis, axis_swaps(odd))
    parts = jnp.where((np.arange(16) < 12)[:, None], small, jnp.zeros_like(small))
    others = swap(parts, "ylo")
    small = (small + others + swap(parts + others, "core")).astype(F32)

    own_rows = pair_columns(hidden_in, out_grad, got)
    below, above = move_y(own_rows, 1), move_y(own_rows, -1)
    one = (1,) + own_rows.shape[1:]
    far_hidden, far_grad = take_parts((below, one, (0, 0, 0)), (above, one, (1, 0, 0)))
    far_hidden, far_grad = move_y(far_hidden, 1), move_y(far_grad, -1)
    far_rows = jnp.concatenate([far_hidden, far_grad], 0)
    sources = [
        ref for rows in (own_rows, below, above, far_rows) for ref in (rows, swap(rows, "core"))
    ]
    at_y = at_yhi * 2 + at_ylo
    chips = jnp.stack([at_y, (at_y + 3) % RING, (at_y + 1) % RING, (at_y + 2) % RING, at_core])
    chips = chips.astype(jnp.int32)

    ends = jnp.cumsum(length_rows, 1)
    row_ids = jnp.arange(pack_rows, dtype=jnp.int32)
    begun = row_ids[None, :, None] >= ends[:, None, :]
    start = jnp.max(jnp.where(begun, ends[:, None, :], 0), 2).reshape(-1, 1)
    position = (jnp.tile(row_ids, 2)[:, None] - start).astype(F32)
    lane = np.arange(lanes) % HEAD_DIM
    half = ROT // 2
    inverse = np.float32(10000.0) ** (np.float32(-2.0) * (lane % half).astype(np.float32) / ROT)
    angles = position * inverse.astype(np.float32)[None, :]
    cos = jnp.where((lane < ROT)[None, :], jnp.cos(angles), 1.0)
    sine = jnp.sin(angles)
    sin_low = jnp.where((lane < half)[None, :], -sine, 0.0)
    sin_high = jnp.where(((lane >= half) & (lane < ROT))[None, :], sine, 0.0)
    start = jnp.broadcast_to(start, (start.shape[0], lanes))

    normed, normed_turned, x_hat, grad_all, grad_turned, grad_sum = rows_layer(
        chips, turned, small, sources, cos, sin_low, sin_high, start
    )
    activated, slope, projected = expand_layer(weights, normed, small)
    expanded_grad, expand_bias_grad, attended_grad, expand_1, reduce_1 = feed_back(
        weights, grad_all, slope, normed_turned, activated, grad_turned
    )
    expand_sent = ring_send(expand_1, False, 1)
    reduce_sent = ring_send(reduce_1, False, -1)
    attended, proj_grad, attn_bias_grad = attention(
        projected, attended_grad, cos, sin_low, sin_high, start, pack_rows
    )
    normed_part, norm_sums = normed_grad_layer(proj_grad, expanded_grad, weights, x_hat)
    expand_up, reduce_up, normed_part = add_pairs(
        [(expand_1[2], expand_sent[0]), (reduce_1[1], reduce_sent[0])],
        normed_part,
        (expand_sent[1], reduce_sent[1]),
    )
    expand_last, reduce_last = move(expand_up, False, 1), move(reduce_up, False, -1)

    places = heads // block_rows
    out_bias_grad = lax.dynamic_slice(
        grad_sum.reshape(plane, 2, block_rows),
        (column_rank % (plane // places) * places, column_rank // (plane // places), 0),
        (places, 1, block_rows),
    ).reshape(1, heads)
    attn_row = jnp.concatenate([jnp.sum(attn_bias_grad, 0), out_bias_grad], 1)
    small_grad = jnp.concatenate(
        [norm_sums.reshape(4, cols), attn_row, expand_bias_grad, jnp.zeros((10, cols), F32)], 0
    ).astype(BF)
    attn_1 = weight_grad(
        [(normed_turned, proj_grad), (grad_turned, attended)], fold(small_grad), (expand_up,)
    )
    attn_sent = ring_send(attn_1, False, -1)
    feed_2 = add_lines(
        [
            (expand_1[0], expand_sent[1], expand_last),
            (reduce_1[0], reduce_sent[1], reduce_last),
        ],
        (attn_1[0],),
    )
    feed_terms = ring_terms(feed_2)
    branch = branch_layer(
        column_rank.reshape(1).astype(jnp.int32),
        activated, attended, weights, small, attn_1[0], feed_2[0],
    )
    attn_up, branch = add_pairs(
        [(attn_1[1], attn_sent[0])], branch, (attn_sent[1], *feed_terms[1:])
    )
    attn_last = move(attn_up, False, -1)

    normed_grad = lax.psum_scatter(normed_part, COLUMN, scatter_dimension=0, tiled=True)
    branch = lax.psum_scatter(branch, COLUMN, scatter_dimension=0, tiled=True)
    input_grad = input_grad_layer(own_rows, normed_grad, small)

    yhi_index = at_yhi.reshape(1).astype(jnp.int32)
    feed_keep, send = finish_sums(yhi_index, feed_terms, 2 * cols, (attn_up,))
    feed_got = swap(send, "yhi")
    attn_2 = add_lines([(attn_1[0], attn_sent[1], attn_last)], (input_grad, feed_got))
    attn_terms = ring_terms(attn_2)
    expand_w_grad, reduce_w_grad = join_halves(
        yhi_index, feed_keep, feed_got, ((1, 0, cols), (1, cols, cols)), (attn_2[0],)
    )
    attn_keep, attn_send, small_total = finish_sums(
        yhi_index, attn_terms, cols, (expand_w_grad,)
    )
    block_out = output_layer(own_rows, branch, attn_send)
    small_total = unfold(small_total)
    norm_total = lax.dynamic_slice_in_dim(
        small_total[:4].reshape(2, width), at_plane * 8 * unit, 8 * unit, 1
    ).reshape(2, 2, 4 * unit)
    norm_keep, norm_send = pick(first_yhi, norm_total[:, 0], norm_total[:, 1])
    rider = jnp.pad(norm_send.astype(BF), ((0, 14), (0, cols - 4 * unit)))
    got = swap(jnp.concatenate([attn_send, rider], 0), "yhi")
    attn_w_grad, dense_w_grad = join_halves(
        yhi_index,
        attn_keep,
        got[:block_rows],
        ((3, 0, heads), (1, 3 * heads, heads)),
        (block_out,),
    )
    keep = norm_keep + got[block_rows : block_rows + 2, : 4 * unit].astype(F32)
    keep = keep.reshape(2, 2, 2, unit)
    keep, send = pick(first_ylo, keep[:, 0], keep[:, 1])
    keep = keep + swap(send, "ylo")
    keep, send = pick(first_core, keep[:, 0], keep[:, 1])
    norm_grads = keep + swap(send, "core")

    bias_total = lax.dynamic_slice_in_dim(
        small_total[4].reshape(4, heads), at_plane * unit, unit, 1
    )
    expand_b_grad = lax.dynamic_slice_in_dim(
        small_total[5], at_plane * expand_bias.shape[0], expand_bias.shape[0]
    )
    return (
        block_out,
        input_grad,
        norm_grads[0],
        norm_grads[1],
        attn_w_grad,
        bias_total[:3],
        dense_w_grad.T,
        bias_total[3],
        expand_w_grad,
        expand_b_grad,
        reduce_w_grad.T,
        bias_total[3],
    )


def solution(mesh):
    split = Mesh(mesh.devices.reshape(2, RING, RING, 2, 2), AXES)
    dp, tensor = ("yhi", "x", "z"), ("ylo", "core")
    rows = P(dp + tensor, None)
    vector = P(dp + tensor)
    bias = P(tensor + dp)
    parameters = (
        vector,
        vector,
        P(None, dp, tensor),
        P(None, tensor + dp),
        P(tensor, dp),
        bias,
        P(dp, tensor),
        bias,
        P(tensor, dp),
        bias,
    )
    return jax.shard_map(
        body,
        mesh=split,
        in_specs=(rows, P(dp, None)) + parameters + (rows,),
        out_specs=(rows, rows) + parameters,
        check_vma=False,
    )
```

```python
import numpy as np
import jax
import jax.numpy as jnp
from jax import lax
from jax.experimental import pallas as pl
from jax.experimental.pallas import tpu as pltpu
from jax.sharding import Mesh, PartitionSpec as P

HEAD_DIM = 64
ROT = 32
RING = 4
AXES = ("yhi", "x", "z", "ylo", "core")
COLUMN = ("yhi", "ylo", "core")
BF = jnp.bfloat16
F32 = jnp.float32
MIB = 1 << 20
BIG = 58
SMALL = 16


def ring_pairs(first_ring, step):
    pairs = []
    for x in range(RING):
        for z in range(RING):
            for core in range(2):
                along_x = (core == 0) == first_ring
                to_x = (x + step) % RING if along_x else x
                to_z = z if along_x else (z + step) % RING
                pairs.append(((x * RING + z) * 2 + core, (to_x * RING + to_z) * 2 + core))
    return pairs


def move(value, first_ring, step):
    return lax.ppermute(value, ("x", "z", "core"), ring_pairs(first_ring, step))


def axis_swaps(odd):
    return [(n, (n + (1 if n % 2 == odd else -1)) % RING) for n in range(RING)]


def move_y(value, step):
    pairs = [(y, (y + step) % RING) for y in range(RING)]
    return lax.ppermute(value, ("yhi", "ylo"), pairs)


def swap(value, axis):
    return lax.ppermute(value, axis, [(0, 1), (1, 0)])


def ring_send(blocks, first_ring, way):
    _, minus, plus, far = blocks
    direct = move(minus, first_ring, -1) if way > 0 else move(plus, first_ring, 1)
    return move(far, first_ring, way), direct


def ring_terms(blocks):
    here, minus, plus, far = blocks
    return here, move(minus, True, -1), move(plus, True, 1), move(far, True, 2)


ANY = pl.BlockSpec(memory_space=pl.ANY)
SMEM = pl.BlockSpec(memory_space=pltpu.SMEM)


def whole(shape):
    return pl.BlockSpec(shape, lambda *at: (0,) * len(shape))


def row_block(rows, cols):
    return pl.BlockSpec((rows, cols), lambda i: (i, 0))


def shaped(shape, dtype):
    return jax.ShapeDtypeStruct(shape, dtype)


def kernel_call(kernel, operands, waits, *, in_specs, **options):
    count, more = len(operands), len(waits)

    def run(*refs):
        kernel(*refs[:count], *refs[count + more :])

    in_specs = list(in_specs) + [ANY] * more
    scalars = count - len(in_specs) + more
    if scalars:
        parts = {key: options.pop(key) for key in ("grid", "out_specs", "scratch_shapes")}
        options["grid_spec"] = pltpu.PrefetchScalarGridSpec(
            num_scalar_prefetch=scalars, in_specs=in_specs, **parts
        )
    else:
        options["in_specs"] = in_specs
    return pl.pallas_call(run, **options)(*operands, *waits)


def parts_kernel(*refs):
    count = len(refs) // 2
    for ref, out in zip(refs[:count], refs[count:]):
        out[...] = ref[...]


def take_parts(*chosen):
    specs = [pl.BlockSpec(shape, lambda i, at=at: at) for _, shape, at in chosen]
    return kernel_call(
        parts_kernel,
        tuple(array for array, _, _ in chosen),
        (),
        grid=(1,),
        in_specs=specs,
        out_specs=tuple(whole(shape) for _, shape, _ in chosen),
        out_shape=tuple(shaped(shape, array.dtype) for array, shape, _ in chosen),
        compiler_params=params(SMALL),
        cost_estimate=cost(0, 4 * sum(int(np.prod(shape)) for _, shape, _ in chosen)),
        name="take_parts",
    )


def add_pairs_kernel(*refs):
    count = (len(refs) - 2) // 3
    for n in range(count):
        a, b, out = refs[2 * n], refs[2 * n + 1], refs[2 * count + 1 + n]
        out[...] = (a[...].astype(F32) + b[...].astype(F32)).astype(BF)


def add_pairs(pairs, carried, waits=()):
    shapes = [a.shape for a, _ in pairs]
    flat = [term.reshape(-1, term.shape[-1]) for pair in pairs for term in pair]
    halves = [row_block(term.shape[0] // 2, term.shape[1]) for term in flat]
    *sums, carried = kernel_call(
        add_pairs_kernel,
        (*flat, carried),
        waits,
        grid=(2,),
        in_specs=halves + [ANY],
        out_specs=tuple(halves[::2]) + (ANY,),
        out_shape=tuple(shaped(term.shape, BF) for term in flat[::2])
        + (shaped(carried.shape, carried.dtype),),
        input_output_aliases={len(flat): len(pairs)},
        compiler_params=params(BIG),
        cost_estimate=cost(0, 3 * sum(term.size for term in flat)),
        name="add_pairs",
    )
    return [total.reshape(shape) for total, shape in zip(sums, shapes)] + [carried]


def add_lines_kernel(riders, *refs):
    outs = refs[-RING:]
    sources, at = refs[: -RING - riders], 0
    for n in range(0, len(sources), 3):
        total = sum(ref[...].astype(F32) for ref in sources[n : n + 3])
        for i, out in enumerate(outs):
            out[:, at : at + total.shape[-1]] = total[i].astype(BF)
        at += total.shape[-1]
    for ref in refs[len(sources) : -RING]:
        for out in outs:
            out[:, at:] = ref[...]


def add_lines(lines, riders=(), waits=()):
    operands = [term for terms in lines for term in terms]
    rows = operands[0].shape[1]
    cols = sum(terms[0].shape[2] for terms in lines) + sum(rider.shape[1] for rider in riders)
    at_once = rows // 2

    def kernel(*refs):
        add_lines_kernel(len(riders), *refs)

    specs = [
        pl.BlockSpec((RING, at_once, term.shape[2]), lambda i: (0, i, 0)) for term in operands
    ]
    return kernel_call(
        kernel,
        (*operands, *riders),
        waits,
        grid=(2,),
        in_specs=specs + [row_block(at_once, rider.shape[1]) for rider in riders],
        out_specs=(row_block(at_once, cols),) * RING,
        out_shape=(shaped((rows, cols), BF),) * RING,
        compiler_params=params(BIG),
        cost_estimate=cost(0, 8 * RING * rows * cols),
        name="add_lines",
    )


def finish_kernel(count, at_yhi, *refs):
    outs = refs[count * (len(refs) // (count + 1)) :]
    for n, out in enumerate(outs):
        total = sum(ref[...].astype(F32) for ref in refs[n * count : (n + 1) * count])
        out[...] = total.astype(out.dtype)


def finish_sums(at_yhi, terms, cols, waits=()):
    rows, more = terms[0].shape[0], terms[0].shape[1] - cols
    half = rows // 2
    keep = pl.BlockSpec((half, cols), lambda i, at: (at[0], 0))
    send = pl.BlockSpec((half, cols), lambda i, at: (1 - at[0], 0))
    out = pl.BlockSpec((half, cols), lambda i, at: (0, 0))
    count = len(terms)
    specs, outs = [keep] * count + [send] * count, [out] * 2
    shapes = [shaped((half, cols), F32), shaped((half, cols), BF)]
    if more:
        specs += [pl.BlockSpec((rows, more), lambda i, at: (0, cols // more))] * count
        outs.append(pl.BlockSpec((rows, more), lambda i, at: (0, 0)))
        shapes.append(shaped((rows, more), F32))

    def kernel(*refs):
        finish_kernel(count, *refs)

    return kernel_call(
        kernel,
        (at_yhi, *(tuple(terms) * (len(specs) // count))),
        waits,
        grid=(1,),
        in_specs=specs,
        out_specs=tuple(outs),
        out_shape=tuple(shapes),
        scratch_shapes=(),
        compiler_params=params(SMALL),
        cost_estimate=cost(0, 8 * rows * cols),
        name="finish_sums",
    )


def join_kernel(layout, at_yhi, keep, got, *outs):
    part = jnp.where(pl.program_id(0) == 0, keep[...], got[...].astype(F32))
    for (count, first, width), out in zip(layout, outs):
        for n in range(count):
            block = part[:, first + n * width : first + (n + 1) * width]
            if len(out.shape) == 3:
                out[n] = block
            else:
                out[...] = block


def join_halves(at_yhi, keep, got, layout, waits=()):
    rows, cols = keep.shape

    def kernel(*refs):
        join_kernel(layout, *refs)

    def side(i, at):
        return at[0] + i * (1 - 2 * at[0])

    specs, shapes = [], []
    for count, _, width in layout:
        lead = (count,) if count > 1 else ()
        zeros = (0,) * (len(lead) + 1)
        specs.append(
            pl.BlockSpec(lead + (rows, width), lambda i, at, zeros=zeros: (*zeros, side(i, at)))
        )
        shapes.append(shaped(lead + (rows, 2 * width), F32))
    here = pl.BlockSpec((rows, cols), lambda i, at: (0, 0))
    return kernel_call(
        kernel,
        (at_yhi, keep, got),
        waits,
        grid=(2,),
        in_specs=[here, here],
        out_specs=tuple(specs),
        out_shape=tuple(shapes),
        scratch_shapes=(),
        compiler_params=params(BIG),
        cost_estimate=cost(0, 12 * rows * cols),
        name="join_halves",
    )


def params(megabytes):
    return pltpu.CompilerParams(vmem_limit_bytes=megabytes * MIB)


def cost(flops, moved, special=0):
    return pl.CostEstimate(flops=flops, bytes_accessed=moved, transcendentals=special)


def dot_nn(a, b):
    return jnp.dot(a, b, preferred_element_type=F32)


def dot_nt(a, b):
    return lax.dot_general(a, b, (((1,), (1,)), ((), ())), preferred_element_type=F32)


def dot_tn(a, b):
    return lax.dot_general(a, b, (((0,), (0,)), ((), ())), preferred_element_type=F32)


def split_kernel(at_yhi, *refs):
    ins, outs = refs[:8], refs[8:]
    for n, out in enumerate(outs):
        attn, *others = ins[4 * n : 4 * n + 4]
        at = 0
        for part in [attn[j] for j in range(3)] + [ref[...] for ref in others]:
            out[:, at : at + part.shape[1]] = part
            at += part.shape[1]


def split_columns(at_yhi, attn, dense, expand, reduce):
    rows, cols = expand.shape[0], expand.shape[1] // 2
    ins = []
    for n in range(2):

        def side(at, n=n):
            return at[0] if n == 0 else 1 - at[0]

        ins.append(pl.BlockSpec((3, rows, cols // 4), lambda i, at, side=side: (0, 0, side(at))))
        for width in (cols // 4, cols, cols):
            ins.append(pl.BlockSpec((rows, width), lambda i, at, side=side: (0, side(at))))
    return pl.pallas_call(
        split_kernel,
        grid_spec=pltpu.PrefetchScalarGridSpec(
            num_scalar_prefetch=1,
            grid=(1,),
            in_specs=ins,
            out_specs=(whole((rows, 3 * cols)),) * 2,
        ),
        out_shape=(shaped((rows, 3 * cols), BF),) * 2,
        compiler_params=params(BIG),
        cost_estimate=cost(0, 6 * rows * cols * 4),
        name="split_columns",
    )(at_yhi, *[attn, dense, expand, reduce] * 2)


def paired(rows):
    lanes = 2 * HEAD_DIM
    low = lax.broadcasted_iota(jnp.int32, (rows.shape[0], lanes), 1) < HEAD_DIM
    half = rows.shape[1] // 2
    for k in range(half // lanes):
        a = rows[:, k * lanes : (k + 1) * lanes]
        b = rows[:, half + k * lanes : half + (k + 1) * lanes]
        yield 2 * k * lanes, jnp.where(low, a, pltpu.roll(b, HEAD_DIM, 1))
        yield (2 * k + 1) * lanes, jnp.where(low, pltpu.roll(a, HEAD_DIM, 1), b)


def unpaired(rows):
    lanes = 2 * HEAD_DIM
    low = lax.broadcasted_iota(jnp.int32, (rows.shape[0], lanes), 1) < HEAD_DIM
    half = rows.shape[1] // 2
    for k in range(half // lanes):
        a = rows[:, 2 * k * lanes : (2 * k + 1) * lanes]
        b = rows[:, (2 * k + 1) * lanes : (2 * k + 2) * lanes]
        yield k * lanes, jnp.where(low, a, pltpu.roll(b, HEAD_DIM, 1))
        yield half + k * lanes, jnp.where(low, pltpu.roll(a, HEAD_DIM, 1), b)


def pair_kernel(hidden, grad, out):
    for n, ref in enumerate((hidden, grad)):
        for at, block in paired(ref[...].astype(F32)):
            out[n, :, at : at + block.shape[1]] = block.astype(BF)


def pair_columns(hidden, grad, *waits):
    rows, width = hidden.shape
    at_once = rows // 2
    return kernel_call(
        pair_kernel,
        (hidden, grad),
        waits,
        grid=(2,),
        in_specs=[row_block(at_once, width)] * 2,
        out_specs=pl.BlockSpec((2, at_once, width), lambda i: (0, i, 0)),
        out_shape=shaped((2, rows, width), BF),
        compiler_params=params(SMALL),
        cost_estimate=cost(0, 8 * rows * width),
        name="pair_columns",
    )


def output_kernel(hidden, branch, out):
    total = hidden[0].astype(F32) + branch[...].astype(F32)
    for at, block in unpaired(total):
        out[:, at : at + block.shape[1]] = block.astype(BF)


def own_block(which, rows, width):
    return pl.BlockSpec((1, rows, width), lambda i: (which, i, 0))


def output_layer(own, branch, *waits):
    _, rows, width = own.shape
    at_once = rows // 2
    return kernel_call(
        output_kernel,
        (own, branch),
        waits,
        grid=(2,),
        in_specs=[own_block(0, at_once, width), row_block(at_once, width)],
        out_specs=row_block(at_once, width),
        out_shape=shaped((rows, width), BF),
        compiler_params=params(SMALL),
        cost_estimate=cost(0, 6 * rows * width),
        name="output",
    )


def input_grad_kernel(hidden, grad, normed_grad, small, out):
    rows = hidden[0].astype(F32)
    center = rows - jnp.mean(rows, -1, keepdims=True)
    spread = lax.rsqrt(jnp.mean(center * center, -1, keepdims=True) + 1e-05)
    x_hat = center * spread
    gain, _ = norm_rows(small)
    scaled = normed_grad[...].astype(F32) * gain
    total = grad[0].astype(F32) + spread * (
        scaled
        - jnp.mean(scaled, -1, keepdims=True)
        - x_hat * jnp.mean(scaled * x_hat, -1, keepdims=True)
    )
    for at, block in unpaired(total):
        out[:, at : at + block.shape[1]] = block.astype(BF)


def input_grad_layer(own, normed_grad, small, *waits):
    _, rows, width = own.shape
    at_once = rows // 2
    return kernel_call(
        input_grad_kernel,
        (own, own, normed_grad, small),
        waits,
        grid=(2,),
        in_specs=[own_block(n, at_once, width) for n in range(2)]
        + [row_block(at_once, width), whole(small.shape)],
        out_specs=row_block(at_once, width),
        out_shape=shaped((rows, width), BF),
        compiler_params=params(SMALL),
        cost_estimate=cost(0, 8 * rows * width),
        name="input_grad",
    )


def put_in_turn(rows, turned, out):
    lanes = 2 * HEAD_DIM
    for n in range(rows.shape[1] // lanes):
        at = pl.multiple_of(turned[n] * lanes, lanes)
        out[:, pl.ds(at, lanes)] = rows[:, n * lanes : (n + 1) * lanes].astype(out.dtype)


def fold(small):
    return small.reshape(16, -1, 128).transpose(1, 0, 2).reshape(-1, 128)


def unfold(small):
    return small.reshape(-1, 16, 128).transpose(1, 0, 2).reshape(16, -1)


def norm_rows(small):
    def row(at):
        return small[at : at + 1] + small[at + 1 : at + 2] + small[at + 2 : at + 3]

    gain = jnp.concatenate([row(0), row(6)], 1)
    offset = jnp.concatenate([row(3), row(9)], 1)
    return gain, offset


def load_rows(chips, sources, held, sems, step):
    copies = []
    for n, ref in enumerate(sources):
        core = chips[RING] if n % 2 == 0 else 1 - chips[RING]
        copies.append(pltpu.make_async_copy(ref, held.at[n // 2, core], sems.at[n]))

    @pl.when(step == 0)
    def _():
        for copy in copies:
            copy.start()

    for n in range(RING):

        @pl.when(step == n)
        def _(n=n):
            copies[2 * n].wait()
            copies[2 * n + 1].wait()

    rows = held[step]
    return rows.reshape(-1, rows.shape[-1])


def chip_block(rows, cols):
    return pl.BlockSpec((rows, cols), lambda i, chips: (chips[i], 0))


def prefetched(specs):
    return [
        spec
        if spec.index_map is None
        else pl.BlockSpec(spec.block_shape, lambda i, chips, at=spec.index_map: at(i))
        for spec in specs
    ]


def rows_kernel(chips, turned, small, *refs):
    sources, rest = refs[: 2 * RING], refs[2 * RING :]
    normed, normed_turned, x_hat, grad, grad_turned, grad_sum, held, grad_held, sems, grad_sems = rest
    step = pl.program_id(0)

    @pl.when(step == 0)
    def _():
        grad_sum[...] = jnp.zeros_like(grad_sum)

    rows = load_rows(chips, [hidden_of(ref) for ref in sources], held, sems, step).astype(F32)
    gain, offset = norm_rows(small)
    center = rows - jnp.mean(rows, -1, keepdims=True)
    scaled = center * lax.rsqrt(jnp.mean(center * center, -1, keepdims=True) + 1e-05)
    x_hat[...] = scaled.astype(BF)
    normed[...] = (scaled * gain + offset).astype(BF)
    put_in_turn(normed, turned, normed_turned)
    rows = load_rows(chips, [grad_of(ref) for ref in sources], grad_held, grad_sems, step)
    grad[...] = rows
    put_in_turn(grad, turned, grad_turned)
    grad_sum[...] += jnp.sum(rows.astype(F32), 0, keepdims=True)


def hidden_of(ref):
    return ref.at[0] if len(ref.shape) == 3 else ref


def grad_of(ref):
    return ref.at[1] if len(ref.shape) == 3 else ref


def rows_layer(chips, turned, small, sources, *waits):
    local_rows, width = sources[0].shape[-2:]
    rows = 2 * RING * local_rows
    at_once = 2 * local_rows
    return kernel_call(
        rows_kernel,
        (chips, turned, small, *sources),
        waits,
        grid=(RING,),
        in_specs=[SMEM] + prefetched([whole(small.shape)]) + [ANY] * len(sources),
        out_specs=(chip_block(at_once, width),) * 5 + tuple(prefetched([whole((1, width))])),
        out_shape=(shaped((rows, width), BF),) * 5 + (shaped((1, width), F32),),
        scratch_shapes=[pltpu.VMEM((RING, 2, local_rows, width), BF)] * 2
        + [pltpu.SemaphoreType.DMA((2 * RING,))] * 2,
        compiler_params=params(BIG),
        cost_estimate=cost(0, 14 * rows * width),
        name="rows",
    )


def expand_kernel(
    weight, qkv_w, dense_w, normed, grad, small, activated, slope, projected, attended_grad
):
    attended_grad[...] = dot_nn(grad[...], dense_w[...]).astype(BF)
    projected[...] = dot_nn(normed[...], qkv_w[...]) + small[12:13, : projected.shape[1]]
    u = dot_nn(normed[...], weight[...]) + small[14:15]
    factor = (2.0 / np.pi) ** 0.5
    square = u * u
    bent = jnp.tanh(factor * u * (1.0 + 0.044715 * square))
    half = 0.5 + 0.5 * bent
    activated[...] = (u * half).astype(BF)
    rise = factor * (1.0 + 3.0 * 0.044715 * square)
    slope[...] = (half + 0.5 * u * (1.0 - bent * bent) * rise).astype(BF)


def expand_layer(weights, normed, grad, small, *waits):
    rows, width = normed.shape
    cols = weights.shape[1] // 2
    three = cols // 4 * 3
    at_once = 256
    return kernel_call(
        expand_kernel,
        (weights, weights, weights, normed, grad, small),
        waits,
        grid=(rows // at_once,),
        in_specs=[
            pl.BlockSpec((width, cols), lambda i: (0, 1)),
            pl.BlockSpec((width, three), lambda i: (0, 0)),
            pl.BlockSpec((width, cols // 4), lambda i: (0, 3)),
            row_block(at_once, width),
            row_block(at_once, width),
            whole(small.shape),
        ],
        out_specs=(row_block(at_once, cols),) * 2 + (row_block(at_once, three), row_block(at_once, cols // 4)),
        out_shape=(shaped((rows, cols), BF),) * 2
        + (shaped((rows, three), F32), shaped((rows, cols // 4), BF)),
        compiler_params=params(BIG),
        cost_estimate=cost(2 * rows * width * (cols + three), 4 * rows * width, rows * cols),
        name="expand",
    )


def feed_back_kernel(weights, grad, slope, normed, activated, grad_turned, *refs):
    eg_out, bias_grad, *outs = refs[: 2 + 2 * RING]
    weight_v, grad_v, slope_v, normed_v, activated_v, turned_v, eg_v, hold, *rest = refs[
        2 + 2 * RING :
    ]
    sems, out_sems = rest
    step = pl.program_id(0)
    tile = grad.shape[0] // RING
    quarter = grad.shape[1] // RING

    def loads():
        made = [(weights, weight_v)]
        for n in range(RING):
            made.append((grad.at[pl.ds(n * tile, tile)], grad_v.at[pl.ds(n * tile, tile)]))
        made += [
            (slope, slope_v), (normed, normed_v), (activated, activated_v), (grad_turned, turned_v),
        ]
        return [pltpu.make_async_copy(a, b, sems.at[n]) for n, (a, b) in enumerate(made)]

    def stores():
        made = [pltpu.make_async_copy(hold.at[n], out, out_sems.at[n]) for n, out in enumerate(outs)]
        return made + [pltpu.make_async_copy(eg_v, eg_out, out_sems.at[2 * RING])]

    @pl.when(step == 0)
    def _():
        copies = loads()
        for n in (0, 1, 5, 2, 3, 4, 6, 7, 8):
            copies[n].start()
        copies[0].wait()
        copies[5].wait()
        bias_grad[...] = jnp.zeros_like(bias_grad)

    for n in range(RING):

        @pl.when(step == n)
        def _(n=n):
            loads()[1 + n].wait()

    @pl.when(step < RING)
    def _():
        at = pl.ds(pl.multiple_of(step * tile, tile), tile)
        low = dot_nn(grad_v[at, :], weight_v[...]) * slope_v[at, :].astype(F32)
        low = low.astype(BF)
        eg_v[at, :] = low
        bias_grad[...] += jnp.sum(low.astype(F32), 0, keepdims=True)

    @pl.when(step == RING)
    def _():
        stores()[2 * RING].start()
        loads()[6].wait()

    @pl.when(step == 2 * RING)
    def _():
        loads()[7].wait()
        loads()[8].wait()

    def columns(first):
        return pl.ds(pl.multiple_of((step - first) * quarter, quarter), quarter)

    @pl.when((step >= RING) & (step < 2 * RING))
    def _():
        hold[step - RING] = dot_tn(normed_v[:, columns(RING)], eg_v[...]).astype(BF)

    @pl.when(step >= 2 * RING)
    def _():
        hold[step - RING] = dot_tn(turned_v[:, columns(2 * RING)], activated_v[...]).astype(BF)

    for n in range(2 * RING):

        @pl.when(step == n + RING)
        def _(n=n):
            stores()[n].start()

    @pl.when(step == 3 * RING - 1)
    def _():
        for copy in stores():
            copy.wait()


def feed_back(weights, grad, slope, normed, activated, grad_turned, *waits):
    rows, width = grad.shape
    cols = weights.shape[1]
    depth = width // RING
    outs = kernel_call(
        feed_back_kernel,
        (weights, grad, slope, normed, activated, grad_turned),
        waits,
        grid=(3 * RING,),
        in_specs=[ANY] * 6,
        out_specs=(ANY, whole((1, cols))) + (ANY,) * (2 * RING),
        out_shape=(shaped((rows, cols), BF), shaped((1, cols), F32))
        + (shaped((depth, cols), BF),) * (2 * RING),
        scratch_shapes=[
            pltpu.VMEM((width, cols), BF),
            pltpu.VMEM((rows, width), BF),
            pltpu.VMEM((rows, cols), BF),
            pltpu.VMEM((rows, width), BF),
            pltpu.VMEM((rows, cols), BF),
            pltpu.VMEM((rows, width), BF),
            pltpu.VMEM((rows, cols), BF),
            pltpu.VMEM((2 * RING, depth, cols), BF),
            pltpu.SemaphoreType.DMA((RING + 5,)),
            pltpu.SemaphoreType.DMA((2 * RING + 1,)),
        ],
        compiler_params=params(BIG),
        cost_estimate=cost(6 * rows * width * cols, 20 * rows * width),
        name="feed_back",
    )
    quarters = [quarter.reshape(RING, -1, cols) for quarter in outs[2:]]
    return *outs[:2], quarters[:RING], quarters[RING:]


def branch_kernel(rank, dense, reduce, activated, attended, small, branch, bias):
    heads = attended.shape[1]
    lanes = 2 * HEAD_DIM

    @pl.when(pl.program_id(0) == 0)
    def _():
        mine = small[12:13, 3 * heads :] + small[13:14, 3 * heads :]
        lane = lax.broadcasted_iota(jnp.int32, (1, lanes), 1)
        places = heads // HEAD_DIM
        side = (lane // HEAD_DIM) == rank[0] // (RING * RING // places)
        for n in range(RING * RING):
            part = mine[:, (n % places) * HEAD_DIM : (n % places + 1) * HEAD_DIM]
            part = jnp.concatenate([part, part], 1)
            here = rank[0] % (RING * RING // places) == n // places
            bias[:, n * lanes : (n + 1) * lanes] = jnp.where(side & here, part, 0.0)

    total = dot_nt(activated[...], reduce[...]) + dot_nt(attended[...], dense[...])
    branch[...] = (total + bias[...]).astype(BF)


def branch_layer(rank, activated, attended, weights, reduce_w, small, *waits):
    rows, cols = activated.shape
    heads = attended.shape[1]
    width = weights.shape[0]
    at_once = 256
    return kernel_call(
        branch_kernel,
        (rank, weights, reduce_w, activated, attended, small),
        waits,
        grid=(rows // at_once,),
        in_specs=[SMEM]
        + [pl.BlockSpec((width, heads), lambda i: (0, 3))]
        + [whole((width, cols))]
        + [row_block(at_once, cols), row_block(at_once, heads), whole(small.shape)],
        out_specs=row_block(at_once, width),
        out_shape=shaped((rows, width), BF),
        scratch_shapes=[pltpu.VMEM((1, width), F32)],
        compiler_params=params(BIG),
        cost_estimate=cost(
            2 * rows * width * (cols + heads), 2 * (width + rows) * (cols + heads) + 2 * rows * width
        ),
        name="branch",
    )


def normed_grad_kernel(qkv_w, expand_w, proj_grad, expanded_grad, x_hat, part, sums):
    @pl.when(pl.program_id(0) == 0)
    def _():
        sums[...] = jnp.zeros_like(sums)

    total = dot_nt(proj_grad[...], qkv_w[...]) + dot_nt(expanded_grad[...], expand_w[...])
    part[...] = total.astype(BF)
    gain = jnp.sum(total * x_hat[...].astype(F32), 0, keepdims=True)
    offset = jnp.sum(total, 0, keepdims=True)
    sums[...] += jnp.concatenate([gain, offset], 0)


def normed_grad_layer(proj_grad, expanded_grad, weights, x_hat, *waits):
    rows, width = x_hat.shape
    cols, three = expanded_grad.shape[1], proj_grad.shape[1]
    depth = width // RING
    at_once = 256
    return kernel_call(
        normed_grad_kernel,
        (weights, weights, proj_grad, expanded_grad, x_hat),
        waits,
        grid=(rows // at_once,),
        in_specs=[pl.BlockSpec((width, three), lambda i: (0, 0))]
        + [pl.BlockSpec((width, cols), lambda i: (0, 1))]
        + [row_block(at_once, three), row_block(at_once, cols), row_block(at_once, width)],
        out_specs=(row_block(at_once, width), whole((2, width))),
        out_shape=(shaped((rows, width), BF), shaped((2, width), F32)),
        compiler_params=params(BIG),
        cost_estimate=cost(
            2 * rows * width * (cols + three), 2 * (width + rows) * (cols + three) + 4 * rows * width
        ),
        name="normed_grad",
    )


def weight_grad_kernel(count, *refs):
    lefts, rights = refs[:count], refs[count : 2 * count]
    *small, out0, out1, out2, out3, hold, sems = refs[2 * count :]
    outs = (out0, out1, out2, out3)
    step, last = pl.program_id(0), pl.num_programs(0) - 1
    cols = 0
    for a, b in zip(lefts, rights):
        hold[step, :, cols : cols + b.shape[1]] = dot_tn(a[...], b[...]).astype(BF)
        cols += b.shape[1]
    for ref in small:
        for n in range(RING):
            lanes = ref.shape[1]
            hold[step, n * lanes : (n + 1) * lanes, cols:] = ref[...]
    for n, out in enumerate(outs):

        @pl.when(step == n)
        def _(n=n, out=out):
            pltpu.make_async_copy(hold.at[n], out, sems.at[n]).start()

    @pl.when(step == last)
    def _():
        for n, out in enumerate(outs):
            pltpu.make_async_copy(hold.at[n], out, sems.at[n]).wait()


def weight_grad(pairs, small=None, waits=()):
    rows, width = pairs[0][0].shape
    more = [] if small is None else [small]
    cols = sum(right.shape[1] for _, right in pairs) + sum(extra.shape[1] for extra in more)
    at_once = width // RING

    def kernel(*refs):
        weight_grad_kernel(len(pairs), *refs)

    left = pl.BlockSpec((rows, at_once), lambda i: (0, i))
    quarters = kernel_call(
        kernel,
        (*[a for a, _ in pairs], *[b for _, b in pairs], *more),
        waits,
        grid=(RING,),
        in_specs=[left] * len(pairs)
        + [whole(right.shape) for _, right in pairs]
        + [whole(extra.shape) for extra in more],
        out_specs=(ANY,) * RING,
        out_shape=(shaped((at_once, cols), BF),) * RING,
        scratch_shapes=[
            pltpu.VMEM((RING, at_once, cols), BF),
            pltpu.SemaphoreType.DMA((RING,)),
        ],
        compiler_params=params(BIG),
        cost_estimate=cost(
            2 * rows * width * cols, 2 * (len(pairs) * rows * width + rows * cols + width * cols)
        ),
        name="weight_grad",
    )
    return [quarter.reshape(RING, -1, cols) for quarter in quarters]


def rolled(value, shift):
    return pltpu.roll(value, shift % value.shape[-1], value.ndim - 1)


def rotate(value, cos, sin_low, sin_high, sign):
    half = ROT // 2
    turned = rolled(value, -half) * sin_low + rolled(value, half) * sin_high
    return value * cos + sign * turned


def attention_kernel(
    projected, out_grad, cos, sin_low, sin_high, start, mixed, proj_grad, bias_grad
):
    rows, width = out_grad.shape
    heads = width // HEAD_DIM
    scale = HEAD_DIM**-0.5
    tables = [
        jnp.concatenate([ref[...]] * (width // ref.shape[1]), 1) for ref in (cos, sin_low, sin_high)
    ]
    query_rot = (rotate(projected[:, :width], *tables, 1.0).astype(BF) * scale).astype(BF)
    key_rot = rotate(projected[:, width : 2 * width], *tables, 1.0).astype(BF)
    value_rows = projected[:, 2 * width :].astype(BF)
    grad_rows = out_grad[...]
    half = rows // 4
    lane = lax.broadcasted_iota(jnp.int32, (half, width), 1)
    mine = [(lane >= h * HEAD_DIM) & (lane < (h + 1) * HEAD_DIM) for h in range(heads)]

    def stacked(block):
        return jnp.concatenate([jnp.where(m, block, jnp.zeros_like(block)) for m in mine], 0)

    def gathered(stack):
        total = None
        for h in range(heads):
            part = stack[h * half : (h + 1) * half]
            total = part if total is None else jnp.where(mine[h], part, total)
        return total

    key_sum, value_sum = {}, {}
    for first in range(0, rows, half):
        last = first + half
        here = slice(first, last)
        row_id = lax.broadcasted_iota(jnp.int32, (half, last), 0) + first
        col_id = lax.broadcasted_iota(jnp.int32, (half, last), 1)
        allowed = ((col_id <= row_id) & (col_id >= start[here, 0:1]))[None]
        queries, grads = stacked(query_rot[here]), stacked(grad_rows[here])
        scores = dot_nt(queries, key_rot[:last]).reshape(heads, half, last)
        scores = jnp.where(allowed, scores, -1000000000.0)
        top = jnp.max(scores, -1, keepdims=True)
        expd = jnp.exp(scores - top)
        probs = expd * (1.0 / jnp.sum(expd, -1, keepdims=True))
        prob_low = probs.astype(BF).reshape(heads * half, last)
        prob_grad = dot_nt(grads, value_rows[:last]).reshape(heads, half, last)
        row_dot = jnp.sum(probs * prob_grad, -1, keepdims=True)
        score_grad = (probs * (prob_grad - row_dot)).astype(BF).reshape(heads * half, last)
        mixed[here, :] = gathered(dot_nn(prob_low, value_rows[:last])).astype(BF)
        query_part = gathered(dot_nn(score_grad, key_rot[:last])) * scale
        query_part = rotate(query_part, *[table[here] for table in tables], -1.0).astype(BF)
        proj_grad[here, :width] = query_part
        query_bias = jnp.sum(query_part.astype(F32), 0, keepdims=True)
        bias_grad[0, :, :width] = query_bias if first == 0 else bias_grad[0, :, :width] + query_bias
        key_part, value_part = dot_tn(score_grad, queries), dot_tn(prob_low, grads)
        for n in range(0, last, half):
            for sums, part in ((key_sum, key_part), (value_sum, value_part)):
                block = part[n : n + half]
                sums[n] = sums[n] + block if n in sums else block
    for j, sums in ((1, key_sum), (2, value_sum)):
        total = jnp.concatenate([sums[n] for n in range(0, rows, half)], 0)
        if j == 1:
            total = rotate(total, *tables, -1.0)
        low = total.astype(BF)
        proj_grad[:, j * width : (j + 1) * width] = low
        bias_grad[0, :, j * width : (j + 1) * width] = jnp.sum(low.astype(F32), 0, keepdims=True)


def attention(projected, out_grad, cos, sin_low, sin_high, start, pack_rows, *waits):
    rows, width = out_grad.shape
    lanes = cos.shape[1]
    packs = rows // pack_rows
    return kernel_call(
        attention_kernel,
        (projected, out_grad, cos, sin_low, sin_high, start),
        waits,
        grid=(packs,),
        in_specs=[row_block(pack_rows, 3 * width), row_block(pack_rows, width)]
        + [row_block(pack_rows, lanes)] * 4,
        out_specs=(
            row_block(pack_rows, width),
            row_block(pack_rows, 3 * width),
            pl.BlockSpec((1, 1, 3 * width), lambda p: (p, 0, 0)),
        ),
        out_shape=(
            shaped((rows, width), BF),
            shaped((rows, 3 * width), BF),
            shaped((packs, 1, 3 * width), F32),
        ),
        compiler_params=params(BIG),
        cost_estimate=cost(
            14 * rows * pack_rows * width, rows * width * 32, rows * pack_rows * width // HEAD_DIM
        ),
        name="attention",
    )


def pick(first, a, b):
    return jnp.where(first, a, b), jnp.where(first, b, a)


def three_parts(value):
    high = lax.reduce_precision(value, 8, 7)
    rest = value - high
    mid = lax.reduce_precision(rest, 8, 7)
    return [high, mid, rest - mid]


def body(
    hidden_in,
    seq_lengths,
    norm_gain,
    norm_offset,
    attn_weight,
    attn_bias,
    dense_weight,
    dense_bias,
    expand_weight,
    expand_bias,
    reduce_weight,
    reduce_bias,
    out_grad,
):
    at_yhi, at_x, at_z, at_ylo, at_core = (lax.axis_index(a) for a in AXES)
    first_yhi, first_ylo, first_core = at_yhi == 0, at_ylo == 0, at_core == 0
    local_rows, width = hidden_in.shape
    pack_rows = local_rows * RING
    at_tensor = at_ylo * 2 + at_core
    column_rank = at_tensor * 2 + at_yhi
    plane = RING * RING
    at_plane = at_x * RING + at_z

    place = np.arange(plane, dtype=np.int32)
    x, z = (place // RING - at_x) % RING, (place % RING - at_z) % RING
    inner, outer = jnp.where(first_core, x, z), jnp.where(first_core, z, x)
    order = np.array([0, 2, 3, 1], np.int32)

    def position(step):
        return sum(jnp.where(step == n, order[n], 0) for n in range(1, RING))

    turned = (position(outer) * RING + position(inner)).astype(jnp.int32)

    lanes = 2 * HEAD_DIM
    block_rows, cols = expand_weight.shape[0], expand_weight.shape[1] // 2
    heads = cols // 4

    unit = norm_gain.shape[0]
    norms = jnp.stack(three_parts(norm_gain) + three_parts(norm_offset))
    lengths = seq_lengths[0]
    count = lengths.shape[0]
    small = lax.dynamic_update_slice(
        jnp.zeros((16, cols), F32),
        norms,
        (at_plane // 8 * 6, at_plane % 8 * 8 * unit + at_yhi * 4 * unit + at_tensor * unit),
    )
    two = jnp.concatenate([lengths // 16, lengths % 16]).astype(F32)
    small = lax.dynamic_update_slice(small, two[None], (15, at_yhi * 2 * count)).astype(BF)

    own, other = split_columns(
        at_yhi.reshape(1).astype(jnp.int32),
        attn_weight, dense_weight.T, expand_weight, reduce_weight.T,
    )
    got = swap(other, "yhi")
    block = jnp.concatenate(pick(first_yhi, own, got), 0)
    weights = lax.all_gather(block[:, : 2 * cols], ("x", "z"), axis=0, tiled=True)
    reduce_w = lax.all_gather(block[:, 2 * cols :], ("x", "z"), axis=0, tiled=True)

    small = small + swap(small, "yhi")
    two = small[15, : 4 * count].astype(F32).reshape(2, 2, count)
    length_rows = (two[:, 0] * 16.0 + two[:, 1]).astype(jnp.int32)
    biases = jnp.stack([dense_bias, reduce_bias])
    biases = jnp.concatenate([jnp.stack([attn_bias, 0 * attn_bias]), biases[:, None]], 1)
    bias_rows = lax.dynamic_update_slice(
        jnp.zeros((2, 4, heads), BF), biases, (0, 0, at_plane * unit)
    ).reshape(2, cols)
    expand_row = lax.dynamic_update_slice(
        jnp.zeros((2, cols), BF), expand_bias[None], (0, at_plane * expand_bias.shape[0])
    )
    small = jnp.concatenate([small[:12], bias_rows, expand_row], 0)

    for axis in ("x", "z"):
        for odd in range(2):
            small = small + lax.ppermute(small, axis, axis_swaps(odd))
    parts = jnp.where((np.arange(16) < 12)[:, None], small, jnp.zeros_like(small))
    others = swap(parts, "ylo")
    small = (small + others + swap(parts + others, "core")).astype(F32)

    own_rows = pair_columns(hidden_in, out_grad, got)
    below, above = move_y(own_rows, 1), move_y(own_rows, -1)
    one = (1,) + own_rows.shape[1:]
    far_hidden, far_grad = take_parts((below, one, (0, 0, 0)), (above, one, (1, 0, 0)))
    far_hidden, far_grad = move_y(far_hidden, 1), move_y(far_grad, -1)
    far_rows = jnp.concatenate([far_hidden, far_grad], 0)
    sources = [
        ref for rows in (own_rows, below, above, far_rows) for ref in (rows, swap(rows, "core"))
    ]
    at_y = at_yhi * 2 + at_ylo
    chips = jnp.stack([at_y, (at_y + 3) % RING, (at_y + 1) % RING, (at_y + 2) % RING, at_core])
    chips = chips.astype(jnp.int32)

    ends = jnp.cumsum(length_rows, 1)
    row_ids = jnp.arange(pack_rows, dtype=jnp.int32)
    begun = row_ids[None, :, None] >= ends[:, None, :]
    start = jnp.max(jnp.where(begun, ends[:, None, :], 0), 2).reshape(-1, 1)
    position = (jnp.tile(row_ids, 2)[:, None] - start).astype(F32)
    lane = np.arange(lanes) % HEAD_DIM
    half = ROT // 2
    inverse = np.float32(10000.0) ** (np.float32(-2.0) * (lane % half).astype(np.float32) / ROT)
    angles = position * inverse.astype(np.float32)[None, :]
    cos = jnp.where((lane < ROT)[None, :], jnp.cos(angles), 1.0)
    sine = jnp.sin(angles)
    sin_low = jnp.where((lane < half)[None, :], -sine, 0.0)
    sin_high = jnp.where(((lane >= half) & (lane < ROT))[None, :], sine, 0.0)
    start = jnp.broadcast_to(start, (start.shape[0], lanes))

    normed, normed_turned, x_hat, grad_all, grad_turned, grad_sum = rows_layer(
        chips, turned, small, sources, cos, sin_low, sin_high, start
    )
    activated, slope, projected, attended_grad = expand_layer(weights, normed, grad_all, small)
    attended, proj_grad, attn_bias_grad = attention(
        projected, attended_grad, cos, sin_low, sin_high, start, pack_rows
    )
    attn_1 = weight_grad([(normed_turned, proj_grad), (grad_turned, attended)])
    attn_sent = ring_send(attn_1, False, -1)
    branch = branch_layer(
        column_rank.reshape(1).astype(jnp.int32),
        activated, attended, weights, reduce_w, small, attn_1[0],
    )
    attn_up, branch = add_pairs([(attn_1[1], attn_sent[0])], branch, (attn_sent[1],))
    attn_last = move(attn_up, False, -1)
    expanded_grad, expand_bias_grad, expand_1, reduce_1 = feed_back(
        reduce_w, grad_all, slope, normed_turned, activated, grad_turned, attn_up
    )
    expand_sent = ring_send(expand_1, False, 1)
    reduce_sent = ring_send(reduce_1, False, -1)
    normed_part, norm_sums = normed_grad_layer(
        proj_grad, expanded_grad, weights, x_hat, expand_1[0], attn_last
    )
    expand_up, reduce_up, normed_part = add_pairs(
        [(expand_1[2], expand_sent[0]), (reduce_1[1], reduce_sent[0])],
        normed_part,
        (expand_sent[1], reduce_sent[1]),
    )
    expand_last, reduce_last = move(expand_up, False, 1), move(reduce_up, False, -1)

    places = heads // block_rows
    out_bias_grad = lax.dynamic_slice(
        grad_sum.reshape(plane, 2, block_rows),
        (column_rank % (plane // places) * places, column_rank // (plane // places), 0),
        (places, 1, block_rows),
    ).reshape(1, heads)
    attn_row = jnp.concatenate([jnp.sum(attn_bias_grad, 0), out_bias_grad], 1)
    small_sums = jnp.concatenate(
        [norm_sums.reshape(4, cols), attn_row, expand_bias_grad, jnp.zeros((10, cols), F32)], 0
    )
    small_sums = sum((move(small_sums, False, step) for step in (1, 2, 3)), small_sums)

    branch = lax.psum_scatter(branch, COLUMN, scatter_dimension=0, tiled=True)
    normed_grad = lax.psum_scatter(normed_part, COLUMN, scatter_dimension=0, tiled=True)
    block_out = output_layer(own_rows, branch, expand_up)

    yhi_index = at_yhi.reshape(1).astype(jnp.int32)
    feed_2 = add_lines(
        [
            (expand_1[0], expand_sent[1], expand_last),
            (reduce_1[0], reduce_sent[1], reduce_last),
        ],
        [fold(small_sums).astype(BF)],
    )
    feed_terms = ring_terms(feed_2)
    attn_2 = add_lines([(attn_1[0], attn_sent[1], attn_last)], waits=(feed_2[0],))
    input_grad = input_grad_layer(own_rows, normed_grad, small, attn_2[0])
    attn_terms = ring_terms(attn_2)
    feed_keep, feed_send, small_total = finish_sums(
        yhi_index, feed_terms, 2 * cols, (attn_2[0], block_out, input_grad)
    )
    attn_keep, attn_send = finish_sums(yhi_index, attn_terms, cols, (feed_send,))
    attn_got = swap(attn_send, "yhi")
    small_total = unfold(small_total)
    norm_total = lax.dynamic_slice_in_dim(
        small_total[:4].reshape(2, width), at_plane * 8 * unit, 8 * unit, 1
    ).reshape(2, 2, 4 * unit)
    norm_keep, norm_send = pick(first_yhi, norm_total[:, 0], norm_total[:, 1])
    rider = jnp.pad(norm_send.astype(BF), ((0, 14), (0, 2 * cols - 4 * unit)))
    got = swap(jnp.concatenate([feed_send, rider], 0), "yhi")
    attn_w_grad, dense_w_grad = join_halves(
        yhi_index,
        attn_keep,
        attn_got,
        ((3, 0, heads), (1, 3 * heads, heads)),
    )
    expand_w_grad, reduce_w_grad = join_halves(
        yhi_index,
        feed_keep,
        got[:block_rows],
        ((1, 0, cols), (1, cols, cols)),
        (attn_w_grad,),
    )
    keep = norm_keep + got[block_rows : block_rows + 2, : 4 * unit].astype(F32)
    keep = keep.reshape(2, 2, 2, unit)
    keep, send = pick(first_ylo, keep[:, 0], keep[:, 1])
    keep = keep + swap(send, "ylo")
    keep, send = pick(first_core, keep[:, 0], keep[:, 1])
    norm_grads = keep + swap(send, "core")

    bias_total = lax.dynamic_slice_in_dim(
        small_total[4].reshape(4, heads), at_plane * unit, unit, 1
    )
    expand_b_grad = lax.dynamic_slice_in_dim(
        small_total[5], at_plane * expand_bias.shape[0], expand_bias.shape[0]
    )
    return (
        block_out,
        input_grad,
        norm_grads[0],
        norm_grads[1],
        attn_w_grad,
        bias_total[:3],
        dense_w_grad.T,
        bias_total[3],
        expand_w_grad,
        expand_b_grad,
        reduce_w_grad.T,
        bias_total[3],
    )


def solution(mesh):
    split = Mesh(mesh.devices.reshape(2, RING, RING, 2, 2), AXES)
    dp, tensor = ("yhi", "x", "z"), ("ylo", "core")
    rows = P(dp + tensor, None)
    vector = P(dp + tensor)
    bias = P(tensor + dp)
    parameters = (
        vector,
        vector,
        P(None, dp, tensor),
        P(None, tensor + dp),
        P(tensor, dp),
        bias,
        P(dp, tensor),
        bias,
        P(tensor, dp),
        bias,
    )
    return jax.shard_map(
        body,
        mesh=split,
        in_specs=(rows, P(dp, None)) + parameters + (rows,),
        out_specs=(rows, rows) + parameters,
        check_vma=False,
    )
```
